32 devices in a mesh: dp: 8 (over z, y), seq: 4 (over x, core).
Axes of the slice: x: 2, y: 2, z: 4, core: 2. Of those that a mesh axis runs over, the one named last changes fastest.
Arguments:
- query: bfloat16 [8, 1536, 4096], P('dp', 'seq'), may hold values from -51 to 51
- caption: bfloat16 [8, 256, 4096], P('dp'), may hold values from -6 to 6
- key_weight: bfloat16 [4096, 4096], P('dp', 'seq'), may hold values from -0.09375 to 0.09375
- value_weight: bfloat16 [4096, 4096], P('dp', 'seq'), may hold values from -0.09375 to 0.09375
- key_gain: float32 [4096], replicated, may hold values from 0.2 to 4.5
- lengths: int32 [8], P('dp'), may hold values from 64 to 128, as said below
- out_grad: bfloat16 [8, 1536, 4096], P('dp', 'seq'), may hold values from -6 to 6
Outputs:
- query_grad: bfloat16 [8, 1536, 4096], P('dp', 'seq')
- key_weight_grad: float32 [4096, 4096], P('dp', 'seq')
- value_weight_grad: float32 [4096, 4096], P('dp', 'seq')
The draws below stay inside these ranges and needn't reach their ends.
Inputs may be any that keep to these rules, and one draw needn't show every extreme that they name: `lengths`: valid caption tokens of each video, at most 128, a count that some video reaches.
All inputs are finite; a program needn't handle non-finite values.
Results may differ from the reference program's by a relative error of at most 0.008.
The reference program's roundings to bfloat16 on the way (of `raw_keys`, `values`, `keys`, `dscores` and `raw_grad`) count: a program that leaves them out, or rounds other values in their place, can miss the bound.
Values may be sent and summed in bfloat16 or wider, within the bound.
No kernel may reach another device: no remote copies, remote signals or barrier semaphores. Data moves between devices by JAX's collectives and lax.ppermute only.
A program may use at most 192 MiB of HBM per device.

```python
import jax
import jax.numpy as jnp
from jax import lax

HEADS = 32
HD = 128
DTXT = 4096
LTXT = 256
HID = 4096
LIVE = 128
SEQ = 1536
VIDEOS = 8


def draw_query(key, part):
    key = jax.random.fold_in(key, 7)
    full_shape = (VIDEOS, SEQ, HID)
    return jnp.clip(jax.random.normal(key, full_shape, jnp.float32), -6.0, 6.0).astype(jnp.bfloat16)


def draw_key_gain(key, part):
    key = jax.random.fold_in(key, 11)
    feature_ramp = jnp.arange(HID).astype(jnp.float32) / HID
    spread = jax.random.uniform(key, (HID,), jnp.float32, -0.4, 0.4)
    return jnp.exp(spread) * 3.0 ** feature_ramp * 0.6


def draw_lengths(key, part):
    key = jax.random.fold_in(key, 5)
    base_draw = jax.random.randint(key, (VIDEOS,), LIVE // 2, LIVE + 1)
    longest = jax.random.randint(jax.random.fold_in(key, 1), (), 0, VIDEOS)
    return base_draw.at[longest].set(LIVE)


def strengthened(result, key, source, target, blocks, factor):
    owner, partner = [(jnp.arange(result.shape[dim]) // (result.shape[dim] // blocks)).reshape([-1 if axis == dim else 1 for axis in range(result.ndim)]) for dim in (source, target)]
    chosen = jax.random.permutation(key, blocks)[partner]
    strong = (owner == chosen) | (owner == (partner + blocks // 2) % blocks)
    return jnp.where(strong, factor * result, result)


def levels(rng, dims, split, least, high):
    def one(axis_at, blocks):
        heights = jax.random.uniform(jax.random.fold_in(jax.random.fold_in(rng, 6), axis_at), (blocks,), jnp.float32, least / len(split), high / len(split))
        return jnp.repeat(jnp.exp(heights), dims[axis_at] // blocks).reshape((-1,) + (1,) * (len(dims) - axis_at - 1))

    level = one(*split[0])
    for cut in split[1:]:
        level = level * one(*cut)
    return level


def scatter_about(rng, dims, width, bound, split=(), dtype=jnp.bfloat16):
    gain = levels(rng, dims, split, -0.22, 0.18) if split else 1.0
    values = jax.random.normal(rng, dims, jnp.float32) * width * gain
    return jnp.minimum(jnp.maximum(values, -bound), bound).astype(dtype)


def gaussian_with(own_key, shape, deviation, bound, pieces, heavy, kind=jnp.bfloat16):
    result = deviation * jax.random.normal(own_key, shape, jnp.float32)
    if pieces:
        result = result * levels(own_key, shape, pieces, -0.22, 0.18)
    return jnp.clip(strengthened(result, jax.random.fold_in(own_key, 3), *heavy), -bound, bound).astype(kind)


def setup_inputs(seed: int = 0) -> dict:
    streams_of = jax.random.split(jax.random.key(seed), 8)
    return {
        "query": draw_query(jax.random.fold_in(streams_of[7], 71), 0),
        "caption": gaussian_with(streams_of[1], (VIDEOS, LTXT, DTXT), 1.0, 6.0, ((0, 8),), (0, 2, 8, 2.0)),
        "key_weight": scatter_about(streams_of[2], (DTXT, HID), DTXT ** -0.5, 0.09375, ((0, 8), (1, 4))),
        "value_weight": scatter_about(streams_of[3], (DTXT, HID), DTXT ** -0.5, 0.09375, ((0, 8), (1, 4))),
        "key_gain": draw_key_gain(jax.random.fold_in(streams_of[7], 71), 0),
        "lengths": draw_lengths(jax.random.fold_in(streams_of[7], 71), 0),
        "out_grad": gaussian_with(streams_of[6], (VIDEOS, SEQ, HID), 1.0, 6.0, ((0, 8), (1, 4)), (1, 2, 4, 2.0)),
    }


def reference(query, caption, key_weight, value_weight, key_gain, lengths, out_grad):
    factor = HD ** (-0.5)

    def one_video(totals, per_video):
        rows_query, caption_rows, text_length, rows_grad = per_video
        raw_keys = jnp.dot(caption_rows, key_weight, preferred_element_type=jnp.float32).astype(jnp.bfloat16)
        values = jnp.dot(caption_rows, value_weight, preferred_element_type=jnp.float32).astype(jnp.bfloat16)
        raw_wide = raw_keys.astype(jnp.float32)
        inv_rms = lax.rsqrt(lax.optimization_barrier(jnp.mean(raw_wide * raw_wide, axis=-1, keepdims=True)) + 1e-06)
        keys = (raw_wide * inv_rms * key_gain).astype(jnp.bfloat16)
        query_heads = rows_query.reshape(SEQ, HEADS, HD).astype(jnp.float32)
        grad_heads = rows_grad.reshape(SEQ, HEADS, HD).astype(jnp.float32)
        key_heads = keys.reshape(LTXT, HEADS, HD).astype(jnp.float32)
        value_heads = values.reshape(LTXT, HEADS, HD).astype(jnp.float32)
        scores = jnp.einsum('thd,lhd->htl', query_heads, key_heads) * factor
        valid_mask = jnp.arange(LTXT) < text_length
        scores = jnp.where(valid_mask, scores, -jnp.inf)
        attend = jax.nn.softmax(scores, axis=-1)
        dattend = jnp.einsum('thd,lhd->htl', grad_heads, value_heads)
        row_delta = lax.optimization_barrier(jnp.sum(attend * dattend, axis=-1, keepdims=True))
        dscores = (attend * (dattend - row_delta)).astype(jnp.bfloat16).astype(jnp.float32)
        attend_low = attend.astype(jnp.bfloat16).astype(jnp.float32)
        query_grad = (jnp.einsum('htl,lhd->thd', dscores, key_heads) * factor).reshape(SEQ, HID).astype(jnp.bfloat16)
        key_grad = (jnp.einsum('htl,thd->lhd', dscores, query_heads) * factor).reshape(LTXT, HID)
        value_grad = jnp.einsum('htl,thd->lhd', attend_low, grad_heads).reshape(LTXT, HID)
        scaled = key_grad * key_gain
        inner_mean = lax.optimization_barrier(jnp.mean(scaled * raw_wide, axis=-1, keepdims=True))
        raw_grad = (inv_rms * scaled - raw_wide * inv_rms ** 3 * inner_mean).astype(jnp.bfloat16)
        grad_pair = jnp.concatenate([raw_grad, value_grad.astype(jnp.bfloat16)], axis=1)
        totals = totals + jnp.dot(caption_rows.T, grad_pair, preferred_element_type=jnp.float32)
        return (totals, query_grad)
    start_totals = jnp.zeros((DTXT, 2 * HID), jnp.float32)
    totals, query_grad = lax.scan(one_video, start_totals, (query, caption, lengths, out_grad))
    return (query_grad, totals[:, :HID], totals[:, HID:])
```

```python
import functools

import jax
import jax.numpy as jnp
from jax import lax
from jax.experimental import pallas as pl
from jax.experimental.pallas import tpu as pltpu
from jax.sharding import PartitionSpec as P

HD = 128
LIVE = 128


ROWS = (((1,), (1,)), ((), ()))
COLUMNS = (((0,), (0,)), ((), ()))
FACTOR = HD ** (-0.5)


def attend_kernel(parts, length_ref, raw_ref, inv_ref, gain_ref, *refs):
    query_refs, grad_refs = refs[:parts], refs[parts : 2 * parts]
    attend_refs = refs[2 * parts : 3 * parts]
    keys_ref, value_grad_ref = refs[3 * parts :]
    raw = raw_ref[...].astype(jnp.float32)
    keys = (raw * inv_ref[...] * gain_ref[...]).astype(jnp.bfloat16)
    keys_ref[...] = keys
    valid = lax.broadcasted_iota(jnp.int32, (LIVE, 1), 0) < length_ref[0]
    value_grad = jnp.zeros((LIVE, HD), jnp.float32)
    for query_ref, grad_ref, attend_ref in zip(query_refs, grad_refs, attend_refs):
        scores = lax.dot_general(keys, query_ref[...], ROWS, preferred_element_type=jnp.float32)
        scores = jnp.where(valid, scores * FACTOR, -jnp.inf)
        powers = jnp.exp(scores - jnp.max(scores, axis=0, keepdims=True))
        attend = powers * (1.0 / jnp.sum(powers, axis=0, keepdims=True))
        attend_ref[0] = attend
        value_grad += jnp.dot(
            attend.astype(jnp.bfloat16), grad_ref[...], preferred_element_type=jnp.float32
        )
    value_grad_ref[...] = value_grad.astype(jnp.bfloat16)


def gradient_kernel(parts, raw_ref, keys_ref, value_ref, gain_ref, *refs):
    query_refs, grad_refs = refs[:parts], refs[parts : 2 * parts]
    attend_refs, out_refs = refs[2 * parts : 3 * parts], refs[3 * parts : 4 * parts]
    scaled_ref, inner_ref = refs[4 * parts :]
    keys, values = keys_ref[...], value_ref[...]
    key_grad = jnp.zeros((LIVE, HD), jnp.float32)
    for query_ref, grad_ref, attend_ref, out_ref in zip(
        query_refs, grad_refs, attend_refs, out_refs
    ):
        attend = attend_ref[0]
        dattend = lax.dot_general(values, grad_ref[...], ROWS, preferred_element_type=jnp.float32)
        delta = jnp.sum(attend * dattend, axis=0, keepdims=True)
        dscores = (attend * (dattend - delta)).astype(jnp.bfloat16)
        out = lax.dot_general(dscores, keys, COLUMNS, preferred_element_type=jnp.float32)
        out_ref[...] = (out * FACTOR).astype(jnp.bfloat16)
        key_grad += jnp.dot(dscores, query_ref[...], preferred_element_type=jnp.float32)
    scaled = key_grad * FACTOR * gain_ref[...]
    scaled_ref[...] = scaled

    @pl.when(pl.program_id(0) == 0)
    def _():
        inner_ref[...] = jnp.zeros_like(inner_ref)

    inner_ref[...] += scaled * raw_ref[...].astype(jnp.float32)


def specs(tokens):
    head = pl.BlockSpec((LIVE, HD), lambda h: (0, h))
    block = pl.BlockSpec((tokens, HD), lambda h: (0, h))
    weights = pl.BlockSpec((1, LIVE, tokens), lambda h: (h, 0, 0))
    gain = pl.BlockSpec((1, HD), lambda h: (0, h))
    return head, block, weights, gain


def attend_call(length, raw, inv, gain, queries, grads):
    parts = len(queries)
    tokens, cols = queries[0].shape
    heads = cols // HD
    head, block, weights, gains = specs(tokens)
    outs = pl.pallas_call(
        functools.partial(attend_kernel, parts),
        grid=(heads,),
        in_specs=[
            pl.BlockSpec(memory_space=pltpu.SMEM),
            head,
            pl.BlockSpec((LIVE, 1), lambda h: (0, 0)),
            gains,
        ]
        + [block] * (2 * parts),
        out_specs=[weights] * parts + [head, head],
        out_shape=[jax.ShapeDtypeStruct((heads, LIVE, tokens), jnp.float32)] * parts
        + [jax.ShapeDtypeStruct((LIVE, cols), jnp.bfloat16)] * 2,
        compiler_params=pltpu.CompilerParams(vmem_limit_bytes=32 * 1024 * 1024),
        cost_estimate=pl.CostEstimate(
            flops=16 * parts * tokens * cols * LIVE,
            bytes_accessed=8 * parts * tokens * cols,
            transcendentals=parts * tokens * heads * LIVE,
        ),
    )(length, raw, inv, gain, *queries, *grads)
    return outs[:parts], outs[parts], outs[parts + 1]


def gradient_call(raw, keys, values, gain, queries, grads, attends):
    parts = len(queries)
    tokens, cols = queries[0].shape
    heads = cols // HD
    head, block, weights, gains = specs(tokens)
    outs = pl.pallas_call(
        functools.partial(gradient_kernel, parts),
        grid=(heads,),
        in_specs=[head, head, head, gains] + [block] * (2 * parts) + [weights] * parts,
        out_specs=[block] * parts + [head, pl.BlockSpec((LIVE, HD), lambda h: (0, 0))],
        out_shape=[jax.ShapeDtypeStruct((tokens, cols), jnp.bfloat16)] * parts
        + [
            jax.ShapeDtypeStruct((LIVE, cols), jnp.float32),
            jax.ShapeDtypeStruct((LIVE, HD), jnp.float32),
        ],
        compiler_params=pltpu.CompilerParams(vmem_limit_bytes=32 * 1024 * 1024),
        cost_estimate=pl.CostEstimate(
            flops=24 * parts * tokens * cols * LIVE,
            bytes_accessed=10 * parts * tokens * cols,
            transcendentals=0,
        ),
    )(raw, keys, values, gain, *queries, *grads, *attends)
    return outs[:parts], outs[parts], outs[parts + 1]


def after(x, *others):
    return lax.optimization_barrier((x, *others))[0]


def shards(n_dp, n_seq, query, caption, key_weight, value_weight, key_gain, lengths, out_grad):
    rows, cols = key_weight.shape
    hid = cols * n_seq
    lines = n_dp // 2
    me = lax.axis_index("dp")
    lane = lax.axis_index("seq")
    line, side = me // 2, me % 2

    def over_dp(x, step):
        return lax.ppermute(x, "dp", [(a, a ^ step) for a in range(n_dp)])

    def over_seq(x, step):
        return lax.ppermute(x, "seq", [(a, a ^ step) for a in range(n_seq)])

    def col_block(x, index, width):
        return lax.dynamic_slice(x, (0, index * width), (x.shape[0], width))

    captions = caption[0, :LIVE]
    key_partner = over_dp(key_weight, 1)
    value_partner = over_dp(after(value_weight, key_partner), 1)
    blocks = [col_block(captions, line, 2 * rows)] + [
        over_dp(col_block(captions, line ^ s, 2 * rows), 2 * s) for s in range(1, lines)
    ]
    own = [col_block(b, side, rows) for b in blocks]
    other = [col_block(b, 1 - side, rows) for b in blocks]

    moved = {}
    previous = ()
    for name, x in (("query", query[0]), ("grad", out_grad[0])):
        moved[name, 0] = col_block(x, lane, cols)
        for s in range(1, n_seq):
            part = col_block(x, lane ^ s, cols)
            if s > 1:
                part = after(part, *previous)
            moved[name, s] = over_seq(part, s)
            if s > 1:
                previous = (moved[name, s],)
    queries = [moved["query", s] for s in range(n_seq)]
    grads = [moved["grad", s] for s in range(n_seq)]
    half = (n_seq + 2) // 2

    def project(weight, partner, first, second):
        def product(chosen):
            a = jnp.concatenate([own[s] for s in chosen], axis=0)
            b = jnp.concatenate([other[s] for s in chosen], axis=0)
            return jnp.dot(a, weight, preferred_element_type=jnp.float32) + jnp.dot(
                b, partner, preferred_element_type=jnp.float32
            )

        odd = after(product([s for s in range(lines) if s & 1]), *first)
        total = product([s for s in range(lines) if not s & 1]) + over_dp(odd, 2)
        total = after(total, *second)
        chunks = lines // 2
        step = 2
        while chunks > 1:
            total = total.reshape(chunks // 2, 2, LIVE, cols)
            total = total[:, 0] + over_dp(total[:, 1], 2 * step)
            chunks //= 2
            step *= 2
        return lax.reduce_precision(total.reshape(LIVE, cols), 8, 7)

    raw_wide = project(key_weight, key_partner, queries[1:half], queries[half:])
    raw = raw_wide.astype(jnp.bfloat16)
    values = project(value_weight, value_partner, (), grads[1:half]).astype(jnp.bfloat16)

    def seq_sum(x):
        return functools.reduce(lambda a, b: a + b, [x] + [over_seq(x, s) for s in range(1, n_seq)])

    squares = seq_sum(jnp.sum(raw_wide * raw_wide, axis=-1, keepdims=True))
    inv_rms = lax.rsqrt(squares / hid + 1e-06)
    gain = lax.dynamic_slice(key_gain, (lane * cols,), (cols,)).reshape(1, cols)
    attends, keys, value_grad = attend_call(lengths, raw, inv_rms, gain, queries, grads)

    def gather(part):
        near = [part] + [over_dp(part, 2 * s) for s in range(1, lines)]
        return near + [over_dp(x, 1) for x in near]

    other_columns = over_dp(jnp.concatenate(other, axis=0), 1)
    columns = jnp.concatenate([*own, other_columns], axis=0)

    def weight_grad(parts):
        return lax.dot_general(
            columns,
            jnp.concatenate(parts, axis=0),
            COLUMNS,
            preferred_element_type=jnp.float32,
        )

    value_parts = gather(value_grad)
    outs, scaled, inner = gradient_call(raw, keys, values, gain, queries, grads, attends)
    inner_mean = seq_sum(jnp.sum(inner, axis=-1, keepdims=True)) / hid
    raw_grad = (inv_rms * scaled - raw_wide * inv_rms**3 * inner_mean).astype(jnp.bfloat16)
    key_parts = gather(raw_grad)

    placed = [outs[0]] + [over_seq(outs[s], s) for s in range(1, n_seq)]
    stacked = jnp.stack(placed)
    query_grad = jnp.concatenate(
        [lax.dynamic_index_in_dim(stacked, lane ^ h, 0, keepdims=False) for h in range(n_seq)],
        axis=1,
    )[None]
    return query_grad, weight_grad(key_parts), weight_grad(value_parts)


def solution(mesh):
    placed = (
        P("dp", "seq", None),
        P("dp", None, None),
        P("dp", "seq"),
        P("dp", "seq"),
        P(),
        P("dp"),
        P("dp", "seq", None),
    )
    return jax.shard_map(
        functools.partial(shards, mesh.shape["dp"], mesh.shape["seq"]),
        mesh=mesh,
        in_specs=placed,
        out_specs=(P("dp", "seq", None), P("dp", "seq"), P("dp", "seq")),
        check_vma=False,
    )
```

```python
import functools

import jax
import jax.numpy as jnp
from jax import lax
from jax.experimental import pallas as pl
from jax.experimental.pallas import tpu as pltpu
from jax.sharding import PartitionSpec as P

HD = 128
LIVE = 128


ROWS = (((1,), (1,)), ((), ()))
COLUMNS = (((0,), (0,)), ((), ()))
FACTOR = HD ** (-0.5)


def attend_kernel(parts, length_ref, raw_ref, inv_ref, gain_ref, *refs):
    query_refs, grad_refs = refs[:parts], refs[parts : 2 * parts]
    attend_refs = refs[2 * parts : 3 * parts]
    keys_ref, value_grad_ref = refs[3 * parts :]
    raw = raw_ref[...].astype(jnp.float32)
    keys = (raw * inv_ref[...] * gain_ref[...]).astype(jnp.bfloat16)
    keys_ref[...] = keys
    valid = lax.broadcasted_iota(jnp.int32, (LIVE, 1), 0) < length_ref[0]
    value_grad = jnp.zeros((LIVE, HD), jnp.float32)
    for query_ref, grad_ref, attend_ref in zip(query_refs, grad_refs, attend_refs):
        scores = lax.dot_general(keys, query_ref[...], ROWS, preferred_element_type=jnp.float32)
        scores = jnp.where(valid, scores * FACTOR, -jnp.inf)
        powers = jnp.exp(scores - jnp.max(scores, axis=0, keepdims=True))
        attend = powers * (1.0 / jnp.sum(powers, axis=0, keepdims=True))
        attend_ref[0] = attend
        value_grad += jnp.dot(
            attend.astype(jnp.bfloat16), grad_ref[...], preferred_element_type=jnp.float32
        )
    value_grad_ref[...] = value_grad.astype(jnp.bfloat16)


def gradient_kernel(parts, raw_ref, keys_ref, value_ref, gain_ref, *refs):
    query_refs, grad_refs = refs[:parts], refs[parts : 2 * parts]
    attend_refs, out_refs = refs[2 * parts : 3 * parts], refs[3 * parts : 4 * parts]
    scaled_ref, inner_ref = refs[4 * parts :]
    keys, values = keys_ref[...], value_ref[...]
    key_grad = jnp.zeros((LIVE, HD), jnp.float32)
    for query_ref, grad_ref, attend_ref, out_ref in zip(
        query_refs, grad_refs, attend_refs, out_refs
    ):
        attend = attend_ref[0]
        dattend = lax.dot_general(values, grad_ref[...], ROWS, preferred_element_type=jnp.float32)
        delta = jnp.sum(attend * dattend, axis=0, keepdims=True)
        dscores = (attend * (dattend - delta)).astype(jnp.bfloat16)
        out = lax.dot_general(dscores, keys, COLUMNS, preferred_element_type=jnp.float32)
        out_ref[...] = (out * FACTOR).astype(jnp.bfloat16)
        key_grad += jnp.dot(dscores, query_ref[...], preferred_element_type=jnp.float32)
    scaled = key_grad * FACTOR * gain_ref[...]
    scaled_ref[...] = scaled

    @pl.when(pl.program_id(0) == 0)
    def _():
        inner_ref[...] = jnp.zeros_like(inner_ref)

    inner_ref[...] += scaled * raw_ref[...].astype(jnp.float32)


def specs(tokens):
    head = pl.BlockSpec((LIVE, HD), lambda h: (0, h))
    block = pl.BlockSpec((tokens, HD), lambda h: (0, h))
    weights = pl.BlockSpec((1, LIVE, tokens), lambda h: (h, 0, 0))
    gain = pl.BlockSpec((1, HD), lambda h: (0, h))
    return head, block, weights, gain


def attend_call(length, raw, inv, gain, queries, grads):
    parts = len(queries)
    tokens, cols = queries[0].shape
    heads = cols // HD
    head, block, weights, gains = specs(tokens)
    outs = pl.pallas_call(
        functools.partial(attend_kernel, parts),
        grid=(heads,),
        in_specs=[
            pl.BlockSpec(memory_space=pltpu.SMEM),
            head,
            pl.BlockSpec((LIVE, 1), lambda h: (0, 0)),
            gains,
        ]
        + [block] * (2 * parts),
        out_specs=[weights] * parts + [head, head],
        out_shape=[jax.ShapeDtypeStruct((heads, LIVE, tokens), jnp.float32)] * parts
        + [jax.ShapeDtypeStruct((LIVE, cols), jnp.bfloat16)] * 2,
        compiler_params=pltpu.CompilerParams(vmem_limit_bytes=32 * 1024 * 1024),
        cost_estimate=pl.CostEstimate(flops=1000, bytes_accessed=1000, transcendentals=0),
    )(length, raw, inv, gain, *queries, *grads)
    return outs[:parts], outs[parts], outs[parts + 1]


def gradient_call(raw, keys, values, gain, queries, grads, attends):
    parts = len(queries)
    tokens, cols = queries[0].shape
    heads = cols // HD
    head, block, weights, gains = specs(tokens)
    outs = pl.pallas_call(
        functools.partial(gradient_kernel, parts),
        grid=(heads,),
        in_specs=[head, head, head, gains] + [block] * (2 * parts) + [weights] * parts,
        out_specs=[block] * parts + [head, pl.BlockSpec((LIVE, HD), lambda h: (0, 0))],
        out_shape=[jax.ShapeDtypeStruct((tokens, cols), jnp.bfloat16)] * parts
        + [
            jax.ShapeDtypeStruct((LIVE, cols), jnp.float32),
            jax.ShapeDtypeStruct((LIVE, HD), jnp.float32),
        ],
        compiler_params=pltpu.CompilerParams(vmem_limit_bytes=32 * 1024 * 1024),
        cost_estimate=pl.CostEstimate(
            flops=24 * parts * tokens * cols * LIVE,
            bytes_accessed=16 * parts * tokens * cols,
            transcendentals=0,
        ),
    )(raw, keys, values, gain, *queries, *grads, *attends)
    return outs[:parts], outs[parts], outs[parts + 1]


def product_kernel(videos, place_ref, *refs):
    mine_refs, sibling_refs = refs[:videos], refs[videos : 2 * videos]
    weight_refs, out_ref = refs[2 * videos : -1], refs[-1]
    rows = weight_refs[0].shape[0]
    total = None
    for step, weight_ref in enumerate(weight_refs):
        here = place_ref[step // 2] == 0
        at = pl.ds(pl.multiple_of(place_ref[2 + step % 2] * rows, rows), rows)
        block = jnp.concatenate(
            [jnp.where(here, m[:, at], s[:, at]) for m, s in zip(mine_refs, sibling_refs)], axis=0
        )
        term = jnp.dot(block, weight_ref[...], preferred_element_type=jnp.float32)
        total = term if total is None else total + term
    out_ref[...] = total


def product_call(place, mine, sibling, weights):
    videos = len(mine)
    width = weights[0].shape[1]
    return pl.pallas_call(
        functools.partial(product_kernel, videos),
        in_specs=[pl.BlockSpec(memory_space=pltpu.SMEM)]
        + [pl.BlockSpec(memory_space=pltpu.VMEM)] * (2 * videos + 4),
        out_specs=pl.BlockSpec(memory_space=pltpu.VMEM),
        out_shape=jax.ShapeDtypeStruct((videos * LIVE, width), jnp.float32),
        compiler_params=pltpu.CompilerParams(vmem_limit_bytes=32 * 1024 * 1024),
        cost_estimate=pl.CostEstimate(flops=1000, bytes_accessed=1000, transcendentals=0),
    )(place, *mine, *sibling, *weights)


def after(x, *others):
    return lax.optimization_barrier((x, *others))[0]


def shards(n_dp, n_seq, query, caption, key_weight, value_weight, key_gain, lengths, out_grad):
    rows, cols = key_weight.shape
    hid = cols * n_seq
    lines = n_dp // 2
    half = cols // 2
    me = lax.axis_index("dp")
    lane = lax.axis_index("seq")
    quad, low, side = me // 4, me // 2 % 2, me % 2
    core = lane % 2

    def over_dp(x, step):
        return lax.ppermute(x, "dp", [(a, a ^ step) for a in range(n_dp)])

    def over_seq(x, step):
        return lax.ppermute(x, "seq", [(a, a ^ step) for a in range(n_seq)])

    def col_block(x, index, width):
        return lax.dynamic_slice(x, (0, index * width), (x.shape[0], width))

    def spread(weight):
        kept = col_block(weight, low, half)
        near = over_dp(col_block(weight, 1 - low, half), 2)
        return kept, over_dp(kept, 1), near, over_dp(near, 1)

    key_quad = spread(key_weight)

    captions = caption[0, :LIVE]
    mine, sibling = [col_block(captions, quad * 2 + core, 2 * rows)], [
        col_block(captions, quad * 2 + 1 - core, 2 * rows)
    ]
    for s in range(1, lines):
        block = over_dp(col_block(captions, (quad ^ (s // 2)) * 2 + core, 2 * rows), 2 * s)
        mine.append(block)
        sibling.append(over_seq(block, 1))
    value_quad = spread(value_weight)

    moved = {}
    for name, x in (("query", query[0]), ("grad", out_grad[0])):
        moved[name, 0] = col_block(x, lane, cols)
        for s in range(1, n_seq):
            moved[name, s] = over_seq(col_block(x, lane ^ s, cols), s)
    queries = [moved["query", s] for s in range(n_seq)]
    grads = [moved["grad", s] for s in range(n_seq)]

    place = jnp.stack([core ^ low, 1 - (core ^ low), side, 1 - side]).astype(jnp.int32)

    def project(weights, first, second):
        def product(chosen):
            return product_call(place, [mine[s] for s in chosen], [sibling[s] for s in chosen], weights)

        sent = after(product([s for s in range(lines) if s & 2]), *first)
        total = product([s for s in range(lines) if not s & 2]) + over_dp(sent, 4)
        total = after(total, *second)
        step = 8
        while step < n_dp:
            count = total.shape[0] // 2
            total = total[:count] + over_dp(total[count:], step)
            step *= 2
        total = lax.reduce_precision(total, 8, 7).astype(jnp.bfloat16)
        kept, other = total[:LIVE], over_dp(total[LIVE:], 2)
        return jnp.where(
            low == 0,
            jnp.concatenate([kept, other], axis=1),
            jnp.concatenate([other, kept], axis=1),
        )

    middle = (n_seq + 2) // 2
    raw = project(key_quad, (*value_quad[:2], *queries[1:middle]), queries[middle:])
    values = project(value_quad, (), grads[1:middle])
    raw_wide = raw.astype(jnp.float32)

    def seq_sum(x):
        return functools.reduce(lambda a, b: a + b, [x] + [over_seq(x, s) for s in range(1, n_seq)])

    squares = seq_sum(jnp.sum(raw_wide * raw_wide, axis=-1, keepdims=True))
    inv_rms = lax.rsqrt(squares / hid + 1e-06)
    gain = lax.dynamic_slice(key_gain, (lane * cols,), (cols,)).reshape(1, cols)
    attends, keys, value_grad = attend_call(lengths, raw, inv_rms, gain, queries, grads)

    def gather(part, before):
        near = [part] + [over_dp(part, 2 * s) for s in range(1, lines)]
        return near + [over_dp(part, 1)] + [over_dp(after(x, *before), 1) for x in near[1:]]

    held = [jnp.where(core == low, m, s) for m, s in zip(mine, sibling)]
    other_columns = over_dp(jnp.concatenate([col_block(x, 1 - side, rows) for x in held], axis=0), 1)
    columns = jnp.concatenate([col_block(x, side, rows) for x in held] + [other_columns], axis=0)

    def weight_grad(parts, before):
        parts = lax.optimization_barrier((*parts, *before))[:n_dp]
        return lax.dot_general(
            columns,
            jnp.concatenate(parts, axis=0),
            COLUMNS,
            preferred_element_type=jnp.float32,
        )

    value_parts = gather(value_grad, ())
    outs, scaled, inner = gradient_call(raw, keys, values, gain, queries, grads, attends)
    inner = after(inner, *value_parts[1:lines])
    inner_mean = seq_sum(jnp.sum(inner, axis=-1, keepdims=True)) / hid
    raw_grad = (inv_rms * scaled - raw_wide * inv_rms**3 * inner_mean).astype(jnp.bfloat16)
    placed = [outs[0]] + [over_seq(after(outs[s], inner_mean), s) for s in range(1, n_seq)]
    key_parts = gather(raw_grad, placed[1:middle])
    stacked = jnp.stack(placed)
    query_grad = jnp.concatenate(
        [lax.dynamic_index_in_dim(stacked, lane ^ h, 0, keepdims=False) for h in range(n_seq)],
        axis=1,
    )[None]
    return query_grad, weight_grad(key_parts, placed[middle:]), weight_grad(value_parts, key_parts[1:lines])


def solution(mesh):
    placed = (
        P("dp", "seq", None),
        P("dp", None, None),
        P("dp", "seq"),
        P("dp", "seq"),
        P(),
        P("dp"),
        P("dp", "seq", None),
    )
    return jax.shard_map(
        functools.partial(shards, mesh.shape["dp"], mesh.shape["seq"]),
        mesh=mesh,
        in_specs=placed,
        out_specs=(P("dp", "seq", None), P("dp", "seq"), P("dp", "seq")),
        check_vma=False,
    )
```

```python
import functools

import jax
import jax.numpy as jnp
from jax import lax
from jax.experimental import pallas as pl
from jax.experimental.pallas import tpu as pltpu
from jax.sharding import PartitionSpec as P

HD = 128
LIVE = 128


ROWS = (((1,), (1,)), ((), ()))
COLUMNS = (((0,), (0,)), ((), ()))
FACTOR = HD ** (-0.5)


def attend_kernel(parts, length_ref, raw_ref, inv_ref, gain_ref, *refs):
    query_refs, grad_refs = refs[:parts], refs[parts : 2 * parts]
    attend_refs = refs[2 * parts : 3 * parts]
    keys_ref, value_grad_ref = refs[3 * parts :]
    raw = raw_ref[...].astype(jnp.float32)
    keys = (raw * inv_ref[...] * gain_ref[...]).astype(jnp.bfloat16)
    keys_ref[...] = keys
    valid = lax.broadcasted_iota(jnp.int32, (LIVE, 1), 0) < length_ref[0]
    value_grad = jnp.zeros((LIVE, HD), jnp.float32)
    for query_ref, grad_ref, attend_ref in zip(query_refs, grad_refs, attend_refs):
        scores = lax.dot_general(keys, query_ref[...], ROWS, preferred_element_type=jnp.float32)
        scores = jnp.where(valid, scores * FACTOR, -jnp.inf)
        powers = jnp.exp(scores - jnp.max(scores, axis=0, keepdims=True))
        attend = powers * (1.0 / jnp.sum(powers, axis=0, keepdims=True))
        attend_ref[0] = attend
        value_grad += jnp.dot(
            attend.astype(jnp.bfloat16), grad_ref[...], preferred_element_type=jnp.float32
        )
    value_grad_ref[...] = value_grad.astype(jnp.bfloat16)


def gradient_kernel(parts, raw_ref, keys_ref, value_ref, gain_ref, *refs):
    query_refs, grad_refs = refs[:parts], refs[parts : 2 * parts]
    attend_refs, out_refs = refs[2 * parts : 3 * parts], refs[3 * parts : 4 * parts]
    scaled_ref, inner_ref = refs[4 * parts :]
    keys, values = keys_ref[...], value_ref[...]
    key_grad = jnp.zeros((LIVE, HD), jnp.float32)
    for query_ref, grad_ref, attend_ref, out_ref in zip(
        query_refs, grad_refs, attend_refs, out_refs
    ):
        attend = attend_ref[0]
        dattend = lax.dot_general(values, grad_ref[...], ROWS, preferred_element_type=jnp.float32)
        delta = jnp.sum(attend * dattend, axis=0, keepdims=True)
        dscores = (attend * (dattend - delta)).astype(jnp.bfloat16)
        out = lax.dot_general(dscores, keys, COLUMNS, preferred_element_type=jnp.float32)
        out_ref[...] = (out * FACTOR).astype(jnp.bfloat16)
        key_grad += jnp.dot(dscores, query_ref[...], preferred_element_type=jnp.float32)
    scaled = key_grad * FACTOR * gain_ref[...]
    scaled_ref[...] = scaled

    @pl.when(pl.program_id(0) == 0)
    def _():
        inner_ref[...] = jnp.zeros_like(inner_ref)

    inner_ref[...] += scaled * raw_ref[...].astype(jnp.float32)


def specs(tokens):
    head = pl.BlockSpec((LIVE, HD), lambda h: (0, h))
    block = pl.BlockSpec((tokens, HD), lambda h: (0, h))
    lower = pl.BlockSpec((tokens, HD), lambda h: (1, h))
    weights = pl.BlockSpec((1, LIVE, tokens), lambda h: (h, 0, 0))
    gain = pl.BlockSpec((1, HD), lambda h: (0, h))
    return head, block, lower, weights, gain


def attend_call(length, raw, inv, gain, moved, tokens):
    parts = len(moved)
    cols = moved[0].shape[1]
    heads = cols // HD
    head, block, lower, weights, gains = specs(tokens)
    outs = pl.pallas_call(
        functools.partial(attend_kernel, parts),
        grid=(heads,),
        in_specs=[
            pl.BlockSpec(memory_space=pltpu.SMEM),
            head,
            pl.BlockSpec((LIVE, 1), lambda h: (0, 0)),
            gains,
        ]
        + [block] * parts
        + [lower] * parts,
        out_specs=[weights] * parts + [head, head],
        out_shape=[jax.ShapeDtypeStruct((heads, LIVE, tokens), jnp.float32)] * parts
        + [jax.ShapeDtypeStruct((LIVE, cols), jnp.bfloat16)] * 2,
        compiler_params=pltpu.CompilerParams(vmem_limit_bytes=32 * 1024 * 1024),
        cost_estimate=pl.CostEstimate(
            flops=16 * parts * tokens * cols * LIVE,
            bytes_accessed=16 * parts * tokens * cols,
            transcendentals=0,
        ),
    )(length, raw, inv, gain, *moved, *moved)
    return outs[:parts], outs[parts], outs[parts + 1]


def gradient_call(raw, keys, values, gain, moved, attends, tokens):
    parts = len(moved)
    cols = moved[0].shape[1]
    heads = cols // HD
    head, block, lower, weights, gains = specs(tokens)
    outs = pl.pallas_call(
        functools.partial(gradient_kernel, parts),
        grid=(heads,),
        in_specs=[head, head, head, gains] + [block] * parts + [lower] * parts + [weights] * parts,
        out_specs=[block] * parts + [head, pl.BlockSpec((LIVE, HD), lambda h: (0, 0))],
        out_shape=[jax.ShapeDtypeStruct((tokens, cols), jnp.bfloat16)] * parts
        + [
            jax.ShapeDtypeStruct((LIVE, cols), jnp.float32),
            jax.ShapeDtypeStruct((LIVE, HD), jnp.float32),
        ],
        compiler_params=pltpu.CompilerParams(vmem_limit_bytes=32 * 1024 * 1024),
        cost_estimate=pl.CostEstimate(
            flops=24 * parts * tokens * cols * LIVE,
            bytes_accessed=16 * parts * tokens * cols,
            transcendentals=0,
        ),
    )(raw, keys, values, gain, *moved, *moved, *attends)
    return outs[:parts], outs[parts], outs[parts + 1]


def rows_spec(part, width, tiled=False):
    _, count, index = part
    if tiled:
        return pl.BlockSpec((count, width), lambda n: (index, n))
    return pl.BlockSpec((count, width), lambda n: (index, 0))


def product_kernel(videos, place_ref, *refs):
    mine_refs, sibling_refs = refs[:videos], refs[videos : 2 * videos]
    weight_refs, out_ref = refs[2 * videos : -1], refs[-1]
    rows = weight_refs[0].shape[0]
    total = None
    for step, weight_ref in enumerate(weight_refs):
        here = place_ref[step // 2] == 0
        at = pl.ds(pl.multiple_of(place_ref[2 + step % 2] * rows, rows), rows)
        block = jnp.concatenate(
            [jnp.where(here, m[:, at], s[:, at]) for m, s in zip(mine_refs, sibling_refs)], axis=0
        )
        term = jnp.dot(block, weight_ref[...], preferred_element_type=jnp.float32)
        total = term if total is None else total + term
    out_ref[...] = total


def product_call(place, mine, sibling, weights):
    videos = len(mine)
    width = weights[0][0].shape[1]
    parts = [*mine, *sibling, *weights]
    return pl.pallas_call(
        functools.partial(product_kernel, videos),
        grid=(1,),
        in_specs=[pl.BlockSpec(memory_space=pltpu.SMEM)]
        + [rows_spec(part, part[0].shape[1]) for part in parts],
        out_specs=pl.BlockSpec((videos * LIVE, width), lambda n: (0, 0)),
        out_shape=jax.ShapeDtypeStruct((videos * LIVE, width), jnp.float32),
        compiler_params=pltpu.CompilerParams(vmem_limit_bytes=32 * 1024 * 1024),
        cost_estimate=pl.CostEstimate(flops=1000, bytes_accessed=1000, transcendentals=0),
    )(place, *[part[0] for part in parts])


def weights_kernel(videos, columns_ref, *refs):
    part_refs, out_refs = refs[:-2], refs[-2:]
    for index, out_ref in enumerate(out_refs):
        parts = [ref[...] for ref in part_refs[index * videos : (index + 1) * videos]]
        out_ref[...] = jnp.dot(
            columns_ref[...], jnp.concatenate(parts, axis=0), preferred_element_type=jnp.float32
        )


def weights_call(columns, parts):
    rows, videos = columns.shape[0], len(parts) // 2
    cols = parts[0][0].shape[1]
    tile = min(cols, 512)
    return pl.pallas_call(
        functools.partial(weights_kernel, videos),
        grid=(cols // tile,),
        in_specs=[pl.BlockSpec(columns.shape, lambda n: (0, 0))]
        + [rows_spec(part, tile, True) for part in parts],
        out_specs=[pl.BlockSpec((rows, tile), lambda n: (0, n))] * 2,
        out_shape=[jax.ShapeDtypeStruct((rows, cols), jnp.float32)] * 2,
        compiler_params=pltpu.CompilerParams(vmem_limit_bytes=32 * 1024 * 1024),
        cost_estimate=pl.CostEstimate(
            flops=4 * rows * cols * videos * LIVE,
            bytes_accessed=8 * rows * cols + 4 * videos * LIVE * cols,
            transcendentals=0,
        ),
    )(columns, *[part[0] for part in parts])


def after(x, *others):
    return lax.optimization_barrier((x, *others))[0]


def shards(n_dp, n_seq, query, caption, key_weight, value_weight, key_gain, lengths, out_grad):
    rows, cols = key_weight.shape
    hid = cols * n_seq
    lines = n_dp // 2
    half = cols // 2
    me = lax.axis_index("dp")
    lane = lax.axis_index("seq")
    quad, low, side = me // 4, me // 2 % 2, me % 2
    core = lane % 2

    def over_dp(x, step):
        return lax.ppermute(x, "dp", [(a, a ^ step) for a in range(n_dp)])

    def over_seq(x, step):
        return lax.ppermute(x, "seq", [(a, a ^ step) for a in range(n_seq)])

    def col_block(x, index, width):
        return lax.dynamic_slice(x, (0, index * width), (x.shape[0], width))

    key_given = col_block(key_weight, 1 - low, half)
    kept = jnp.concatenate(
        [col_block(key_weight, low, half), col_block(value_weight, low, half)], axis=0
    )

    captions = caption[0, :LIVE]
    given = [col_block(captions, (quad ^ (s // 2)) * 2 + core, 2 * rows) for s in range(lines)]
    pieces = 2 * rows // half
    near = over_dp(
        jnp.concatenate(
            [key_given] + [given[1][:, p * half : (p + 1) * half] for p in range(pieces)], axis=0
        ),
        2,
    )
    beside = over_dp(kept, 1)
    arrived = [over_dp(given[s], 2 * s) for s in range(2, lines)]
    near_columns = jnp.concatenate(
        [near[rows + p * LIVE : rows + (p + 1) * LIVE] for p in range(pieces)], axis=1
    )
    mine = [given[0], near_columns, *arrived]
    shared = over_seq(jnp.concatenate(mine[1:], axis=0), 1)
    first = col_block(captions, quad * 2 + 1 - core, 2 * rows)
    key_far = over_dp(near[:rows], 1)
    value_given = col_block(value_weight, 1 - low, half)
    value_near = over_dp(after(value_given, near, *arrived), 2)

    tokens = query.shape[1]

    def both(index):
        return jnp.concatenate(
            [col_block(query[0], index, cols), col_block(out_grad[0], index, cols)], axis=0
        )

    moved = [both(lane)] + [None] * (n_seq - 1)
    previous = ()
    for s in range(2, n_seq):
        moved[s] = over_seq(after(both(lane ^ s), *previous), s)
        previous = (moved[s],)
    moved[1] = over_seq(after(both(lane ^ 1), beside), 1)

    value_far = over_dp(after(value_near, moved[2 % n_seq]), 1)
    key_quad = ((kept, rows, 0), (beside, rows, 0), (near, rows, 0), (key_far, rows, 0))
    value_quad = ((kept, rows, 1), (beside, rows, 1), (value_near, rows, 0), (value_far, rows, 0))

    place = jnp.stack([core ^ low, 1 - (core ^ low), side, 1 - side]).astype(jnp.int32)

    def product(weights, other):
        chosen = [s for s in range(lines) if bool(s & 2) == other]
        return product_call(
            place,
            [(mine[s], LIVE, 0) for s in chosen],
            [(shared, LIVE, s - 1) if s else (first, LIVE, 0) for s in chosen],
            weights,
        )

    def reduced(total):
        step = 8
        while step < n_dp:
            count = total.shape[0] // 2
            total = total[:count] + over_dp(total[count:], step)
            step *= 2
        return lax.reduce_precision(total, 8, 7).astype(jnp.bfloat16)

    def joined(total):
        own, other = total[:LIVE], over_dp(total[LIVE:], 2)
        return jnp.where(
            low == 0,
            jnp.concatenate([own, other], axis=1),
            jnp.concatenate([other, own], axis=1),
        )

    def seq_sum(x):
        step = 1
        while step < n_seq:
            x = x + over_seq(x, step)
            step *= 2
        return x

    key_sent = over_dp(product(key_quad, True), 4)
    value_sent = over_dp(product(value_quad, True), 4)
    key_total = reduced(product(key_quad, False) + key_sent)
    raw = joined(key_total)
    raw_wide = raw.astype(jnp.float32)
    squares = seq_sum(jnp.sum(raw_wide * raw_wide, axis=-1, keepdims=True))
    inv_rms = lax.rsqrt(squares / hid + 1e-06)
    gain = lax.dynamic_slice(key_gain, (lane * cols,), (cols,)).reshape(1, cols)
    attends, keys, value_grad = attend_call(lengths, raw, inv_rms, gain, moved, tokens)
    values = joined(reduced(product(value_quad, False) + after(value_sent, value_grad)))

    value_sent_grad = after(value_grad, values)
    value_near_parts = [over_dp(value_sent_grad, 2 * s) for s in range(1, lines)]
    value_first = over_dp(value_sent_grad, 1)
    outs, scaled, inner = gradient_call(raw, keys, values, gain, moved, attends, tokens)
    inner = after(inner, value_first, *value_near_parts)
    inner_mean = seq_sum(jnp.sum(inner, axis=-1, keepdims=True)) / hid
    raw_grad = (inv_rms * scaled - raw_wide * inv_rms**3 * inner_mean).astype(jnp.bfloat16)
    value_rest = over_dp(jnp.concatenate(value_near_parts, axis=0), 1)
    key_near_parts = [over_dp(raw_grad, 2 * s) for s in range(1, lines)]
    placed = [outs[0]] + [None] * (n_seq - 1)
    previous = (inner_mean,)
    for s in [*range(2, n_seq), 1]:
        placed[s] = over_seq(after(outs[s], *previous), s)
        previous = (placed[s], value_rest, *key_near_parts)
    split = lines // 2
    key_first = over_dp(
        after(jnp.concatenate([raw_grad, *key_near_parts[: split - 1]], axis=0), value_rest), 1
    )
    key_rest = over_dp(
        after(jnp.concatenate(key_near_parts[split - 1 :], axis=0), placed[2 % n_seq]), 1
    )

    held = [
        jnp.where(core == low, mine[s], shared[(s - 1) * LIVE : s * LIVE] if s else first)
        for s in range(lines)
    ]
    other_columns = over_dp(jnp.concatenate([col_block(x, 1 - side, rows) for x in held], axis=0), 1)
    columns = jnp.concatenate([col_block(x, side, rows) for x in held] + [other_columns], axis=0).T
    key_parts = (
        [(x, LIVE, 0) for x in (raw_grad, *key_near_parts)]
        + [(key_first, LIVE, s) for s in range(split)]
        + [(key_rest, LIVE, s) for s in range(split)]
    )
    value_parts = (
        [(x, LIVE, 0) for x in (value_grad, *value_near_parts)]
        + [(value_first, LIVE, 0)]
        + [(value_rest, LIVE, s) for s in range(lines - 1)]
    )
    key_weight_grad, value_weight_grad = weights_call(columns, key_parts + value_parts)

    stacked = jnp.stack(placed)
    query_grad = jnp.concatenate(
        [lax.dynamic_index_in_dim(stacked, lane ^ h, 0, keepdims=False) for h in range(n_seq)],
        axis=1,
    )[None]
    return query_grad, key_weight_grad, value_weight_grad


def solution(mesh):
    placed = (
        P("dp", "seq", None),
        P("dp", None, None),
        P("dp", "seq"),
        P("dp", "seq"),
        P(),
        P("dp"),
        P("dp", "seq", None),
    )
    return jax.shard_map(
        functools.partial(shards, mesh.shape["dp"], mesh.shape["seq"]),
        mesh=mesh,
        in_specs=placed,
        out_specs=(P("dp", "seq", None), P("dp", "seq"), P("dp", "seq")),
        check_vma=False,
    )
```

```python
import functools

import jax
import jax.numpy as jnp
from jax import lax
from jax.experimental import pallas as pl
from jax.experimental.pallas import tpu as pltpu
from jax.sharding import PartitionSpec as P

HD = 128
LIVE = 128
VMEM = 60 * 1024 * 1024


ROWS = (((1,), (1,)), ((), ()))
COLUMNS = (((0,), (0,)), ((), ()))
FACTOR = HD ** (-0.5)


def attend_kernel(parts, length_ref, raw_ref, inv_ref, gain_ref, *refs):
    query_refs, grad_refs = refs[:parts], refs[parts : 2 * parts]
    attend_refs = refs[2 * parts : 3 * parts]
    keys_ref, value_grad_ref = refs[3 * parts :]
    raw = raw_ref[...].astype(jnp.float32)
    keys = (raw * inv_ref[...] * gain_ref[...]).astype(jnp.bfloat16)
    keys_ref[...] = keys
    valid = lax.broadcasted_iota(jnp.int32, (LIVE, 1), 0) < length_ref[0]
    value_grad = jnp.zeros((LIVE, HD), jnp.float32)
    for query_ref, grad_ref, attend_ref in zip(query_refs, grad_refs, attend_refs):
        scores = lax.dot_general(keys, query_ref[...], ROWS, preferred_element_type=jnp.float32)
        scores = jnp.where(valid, scores * FACTOR, -jnp.inf)
        powers = jnp.exp(scores - jnp.max(scores, axis=0, keepdims=True))
        attend = powers * (1.0 / jnp.sum(powers, axis=0, keepdims=True))
        attend_ref[0] = attend
        value_grad += jnp.dot(
            attend.astype(jnp.bfloat16), grad_ref[...], preferred_element_type=jnp.float32
        )
    value_grad_ref[...] = value_grad.astype(jnp.bfloat16)


def gradient_kernel(parts, raw_ref, keys_ref, value_ref, gain_ref, *refs):
    query_refs, grad_refs = refs[:parts], refs[parts : 2 * parts]
    attend_refs, out_refs = refs[2 * parts : 3 * parts], refs[3 * parts : 4 * parts]
    scaled_ref, inner_ref = refs[4 * parts :]
    keys, values = keys_ref[...], value_ref[...]
    key_grad = jnp.zeros((LIVE, HD), jnp.float32)
    for query_ref, grad_ref, attend_ref, out_ref in zip(
        query_refs, grad_refs, attend_refs, out_refs
    ):
        attend = attend_ref[0]
        dattend = lax.dot_general(values, grad_ref[...], ROWS, preferred_element_type=jnp.float32)
        delta = jnp.sum(attend * dattend, axis=0, keepdims=True)
        dscores = (attend * (dattend - delta)).astype(jnp.bfloat16)
        out = lax.dot_general(dscores, keys, COLUMNS, preferred_element_type=jnp.float32)
        out_ref[...] = (out * FACTOR).astype(jnp.bfloat16)
        key_grad += jnp.dot(dscores, query_ref[...], preferred_element_type=jnp.float32)
    scaled = key_grad * FACTOR * gain_ref[...]
    scaled_ref[...] = scaled

    @pl.when(pl.program_id(0) == 0)
    def _():
        inner_ref[...] = jnp.zeros_like(inner_ref)

    inner_ref[...] += scaled * raw_ref[...].astype(jnp.float32)


def specs(tokens):
    head = pl.BlockSpec((LIVE, HD), lambda h: (0, h))
    block = pl.BlockSpec((tokens, HD), lambda h: (0, h))
    lower = pl.BlockSpec((tokens, HD), lambda h: (1, h))
    weights = pl.BlockSpec((1, LIVE, tokens), lambda h: (h, 0, 0))
    gain = pl.BlockSpec((1, HD), lambda h: (0, h))
    return head, block, lower, weights, gain


def attend_call(length, raw, inv, gain, moved, tokens):
    parts = len(moved)
    cols = moved[0].shape[1]
    heads = cols // HD
    head, block, lower, weights, gains = specs(tokens)
    outs = pl.pallas_call(
        functools.partial(attend_kernel, parts),
        grid=(heads,),
        in_specs=[
            pl.BlockSpec(memory_space=pltpu.SMEM),
            head,
            pl.BlockSpec((LIVE, 1), lambda h: (0, 0)),
            gains,
        ]
        + [block] * parts
        + [lower] * parts,
        out_specs=[weights] * parts + [head, head],
        out_shape=[jax.ShapeDtypeStruct((heads, LIVE, tokens), jnp.float32)] * parts
        + [jax.ShapeDtypeStruct((LIVE, cols), jnp.bfloat16)] * 2,
        compiler_params=pltpu.CompilerParams(vmem_limit_bytes=VMEM),
        cost_estimate=pl.CostEstimate(
            flops=16 * parts * tokens * cols * LIVE,
            bytes_accessed=16 * parts * tokens * cols,
            transcendentals=0,
        ),
    )(length, raw, inv, gain, *moved, *moved)
    return outs[:parts], outs[parts], outs[parts + 1]


def gradient_call(raw, keys, values, gain, moved, attends, tokens):
    parts = len(moved)
    cols = moved[0].shape[1]
    heads = cols // HD
    head, block, lower, weights, gains = specs(tokens)
    outs = pl.pallas_call(
        functools.partial(gradient_kernel, parts),
        grid=(heads,),
        in_specs=[head, head, head, gains] + [block] * parts + [lower] * parts + [weights] * parts,
        out_specs=[block] * parts + [head, pl.BlockSpec((LIVE, HD), lambda h: (0, 0))],
        out_shape=[jax.ShapeDtypeStruct((tokens, cols), jnp.bfloat16)] * parts
        + [
            jax.ShapeDtypeStruct((LIVE, cols), jnp.float32),
            jax.ShapeDtypeStruct((LIVE, HD), jnp.float32),
        ],
        compiler_params=pltpu.CompilerParams(vmem_limit_bytes=VMEM),
        cost_estimate=pl.CostEstimate(
            flops=24 * parts * tokens * cols * LIVE,
            bytes_accessed=16 * parts * tokens * cols,
            transcendentals=0,
        ),
    )(raw, keys, values, gain, *moved, *moved, *attends)
    return outs[:parts], outs[parts], outs[parts + 1]


def rows_spec(part, width, tiled=False):
    _, count, index = part
    if tiled:
        return pl.BlockSpec((count, width), lambda n: (index, n))
    return pl.BlockSpec((count, width), lambda n: (index, 0))


def product_kernel(videos, place_ref, *refs):
    mine_refs, sibling_refs = refs[:videos], refs[videos : 2 * videos]
    weight_refs, out_ref = refs[2 * videos : -1], refs[-1]
    rows = weight_refs[0].shape[0]
    total = None
    for step, weight_ref in enumerate(weight_refs):
        here = place_ref[step // 2] == 0
        at = pl.ds(pl.multiple_of(place_ref[2 + step % 2] * rows, rows), rows)
        block = jnp.concatenate(
            [jnp.where(here, m[:, at], s[:, at]) for m, s in zip(mine_refs, sibling_refs)], axis=0
        )
        term = jnp.dot(block, weight_ref[...], preferred_element_type=jnp.float32)
        total = term if total is None else total + term
    out_ref[...] = total


def product_call(place, mine, sibling, weights):
    videos = len(mine)
    width = weights[0][0].shape[1]
    parts = [*mine, *sibling, *weights]
    return pl.pallas_call(
        functools.partial(product_kernel, videos),
        grid=(1,),
        in_specs=[pl.BlockSpec(memory_space=pltpu.SMEM)]
        + [rows_spec(part, part[0].shape[1]) for part in parts],
        out_specs=pl.BlockSpec((videos * LIVE, width), lambda n: (0, 0)),
        out_shape=jax.ShapeDtypeStruct((videos * LIVE, width), jnp.float32),
        compiler_params=pltpu.CompilerParams(vmem_limit_bytes=VMEM),
        cost_estimate=pl.CostEstimate(flops=1000, bytes_accessed=1000, transcendentals=0),
    )(place, *[part[0] for part in parts])


def weights_kernel(videos, columns_ref, *refs):
    part_refs, out_refs = refs[:-2], refs[-2:]
    for index, out_ref in enumerate(out_refs):
        parts = [ref[...] for ref in part_refs[index * videos : (index + 1) * videos]]
        out_ref[...] = jnp.dot(
            columns_ref[...], jnp.concatenate(parts, axis=0), preferred_element_type=jnp.float32
        )


def weights_call(columns, parts):
    rows, videos = columns.shape[0], len(parts) // 2
    cols = parts[0][0].shape[1]
    tile = min(cols, 512)
    return pl.pallas_call(
        functools.partial(weights_kernel, videos),
        grid=(cols // tile,),
        in_specs=[pl.BlockSpec(columns.shape, lambda n: (0, 0))]
        + [rows_spec(part, tile, True) for part in parts],
        out_specs=[pl.BlockSpec((rows, tile), lambda n: (0, n))] * 2,
        out_shape=[jax.ShapeDtypeStruct((rows, cols), jnp.float32)] * 2,
        compiler_params=pltpu.CompilerParams(vmem_limit_bytes=VMEM),
        cost_estimate=pl.CostEstimate(
            flops=4 * rows * cols * videos * LIVE,
            bytes_accessed=8 * rows * cols + 4 * videos * LIVE * cols,
            transcendentals=0,
        ),
    )(columns, *[part[0] for part in parts])


def after(x, *others):
    return lax.optimization_barrier((x, *others))[0]


def pack_kernel(moves, inputs, place_ref, *refs):
    ins, outs, sems = refs[:inputs], refs[inputs:-1], refs[-1]

    def span(at, width):
        if isinstance(at, int):
            return pl.ds(at, width)
        return pl.ds(pl.multiple_of(place_ref[at[0]] * width, width), width)

    copies = []
    for index, (source, row, col, count, width, target, to_row, to_col) in enumerate(moves):
        copy = pltpu.make_async_copy(
            ins[source].at[pl.ds(row, count), span(col, width)],
            outs[target].at[pl.ds(to_row, count), span(to_col, width)],
            sems.at[index],
        )
        copy.start()
        copies.append(copy)
    for copy in copies:
        copy.wait()


def pack_call(place, arrays, shapes, moves):
    return pl.pallas_call(
        functools.partial(pack_kernel, moves, len(arrays)),
        in_specs=[pl.BlockSpec(memory_space=pltpu.SMEM)]
        + [pl.BlockSpec(memory_space=pl.ANY)] * len(arrays),
        out_specs=[pl.BlockSpec(memory_space=pl.ANY)] * len(shapes),
        out_shape=[jax.ShapeDtypeStruct(shape, jnp.bfloat16) for shape in shapes],
        scratch_shapes=[pltpu.SemaphoreType.DMA((len(moves),))],
        compiler_params=pltpu.CompilerParams(vmem_limit_bytes=VMEM),
        cost_estimate=pl.CostEstimate(flops=1000, bytes_accessed=1000, transcendentals=0),
    )(place, *arrays)


def shards(n_dp, n_seq, query, caption, key_weight, value_weight, key_gain, lengths, out_grad):
    rows, cols = key_weight.shape
    hid = cols * n_seq
    lines = n_dp // 2
    half = cols // 2
    wide = 2 * rows
    tokens = query.shape[1]
    me = lax.axis_index("dp")
    lane = lax.axis_index("seq")
    quad, low, side = me // 4, me // 2 % 2, me % 2
    core = lane % 2

    def over_dp(x, step):
        return lax.ppermute(x, "dp", [(a, a ^ step) for a in range(n_dp)])

    def over_seq(x, step):
        return lax.ppermute(x, "seq", [(a, a ^ step) for a in range(n_seq)])

    def col_block(x, index, width):
        return lax.dynamic_slice(x, (0, index * width), (x.shape[0], width))

    pieces = wide // half
    quads = lines // 2
    scalars = [low, 1 - low, quad * 2 + core, quad * 2 + 1 - core]
    scalars += [(quad ^ (s // 2)) * 2 + core for s in range(2, lines)]
    scalars += [(quad * 2 + core) * pieces + p for p in range(pieces)]
    place = jnp.stack(scalars).astype(jnp.int32)
    near_at = lines + 2
    near_given, kept, mine_first, sibling_first, *given = pack_call(
        place,
        [key_weight, value_weight, caption[0]],
        [(2 * rows + pieces * LIVE, half), (2 * rows, half)] + [(LIVE, wide)] * lines,
        [
            (0, 0, (1,), rows, half, 0, 0, 0),
            (1, 0, (1,), rows, half, 0, rows, 0),
        ]
        + [
            (2, 0, (near_at + p,), LIVE, half, 0, 2 * rows + p * LIVE, 0) for p in range(pieces)
        ]
        + [
            (0, 0, (0,), rows, half, 1, 0, 0),
            (1, 0, (0,), rows, half, 1, rows, 0),
        ]
        + [(2, 0, (2 + s,), LIVE, wide, 2 + s, 0, 0) for s in range(lines)],
    )
    near = over_dp(near_given, 2)
    beside = over_dp(kept, 1)
    arrived = [over_dp(x, 2 * s) for s, x in enumerate(given, 2)]

    lanes = jnp.stack([lane ^ s for s in range(n_seq)]).astype(jnp.int32)
    packed = pack_call(
        after(lanes, kept),
        [query[0], out_grad[0]],
        [(2 * tokens, cols)] * n_seq,
        [
            (source, 0, (s,), tokens, cols, s, source * tokens, 0)
            for s in [*range(2, n_seq), 1, 0]
            for source in range(2)
        ],
    )
    moved = [packed[0]] + [None] * (n_seq - 1)
    previous = ()
    for s in range(2, n_seq):
        moved[s] = over_seq(after(packed[s], *previous), s)
        previous = (moved[s],)
    moved[1] = over_seq(after(packed[1], beside), 1)

    key_near, value_near, shared = pack_call(
        place,
        [near, *arrived],
        [(rows, half), (rows, half), ((lines - 1) * LIVE, wide)],
        [(0, 0, 0, rows, half, 0, 0, 0), (0, rows, 0, rows, half, 1, 0, 0)]
        + [
            (0, 2 * rows + p * LIVE, 0, LIVE, half, 2, 0, p * half) for p in range(pieces)
        ]
        + [(s - 1, 0, 0, LIVE, wide, 2, (s - 1) * LIVE, 0) for s in range(2, lines)],
    )
    key_far = over_dp(key_near, 1)
    value_far = over_dp(value_near, 1)
    sibling = over_seq(shared, 1)
    key_quad = ((kept, rows, 0), (beside, rows, 0), (key_near, rows, 0), (key_far, rows, 0))
    value_quad = ((kept, rows, 1), (beside, rows, 1), (value_near, rows, 0), (value_far, rows, 0))

    places = jnp.stack([core ^ low, 1 - (core ^ low), side, 1 - side]).astype(jnp.int32)

    def product(weights, other):
        chosen = [s for s in range(lines) if bool(s & 2) == other]
        return product_call(
            places,
            [(shared, LIVE, s - 1) if s else (mine_first, LIVE, 0) for s in chosen],
            [(sibling, LIVE, s - 1) if s else (sibling_first, LIVE, 0) for s in chosen],
            weights,
        )

    def reduced(total):
        step = 8
        while step < n_dp:
            count = total.shape[0] // 2
            total = total[:count] + over_dp(total[count:], step)
            step *= 2
        return lax.reduce_precision(total, 8, 7).astype(jnp.bfloat16)

    def joined(total):
        own, other = total[:LIVE], over_dp(total[LIVE:], 2)
        return jnp.where(
            low == 0,
            jnp.concatenate([own, other], axis=1),
            jnp.concatenate([other, own], axis=1),
        )

    def seq_sum(x):
        step = 1
        while step < n_seq:
            x = x + over_seq(x, step)
            step *= 2
        return x

    own = jnp.concatenate([mine_first, shared], axis=0)
    other = jnp.concatenate([sibling_first, sibling], axis=0)
    held = jnp.where(core == low, own, other)
    other_columns = over_dp(col_block(held, 1 - side, rows), 1)
    columns = jnp.concatenate([col_block(held, side, rows), other_columns], axis=0).T

    key_sent = over_dp(product(key_quad, True), 4)
    value_sent = over_dp(product(value_quad, True), 4)
    key_total = reduced(product(key_quad, False) + after(key_sent, value_far))
    raw = joined(key_total)
    raw_wide = raw.astype(jnp.float32)
    squares = seq_sum(jnp.sum(raw_wide * raw_wide, axis=-1, keepdims=True))
    inv_rms = lax.rsqrt(squares / hid + 1e-06)
    gain = lax.dynamic_slice(key_gain, (lane * cols,), (cols,)).reshape(1, cols)
    attends, keys, value_grad = attend_call(
        lengths, after(raw, columns), inv_rms, gain, moved, tokens
    )
    values = joined(reduced(product(value_quad, False) + after(value_sent, value_grad)))

    value_given = after(value_grad, values)
    value_near_parts = [over_dp(value_given, 2 * s) for s in range(1, lines)]
    value_first = over_dp(value_given, 1)
    outs, scaled, inner = gradient_call(raw, keys, values, gain, moved, attends, tokens)
    inner = after(inner, value_first, *value_near_parts)
    inner_mean = seq_sum(jnp.sum(inner, axis=-1, keepdims=True)) / hid
    raw_grad = (inv_rms * scaled - raw_wide * inv_rms**3 * inner_mean).astype(jnp.bfloat16)
    value_rest = over_dp(jnp.concatenate(value_near_parts, axis=0), 1)
    key_near_parts = [over_dp(raw_grad, 2 * s) for s in range(1, lines)]
    placed = [outs[0]] + [None] * (n_seq - 1)
    previous = (inner_mean,)
    for s in range(2, n_seq):
        placed[s] = over_seq(after(outs[s], *previous), s)
        previous = (placed[s], value_rest, *key_near_parts)
    placed[1] = over_seq(after(outs[1], value_rest), 1)
    split = lines // 2
    key_first = over_dp(
        after(jnp.concatenate([raw_grad, *key_near_parts[: split - 1]], axis=0), value_rest), 1
    )
    key_rest = over_dp(jnp.concatenate(key_near_parts[split - 1 :], axis=0), 1)
    key_parts = (
        [(x, LIVE, 0) for x in (raw_grad, *key_near_parts)]
        + [(key_first, LIVE, s) for s in range(split)]
        + [(key_rest, LIVE, s) for s in range(split)]
    )
    value_parts = (
        [(x, LIVE, 0) for x in (value_grad, *value_near_parts)]
        + [(value_first, LIVE, 0)]
        + [(value_rest, LIVE, s) for s in range(lines - 1)]
    )
    key_weight_grad, value_weight_grad = weights_call(columns, key_parts + value_parts)

    (query_grad,) = pack_call(
        lanes,
        placed,
        [(tokens, hid)],
        [(s, 0, 0, tokens, cols, 0, 0, (s,)) for s in range(n_seq)],
    )
    return query_grad[None], key_weight_grad, value_weight_grad


def solution(mesh):
    placed = (
        P("dp", "seq", None),
        P("dp", None, None),
        P("dp", "seq"),
        P("dp", "seq"),
        P(),
        P("dp"),
        P("dp", "seq", None),
    )
    return jax.shard_map(
        functools.partial(shards, mesh.shape["dp"], mesh.shape["seq"]),
        mesh=mesh,
        in_specs=placed,
        out_specs=(P("dp", "seq", None), P("dp", "seq"), P("dp", "seq")),
        check_vma=False,
    )
```

```python
import functools

import jax
import jax.numpy as jnp
from jax import lax
from jax.experimental import pallas as pl
from jax.experimental.pallas import tpu as pltpu
from jax.sharding import PartitionSpec as P

HD = 128
LIVE = 128
VMEM = 60 * 1024 * 1024


ROWS = (((1,), (1,)), ((), ()))
COLUMNS = (((0,), (0,)), ((), ()))
FACTOR = HD ** (-0.5)


def attend_kernel(parts, length_ref, raw_ref, inv_ref, gain_ref, *refs):
    query_refs, grad_refs = refs[:parts], refs[parts : 2 * parts]
    attend_refs = refs[2 * parts : 3 * parts]
    keys_ref, value_grad_ref = refs[3 * parts :]
    raw = raw_ref[...].astype(jnp.float32)
    keys = (raw * inv_ref[...] * gain_ref[...]).astype(jnp.bfloat16)
    keys_ref[...] = keys
    valid = lax.broadcasted_iota(jnp.int32, (LIVE, 1), 0) < length_ref[0]
    value_grad = jnp.zeros((LIVE, HD), jnp.float32)
    for query_ref, grad_ref, attend_ref in zip(query_refs, grad_refs, attend_refs):
        scores = lax.dot_general(keys, query_ref[...], ROWS, preferred_element_type=jnp.float32)
        scores = jnp.where(valid, scores * FACTOR, -jnp.inf)
        powers = jnp.exp(scores - jnp.max(scores, axis=0, keepdims=True))
        attend = powers * (1.0 / jnp.sum(powers, axis=0, keepdims=True))
        attend_ref[0] = attend
        value_grad += jnp.dot(
            attend.astype(jnp.bfloat16), grad_ref[...], preferred_element_type=jnp.float32
        )
    value_grad_ref[...] = value_grad.astype(jnp.bfloat16)


def gradient_kernel(parts, raw_ref, keys_ref, value_ref, gain_ref, *refs):
    query_refs, grad_refs = refs[:parts], refs[parts : 2 * parts]
    attend_refs, out_refs = refs[2 * parts : 3 * parts], refs[3 * parts : 4 * parts]
    scaled_ref, inner_ref = refs[4 * parts :]
    keys, values = keys_ref[...], value_ref[...]
    key_grad = jnp.zeros((LIVE, HD), jnp.float32)
    for query_ref, grad_ref, attend_ref, out_ref in zip(
        query_refs, grad_refs, attend_refs, out_refs
    ):
        attend = attend_ref[0]
        dattend = lax.dot_general(values, grad_ref[...], ROWS, preferred_element_type=jnp.float32)
        delta = jnp.sum(attend * dattend, axis=0, keepdims=True)
        dscores = (attend * (dattend - delta)).astype(jnp.bfloat16)
        out = lax.dot_general(dscores, keys, COLUMNS, preferred_element_type=jnp.float32)
        out_ref[...] = (out * FACTOR).astype(jnp.bfloat16)
        key_grad += jnp.dot(dscores, query_ref[...], preferred_element_type=jnp.float32)
    scaled = key_grad * FACTOR * gain_ref[...]
    scaled_ref[...] = scaled

    @pl.when(pl.program_id(0) == 0)
    def _():
        inner_ref[...] = jnp.zeros_like(inner_ref)

    inner_ref[...] += scaled * raw_ref[...].astype(jnp.float32)


def specs(tokens):
    head = pl.BlockSpec((LIVE, HD), lambda h: (0, h))
    block = pl.BlockSpec((tokens, HD), lambda h: (0, h))
    lower = pl.BlockSpec((tokens, HD), lambda h: (1, h))
    weights = pl.BlockSpec((1, LIVE, tokens), lambda h: (h, 0, 0))
    gain = pl.BlockSpec((1, HD), lambda h: (0, h))
    return head, block, lower, weights, gain


def attend_call(length, raw, inv, gain, moved, tokens):
    parts = len(moved)
    cols = moved[0].shape[1]
    heads = cols // HD
    head, block, lower, weights, gains = specs(tokens)
    outs = pl.pallas_call(
        functools.partial(attend_kernel, parts),
        grid=(heads,),
        in_specs=[
            pl.BlockSpec(memory_space=pltpu.SMEM),
            head,
            pl.BlockSpec((LIVE, 1), lambda h: (0, 0)),
            gains,
        ]
        + [block] * parts
        + [lower] * parts,
        out_specs=[weights] * parts + [head, head],
        out_shape=[jax.ShapeDtypeStruct((heads, LIVE, tokens), jnp.float32)] * parts
        + [jax.ShapeDtypeStruct((LIVE, cols), jnp.bfloat16)] * 2,
        compiler_params=pltpu.CompilerParams(vmem_limit_bytes=VMEM),
        cost_estimate=pl.CostEstimate(
            flops=16 * parts * tokens * cols * LIVE,
            bytes_accessed=16 * parts * tokens * cols,
            transcendentals=0,
        ),
    )(length, raw, inv, gain, *moved, *moved)
    return outs[:parts], outs[parts], outs[parts + 1]


def gradient_call(raw, keys, values, gain, moved, attends, tokens):
    parts = len(moved)
    cols = moved[0].shape[1]
    heads = cols // HD
    head, block, lower, weights, gains = specs(tokens)
    outs = pl.pallas_call(
        functools.partial(gradient_kernel, parts),
        grid=(heads,),
        in_specs=[head, head, head, gains] + [block] * parts + [lower] * parts + [weights] * parts,
        out_specs=[block] * parts + [head, pl.BlockSpec((LIVE, HD), lambda h: (0, 0))],
        out_shape=[jax.ShapeDtypeStruct((tokens, cols), jnp.bfloat16)] * parts
        + [
            jax.ShapeDtypeStruct((LIVE, cols), jnp.float32),
            jax.ShapeDtypeStruct((LIVE, HD), jnp.float32),
        ],
        compiler_params=pltpu.CompilerParams(vmem_limit_bytes=VMEM),
        cost_estimate=pl.CostEstimate(
            flops=24 * parts * tokens * cols * LIVE,
            bytes_accessed=16 * parts * tokens * cols,
            transcendentals=0,
        ),
    )(raw, keys, values, gain, *moved, *moved, *attends)
    return outs[:parts], outs[parts], outs[parts + 1]


def rows_spec(part, width, tiled=False):
    _, count, index = part
    if tiled:
        return pl.BlockSpec((count, width), lambda n: (index, n))
    return pl.BlockSpec((count, width), lambda n: (index, 0))


def pick_kernel(place_ref, first_ref, mine_ref, sibling_first_ref, sibling_ref, *out_refs):
    here = place_ref[0] == 0
    rows = out_refs[0].shape[1]
    for index, out_ref in enumerate(out_refs):
        at = pl.ds(pl.multiple_of(place_ref[2 + index] * rows, rows), rows)
        out_ref[:LIVE] = jnp.where(here, first_ref[:, at], sibling_first_ref[:, at])
        out_ref[LIVE:] = jnp.where(here, mine_ref[:, at], sibling_ref[:, at])


def pick_call(place, first, mine, sibling_first, sibling, rows):
    arrays = (first, mine, sibling_first, sibling)
    shape = (LIVE + mine.shape[0], rows)
    return pl.pallas_call(
        pick_kernel,
        grid=(1,),
        in_specs=[pl.BlockSpec(memory_space=pltpu.SMEM)]
        + [pl.BlockSpec(x.shape, lambda n: (0, 0)) for x in arrays],
        out_specs=[pl.BlockSpec(shape, lambda n: (0, 0))] * 2,
        out_shape=[jax.ShapeDtypeStruct(shape, jnp.bfloat16)] * 2,
        compiler_params=pltpu.CompilerParams(vmem_limit_bytes=VMEM),
        cost_estimate=pl.CostEstimate(flops=1000, bytes_accessed=1000, transcendentals=0),
    )(place, *arrays)


def product_kernel(videos, place_ref, *refs):
    mine_refs, sibling_refs = refs[:videos], refs[videos : 2 * videos]
    weight_refs, out_ref = refs[2 * videos : -1], refs[-1]
    rows = weight_refs[0].shape[0]
    total = None
    for step, weight_ref in enumerate(weight_refs):
        here = place_ref[step // 2] == 0
        at = pl.ds(pl.multiple_of(place_ref[2 + step % 2] * rows, rows), rows)
        block = jnp.concatenate(
            [jnp.where(here, m[:, at], s[:, at]) for m, s in zip(mine_refs, sibling_refs)], axis=0
        )
        term = jnp.dot(block, weight_ref[...], preferred_element_type=jnp.float32)
        total = term if total is None else total + term
    out_ref[...] = total


def product_call(place, mine, sibling, weights):
    videos = len(mine)
    width = weights[0][0].shape[1]
    parts = [*mine, *sibling, *weights]
    return pl.pallas_call(
        functools.partial(product_kernel, videos),
        grid=(1,),
        in_specs=[pl.BlockSpec(memory_space=pltpu.SMEM)]
        + [rows_spec(part, part[0].shape[1]) for part in parts],
        out_specs=pl.BlockSpec((videos * LIVE, width), lambda n: (0, 0)),
        out_shape=jax.ShapeDtypeStruct((videos * LIVE, width), jnp.float32),
        compiler_params=pltpu.CompilerParams(vmem_limit_bytes=VMEM),
        cost_estimate=pl.CostEstimate(flops=1000, bytes_accessed=1000, transcendentals=0),
    )(place, *[part[0] for part in parts])


def weights_kernel(videos, columns_ref, *refs):
    part_refs, out_refs = refs[:-2], refs[-2:]
    for index, out_ref in enumerate(out_refs):
        parts = [ref[...] for ref in part_refs[index * videos : (index + 1) * videos]]
        out_ref[...] = jnp.dot(
            columns_ref[...], jnp.concatenate(parts, axis=0), preferred_element_type=jnp.float32
        )


def weights_call(columns, parts):
    rows, videos = columns.shape[0], len(parts) // 2
    cols = parts[0][0].shape[1]
    tile = min(cols, 512)
    return pl.pallas_call(
        functools.partial(weights_kernel, videos),
        grid=(cols // tile,),
        in_specs=[pl.BlockSpec(columns.shape, lambda n: (0, 0))]
        + [rows_spec(part, tile, True) for part in parts],
        out_specs=[pl.BlockSpec((rows, tile), lambda n: (0, n))] * 2,
        out_shape=[jax.ShapeDtypeStruct((rows, cols), jnp.float32)] * 2,
        compiler_params=pltpu.CompilerParams(vmem_limit_bytes=VMEM),
        cost_estimate=pl.CostEstimate(
            flops=4 * rows * cols * videos * LIVE,
            bytes_accessed=8 * rows * cols + 4 * videos * LIVE * cols,
            transcendentals=0,
        ),
    )(columns, *[part[0] for part in parts])


def after(x, *others):
    return lax.optimization_barrier((x, *others))[0]


def pack_kernel(moves, inputs, place_ref, *refs):
    ins, outs = refs[:inputs], refs[inputs:]

    def span(at, width):
        if isinstance(at, int):
            return pl.ds(at, width)
        return pl.ds(pl.multiple_of(place_ref[at[0]] * width, width), width)

    for source, row, col, count, width, target, to_row, to_col in moves:
        block = ins[source][pl.ds(row, count), span(col, width)]
        outs[target][pl.ds(to_row, count), span(to_col, width)] = block


def pack_call(place, arrays, shapes, moves, tiles=1, size=1000):
    def spec(shape):
        return pl.BlockSpec((shape[0] // tiles, shape[1]), lambda n: (n, 0))

    return pl.pallas_call(
        functools.partial(pack_kernel, moves, len(arrays)),
        grid=(tiles,),
        in_specs=[pl.BlockSpec(memory_space=pltpu.SMEM)] + [spec(x.shape) for x in arrays],
        out_specs=[spec(shape) for shape in shapes],
        out_shape=[jax.ShapeDtypeStruct(shape, jnp.bfloat16) for shape in shapes],
        compiler_params=pltpu.CompilerParams(vmem_limit_bytes=VMEM),
        cost_estimate=pl.CostEstimate(flops=1000, bytes_accessed=size, transcendentals=0),
    )(place, *arrays)


def shards(n_dp, n_seq, query, caption, key_weight, value_weight, key_gain, lengths, out_grad):
    rows, cols = key_weight.shape
    hid = cols * n_seq
    lines = n_dp // 2
    half = cols // 2
    wide = 2 * rows
    tokens = query.shape[1]
    me = lax.axis_index("dp")
    lane = lax.axis_index("seq")
    quad, low, side = me // 4, me // 2 % 2, me % 2
    core = lane % 2

    def over_dp(x, step):
        return lax.ppermute(x, "dp", [(a, a ^ step) for a in range(n_dp)])

    def over_seq(x, step):
        return lax.ppermute(x, "seq", [(a, a ^ step) for a in range(n_seq)])

    def col_block(x, index, width):
        return lax.dynamic_slice(x, (0, index * width), (x.shape[0], width))

    pieces = wide // half
    quads = lines // 2
    scalars = [low, 1 - low, quad * 2 + core, quad * 2 + 1 - core]
    scalars += [(quad ^ (s // 2)) * 2 + core for s in range(2, lines)]
    scalars += [(quad * 2 + core) * pieces + p for p in range(pieces)]
    place = jnp.stack(scalars).astype(jnp.int32)
    near_at = lines + 2
    near_given, kept, value_given, mine_first, sibling_first, *given = pack_call(
        place,
        [key_weight, value_weight, caption[0]],
        [(rows + pieces * LIVE, half), (2 * rows, half), (rows, half)] + [(LIVE, wide)] * lines,
        [
            (0, 0, (1,), rows, half, 0, 0, 0),
            (0, 0, (0,), rows, half, 1, 0, 0),
            (1, 0, (0,), rows, half, 1, rows, 0),
            (1, 0, (1,), rows, half, 2, 0, 0),
        ]
        + [(2, 0, (near_at + p,), LIVE, half, 0, rows + p * LIVE, 0) for p in range(pieces)]
        + [(2, 0, (2 + s,), LIVE, wide, 3 + s, 0, 0) for s in range(lines)],
    )
    near = over_dp(near_given, 2)
    beside = over_dp(kept, 1)
    arrived = [over_dp(x, 2 * s) for s, x in enumerate(given, 2)]

    lanes = jnp.stack([lane ^ s for s in range(n_seq)]).astype(jnp.int32)
    packed = pack_call(
        after(lanes, kept),
        [query[0], out_grad[0]],
        [(2 * tokens, cols)] * n_seq,
        [
            (source, 0, (s,), tokens, cols, s, source * tokens, 0)
            for s in range(n_seq)
            for source in range(2)
        ],
        size=8 * tokens * hid,
    )
    moved = [packed[0]] + [None] * (n_seq - 1)
    previous = ()
    for s in range(2, n_seq):
        moved[s] = over_seq(after(packed[s], *previous), s)
        previous = (moved[s],)
    moved[1] = over_seq(after(packed[1], beside), 1)

    value_near = over_dp(after(value_given, near, *arrived), 2)
    key_near, shared, shared_given = pack_call(
        place,
        [near, *arrived],
        [(rows, half)] + [((lines - 1) * LIVE, wide)] * 2,
        [(0, 0, 0, rows, half, 0, 0, 0)]
        + [
            (0, rows + p * LIVE, 0, LIVE, half, out, 0, p * half)
            for p in range(pieces)
            for out in (1, 2)
        ]
        + [
            (s - 1, 0, 0, LIVE, wide, out, (s - 1) * LIVE, 0)
            for s in range(2, lines)
            for out in (1, 2)
        ],
    )
    key_far = over_dp(key_near, 1)
    value_far = over_dp(value_near, 1)
    sibling = over_seq(shared_given, 1)
    key_quad = ((kept, rows, 0), (beside, rows, 0), (key_near, rows, 0), (key_far, rows, 0))
    value_quad = ((kept, rows, 1), (beside, rows, 1), (value_near, rows, 0), (value_far, rows, 0))

    places = jnp.stack([core ^ low, 1 - (core ^ low), side, 1 - side]).astype(jnp.int32)

    def product(weights, other):
        chosen = [s for s in range(lines) if bool(s & 2) == other]
        return product_call(
            places,
            [(shared, LIVE, s - 1) if s else (mine_first, LIVE, 0) for s in chosen],
            [(sibling, LIVE, s - 1) if s else (sibling_first, LIVE, 0) for s in chosen],
            weights,
        )

    def reduced(total):
        step = 8
        while step < n_dp:
            count = total.shape[0] // 2
            total = total[:count] + over_dp(total[count:], step)
            step *= 2
        return lax.reduce_precision(total, 8, 7).astype(jnp.bfloat16)

    def joined(total):
        own, other = total[:LIVE], over_dp(total[LIVE:], 2)
        return jnp.where(
            low == 0,
            jnp.concatenate([own, other], axis=1),
            jnp.concatenate([other, own], axis=1),
        )

    def seq_sum(x, before=()):
        step = 1
        while step < n_seq:
            x = x + over_seq(x, step)
            if step == 1:
                x = after(x, *before)
            step *= 2
        return x

    own_columns, other_given = pick_call(places, mine_first, shared, sibling_first, sibling, rows)
    other_columns = over_dp(other_given, 1)
    columns = jnp.concatenate([own_columns, other_columns], axis=0).T

    key_sent = over_dp(product(key_quad, True), 4)
    value_product = product(value_quad, True)
    value_sent = over_dp(value_product, 4)
    key_total = reduced(product(key_quad, False) + after(key_sent, value_product))
    raw = joined(key_total)
    raw_wide = raw.astype(jnp.float32)
    squares = seq_sum(jnp.sum(raw_wide * raw_wide, axis=-1, keepdims=True))
    inv_rms = lax.rsqrt(squares / hid + 1e-06)
    gain = lax.dynamic_slice(key_gain, (lane * cols,), (cols,)).reshape(1, cols)
    value_total = reduced(product(value_quad, False) + after(value_sent, inv_rms))
    values = joined(value_total)
    attends, keys, value_grad = attend_call(
        lengths, after(raw, columns, value_total), inv_rms, gain, moved, tokens
    )

    value_near_parts = [over_dp(value_grad, 2 * s) for s in range(1, lines)]
    value_first = over_dp(value_grad, 1)
    outs, scaled, inner = gradient_call(raw, keys, values, gain, moved, attends, tokens)
    inner = after(inner, value_first)
    inner_mean = seq_sum(jnp.sum(inner, axis=-1, keepdims=True), value_near_parts) / hid
    raw_grad = (inv_rms * scaled - raw_wide * inv_rms**3 * inner_mean).astype(jnp.bfloat16)
    value_rest = over_dp(jnp.concatenate(value_near_parts, axis=0), 1)
    key_near_parts = [over_dp(raw_grad, 2 * s) for s in range(1, lines)]
    placed = [outs[0]] + [None] * (n_seq - 1)
    previous = (inner_mean,)
    for s in range(2, n_seq):
        placed[s] = over_seq(after(outs[s], *previous), s)
        previous = (placed[s], value_rest, *key_near_parts)
    placed[1] = over_seq(after(outs[1], value_rest), 1)
    split = lines // 2
    key_first = over_dp(
        after(jnp.concatenate([raw_grad, *key_near_parts[: split - 1]], axis=0), value_rest), 1
    )
    key_rest = over_dp(jnp.concatenate(key_near_parts[split - 1 :], axis=0), 1)
    key_parts = (
        [(x, LIVE, 0) for x in (raw_grad, *key_near_parts)]
        + [(key_first, LIVE, s) for s in range(split)]
        + [(key_rest, LIVE, s) for s in range(split)]
    )
    value_parts = (
        [(x, LIVE, 0) for x in (value_grad, *value_near_parts)]
        + [(value_first, LIVE, 0)]
        + [(value_rest, LIVE, s) for s in range(lines - 1)]
    )
    key_weight_grad, value_weight_grad = weights_call(columns, key_parts + value_parts)

    (query_grad,) = pack_call(
        lanes,
        placed,
        [(tokens, hid)],
        [(s, 0, 0, tokens // 2, cols, 0, 0, (s,)) for s in range(n_seq)],
        2,
    )
    return query_grad[None], key_weight_grad, value_weight_grad


def solution(mesh):
    placed = (
        P("dp", "seq", None),
        P("dp", None, None),
        P("dp", "seq"),
        P("dp", "seq"),
        P(),
        P("dp"),
        P("dp", "seq", None),
    )
    return jax.shard_map(
        functools.partial(shards, mesh.shape["dp"], mesh.shape["seq"]),
        mesh=mesh,
        in_specs=placed,
        out_specs=(P("dp", "seq", None), P("dp", "seq"), P("dp", "seq")),
        check_vma=False,
    )
```

```python
import functools

import jax
import jax.numpy as jnp
from jax import lax
from jax.experimental import pallas as pl
from jax.experimental.pallas import tpu as pltpu
from jax.sharding import PartitionSpec as P

HD = 128
LIVE = 128
VMEM = 60 * 1024 * 1024


ROWS = (((1,), (1,)), ((), ()))
COLUMNS = (((0,), (0,)), ((), ()))
FACTOR = HD ** (-0.5)


def attend_kernel(parts, length_ref, raw_ref, inv_ref, gain_ref, *refs):
    query_refs, grad_refs = refs[:parts], refs[parts : 2 * parts]
    attend_refs = refs[2 * parts : 3 * parts]
    keys_ref, value_grad_ref = refs[3 * parts :]
    raw = raw_ref[...].astype(jnp.float32)
    keys = (raw * inv_ref[...] * gain_ref[...]).astype(jnp.bfloat16)
    keys_ref[...] = keys
    valid = lax.broadcasted_iota(jnp.int32, (LIVE, 1), 0) < length_ref[0]
    value_grad = jnp.zeros((LIVE, HD), jnp.float32)
    for query_ref, grad_ref, attend_ref in zip(query_refs, grad_refs, attend_refs):
        scores = lax.dot_general(keys, query_ref[...], ROWS, preferred_element_type=jnp.float32)
        scores = jnp.where(valid, scores * FACTOR, -jnp.inf)
        powers = jnp.exp(scores - jnp.max(scores, axis=0, keepdims=True))
        attend = powers * (1.0 / jnp.sum(powers, axis=0, keepdims=True))
        attend_ref[0] = attend
        value_grad += jnp.dot(
            attend.astype(jnp.bfloat16), grad_ref[...], preferred_element_type=jnp.float32
        )
    value_grad_ref[...] = value_grad.astype(jnp.bfloat16)


def gradient_kernel(parts, raw_ref, keys_ref, value_ref, gain_ref, *refs):
    query_refs, grad_refs = refs[:parts], refs[parts : 2 * parts]
    attend_refs, out_refs = refs[2 * parts : 3 * parts], refs[3 * parts : 4 * parts]
    scaled_ref, inner_ref = refs[4 * parts :]
    keys, values = keys_ref[...], value_ref[...]
    key_grad = jnp.zeros((LIVE, HD), jnp.float32)
    for query_ref, grad_ref, attend_ref, out_ref in zip(
        query_refs, grad_refs, attend_refs, out_refs
    ):
        attend = attend_ref[0]
        dattend = lax.dot_general(values, grad_ref[...], ROWS, preferred_element_type=jnp.float32)
        delta = jnp.sum(attend * dattend, axis=0, keepdims=True)
        dscores = (attend * (dattend - delta)).astype(jnp.bfloat16)
        out = lax.dot_general(dscores, keys, COLUMNS, preferred_element_type=jnp.float32)
        out_ref[...] = (out * FACTOR).astype(jnp.bfloat16)
        key_grad += jnp.dot(dscores, query_ref[...], preferred_element_type=jnp.float32)
    scaled = key_grad * FACTOR * gain_ref[...]
    scaled_ref[...] = scaled

    @pl.when(pl.program_id(0) == 0)
    def _():
        inner_ref[...] = jnp.zeros_like(inner_ref)

    inner_ref[...] += scaled * raw_ref[...].astype(jnp.float32)


def specs(tokens):
    head = pl.BlockSpec((LIVE, HD), lambda h: (0, h))
    block = pl.BlockSpec((tokens, HD), lambda h: (0, h))
    lower = pl.BlockSpec((tokens, HD), lambda h: (1, h))
    weights = pl.BlockSpec((1, LIVE, tokens), lambda h: (h, 0, 0))
    gain = pl.BlockSpec((1, HD), lambda h: (0, h))
    return head, block, lower, weights, gain


def attend_call(length, raw, inv, gain, moved, tokens):
    parts = len(moved)
    cols = moved[0].shape[1]
    heads = cols // HD
    head, block, lower, weights, gains = specs(tokens)
    outs = pl.pallas_call(
        functools.partial(attend_kernel, parts),
        grid=(heads,),
        in_specs=[
            pl.BlockSpec(memory_space=pltpu.SMEM),
            head,
            pl.BlockSpec((LIVE, 1), lambda h: (0, 0)),
            gains,
        ]
        + [block] * parts
        + [lower] * parts,
        out_specs=[weights] * parts + [head, head],
        out_shape=[jax.ShapeDtypeStruct((heads, LIVE, tokens), jnp.float32)] * parts
        + [jax.ShapeDtypeStruct((LIVE, cols), jnp.bfloat16)] * 2,
        compiler_params=pltpu.CompilerParams(vmem_limit_bytes=VMEM),
        cost_estimate=pl.CostEstimate(
            flops=16 * parts * tokens * cols * LIVE,
            bytes_accessed=16 * parts * tokens * cols,
            transcendentals=0,
        ),
    )(length, raw, inv, gain, *moved, *moved)
    return outs[:parts], outs[parts], outs[parts + 1]


def gradient_call(raw, keys, values, gain, moved, attends, tokens):
    parts = len(moved)
    cols = moved[0].shape[1]
    heads = cols // HD
    head, block, lower, weights, gains = specs(tokens)
    outs = pl.pallas_call(
        functools.partial(gradient_kernel, parts),
        grid=(heads,),
        in_specs=[head, head, head, gains] + [block] * parts + [lower] * parts + [weights] * parts,
        out_specs=[block] * parts + [head, pl.BlockSpec((LIVE, HD), lambda h: (0, 0))],
        out_shape=[jax.ShapeDtypeStruct((tokens, cols), jnp.bfloat16)] * parts
        + [
            jax.ShapeDtypeStruct((LIVE, cols), jnp.float32),
            jax.ShapeDtypeStruct((LIVE, HD), jnp.float32),
        ],
        compiler_params=pltpu.CompilerParams(vmem_limit_bytes=VMEM),
        cost_estimate=pl.CostEstimate(
            flops=24 * parts * tokens * cols * LIVE,
            bytes_accessed=16 * parts * tokens * cols,
            transcendentals=0,
        ),
    )(raw, keys, values, gain, *moved, *moved, *attends)
    return outs[:parts], outs[parts], outs[parts + 1]


def rows_spec(part, width, tiled=False):
    _, count, index = part
    if tiled:
        return pl.BlockSpec((count, width), lambda n: (index, n))
    return pl.BlockSpec((count, width), lambda n: (index, 0))


def pick_kernel(place_ref, first_ref, mine_ref, sibling_first_ref, sibling_ref, *out_refs):
    here = place_ref[0] == 0
    rows = out_refs[0].shape[1]
    for index, out_ref in enumerate(out_refs):
        at = pl.ds(pl.multiple_of(place_ref[2 + index] * rows, rows), rows)
        out_ref[:LIVE] = jnp.where(here, first_ref[:, at], sibling_first_ref[:, at])
        out_ref[LIVE:] = jnp.where(here, mine_ref[:, at], sibling_ref[:, at])


def pick_call(place, first, mine, sibling_first, sibling, rows):
    arrays = (first, mine, sibling_first, sibling)
    shape = (LIVE + mine.shape[0], rows)
    return pl.pallas_call(
        pick_kernel,
        grid=(1,),
        in_specs=[pl.BlockSpec(memory_space=pltpu.SMEM)]
        + [pl.BlockSpec(x.shape, lambda n: (0, 0)) for x in arrays],
        out_specs=[pl.BlockSpec(shape, lambda n: (0, 0))] * 2,
        out_shape=[jax.ShapeDtypeStruct(shape, jnp.bfloat16)] * 2,
        compiler_params=pltpu.CompilerParams(vmem_limit_bytes=VMEM),
        cost_estimate=pl.CostEstimate(flops=1000, bytes_accessed=1000, transcendentals=0),
    )(place, *arrays)


def product_kernel(videos, place_ref, *refs):
    mine_refs, sibling_refs = refs[:videos], refs[videos : 2 * videos]
    weight_refs, out_ref = refs[2 * videos : -1], refs[-1]
    rows = weight_refs[0].shape[0]
    total = None
    for step, weight_ref in enumerate(weight_refs):
        here = place_ref[step // 2] == 0
        at = pl.ds(pl.multiple_of(place_ref[2 + step % 2] * rows, rows), rows)
        block = jnp.concatenate(
            [jnp.where(here, m[:, at], s[:, at]) for m, s in zip(mine_refs, sibling_refs)], axis=0
        )
        term = jnp.dot(block, weight_ref[...], preferred_element_type=jnp.float32)
        total = term if total is None else total + term
    out_ref[...] = total


def product_call(place, mine, sibling, weights):
    videos = len(mine)
    width = weights[0][0].shape[1]
    parts = [*mine, *sibling, *weights]
    return pl.pallas_call(
        functools.partial(product_kernel, videos),
        grid=(1,),
        in_specs=[pl.BlockSpec(memory_space=pltpu.SMEM)]
        + [rows_spec(part, part[0].shape[1]) for part in parts],
        out_specs=pl.BlockSpec((videos * LIVE, width), lambda n: (0, 0)),
        out_shape=jax.ShapeDtypeStruct((videos * LIVE, width), jnp.float32),
        compiler_params=pltpu.CompilerParams(vmem_limit_bytes=VMEM),
        cost_estimate=pl.CostEstimate(flops=1000, bytes_accessed=1000, transcendentals=0),
    )(place, *[part[0] for part in parts])


def weights_kernel(videos, columns_ref, *refs):
    part_refs, out_refs = refs[:-2], refs[-2:]
    for index, out_ref in enumerate(out_refs):
        parts = [ref[...] for ref in part_refs[index * videos : (index + 1) * videos]]
        out_ref[...] = jnp.dot(
            columns_ref[...], jnp.concatenate(parts, axis=0), preferred_element_type=jnp.float32
        )


def weights_call(columns, parts):
    rows, videos = columns.shape[0], len(parts) // 2
    cols = parts[0][0].shape[1]
    tile = min(cols, 512)
    return pl.pallas_call(
        functools.partial(weights_kernel, videos),
        grid=(cols // tile,),
        in_specs=[pl.BlockSpec(columns.shape, lambda n: (0, 0))]
        + [rows_spec(part, tile, True) for part in parts],
        out_specs=[pl.BlockSpec((rows, tile), lambda n: (0, n))] * 2,
        out_shape=[jax.ShapeDtypeStruct((rows, cols), jnp.float32)] * 2,
        compiler_params=pltpu.CompilerParams(vmem_limit_bytes=VMEM),
        cost_estimate=pl.CostEstimate(
            flops=4 * rows * cols * videos * LIVE,
            bytes_accessed=8 * rows * cols + 4 * videos * LIVE * cols,
            transcendentals=0,
        ),
    )(columns, *[part[0] for part in parts])


def after(x, *others):
    return lax.optimization_barrier((x, *others))[0]


def pack_kernel(moves, inputs, place_ref, *refs):
    ins, outs = refs[:inputs], refs[inputs:]

    def span(at, width):
        if isinstance(at, int):
            return pl.ds(at, width)
        return pl.ds(pl.multiple_of(place_ref[at[0]] * width, width), width)

    for source, row, col, count, width, target, to_row, to_col in moves:
        block = ins[source][pl.ds(row, count), span(col, width)]
        outs[target][pl.ds(to_row, count), span(to_col, width)] = block


def pack_call(place, arrays, shapes, moves, tiles=1, size=1000):
    def spec(shape):
        return pl.BlockSpec((shape[0] // tiles, shape[1]), lambda n: (n, 0))

    return pl.pallas_call(
        functools.partial(pack_kernel, moves, len(arrays)),
        grid=(tiles,),
        in_specs=[pl.BlockSpec(memory_space=pltpu.SMEM)] + [spec(x.shape) for x in arrays],
        out_specs=[spec(shape) for shape in shapes],
        out_shape=[jax.ShapeDtypeStruct(shape, jnp.bfloat16) for shape in shapes],
        compiler_params=pltpu.CompilerParams(vmem_limit_bytes=VMEM),
        cost_estimate=pl.CostEstimate(flops=1000, bytes_accessed=size, transcendentals=0),
    )(place, *arrays)


def shards(n_dp, n_seq, query, caption, key_weight, value_weight, key_gain, lengths, out_grad):
    rows, cols = key_weight.shape
    hid = cols * n_seq
    lines = n_dp // 2
    half = cols // 2
    wide = 2 * rows
    tokens = query.shape[1]
    me = lax.axis_index("dp")
    lane = lax.axis_index("seq")
    quad, low, side = me // 4, me // 2 % 2, me % 2
    core = lane % 2

    def over_dp(x, step):
        return lax.ppermute(x, "dp", [(a, a ^ step) for a in range(n_dp)])

    def over_seq(x, step):
        return lax.ppermute(x, "seq", [(a, a ^ step) for a in range(n_seq)])

    def col_block(x, index, width):
        return lax.dynamic_slice(x, (0, index * width), (x.shape[0], width))

    pieces = wide // half
    quads = lines // 2
    scalars = [low, 1 - low, quad * 2 + core, quad * 2 + 1 - core]
    scalars += [(quad ^ (s // 2)) * 2 + core for s in range(2, lines)]
    scalars += [(quad * 2 + core) * pieces + p for p in range(pieces)]
    place = jnp.stack(scalars).astype(jnp.int32)
    near_at = lines + 2
    near_given, kept, value_given, mine_first, sibling_first, *given = pack_call(
        place,
        [key_weight, value_weight, caption[0]],
        [(rows + pieces * LIVE, half), (2 * rows, half), (rows, half)] + [(LIVE, wide)] * lines,
        [
            (0, 0, (1,), rows, half, 0, 0, 0),
            (0, 0, (0,), rows, half, 1, 0, 0),
            (1, 0, (0,), rows, half, 1, rows, 0),
            (1, 0, (1,), rows, half, 2, 0, 0),
        ]
        + [(2, 0, (near_at + p,), LIVE, half, 0, rows + p * LIVE, 0) for p in range(pieces)]
        + [(2, 0, (2 + s,), LIVE, wide, 3 + s, 0, 0) for s in range(lines)],
    )
    near = over_dp(near_given, 2)
    beside = over_dp(kept, 1)
    arrived = [over_dp(x, 2 * s) for s, x in enumerate(given, 2)]

    lanes = jnp.stack([lane ^ s for s in range(n_seq)]).astype(jnp.int32)
    packed = pack_call(
        after(lanes, kept),
        [query[0], out_grad[0]],
        [(2 * tokens, cols)] * n_seq,
        [
            (source, 0, (s,), tokens, cols, s, source * tokens, 0)
            for s in range(n_seq)
            for source in range(2)
        ],
        size=8 * tokens * hid,
    )
    moved = [packed[0]] + [None] * (n_seq - 1)
    previous = ()
    for s in range(2, n_seq):
        moved[s] = over_seq(after(packed[s], *previous), s)
        previous = (moved[s],)
    moved[1] = over_seq(after(packed[1], beside), 1)

    value_near = over_dp(after(value_given, near, *arrived), 2)
    key_near, shared, shared_given = pack_call(
        place,
        [near, *arrived],
        [(rows, half)] + [((lines - 1) * LIVE, wide)] * 2,
        [(0, 0, 0, rows, half, 0, 0, 0)]
        + [
            (0, rows + p * LIVE, 0, LIVE, half, out, 0, p * half)
            for p in range(pieces)
            for out in (1, 2)
        ]
        + [
            (s - 1, 0, 0, LIVE, wide, out, (s - 1) * LIVE, 0)
            for s in range(2, lines)
            for out in (1, 2)
        ],
    )
    key_far = over_dp(key_near, 1)
    value_far = over_dp(value_near, 1)
    sibling = over_seq(shared_given, 1)
    key_quad = ((kept, rows, 0), (beside, rows, 0), (key_near, rows, 0), (key_far, rows, 0))
    value_quad = ((kept, rows, 1), (beside, rows, 1), (value_near, rows, 0), (value_far, rows, 0))

    places = jnp.stack([core ^ low, 1 - (core ^ low), side, 1 - side]).astype(jnp.int32)

    def product(weights, other):
        chosen = [s for s in range(lines) if bool(s & 2) == other]
        return product_call(
            places,
            [(shared, LIVE, s - 1) if s else (mine_first, LIVE, 0) for s in chosen],
            [(sibling, LIVE, s - 1) if s else (sibling_first, LIVE, 0) for s in chosen],
            weights,
        )

    def reduced(total):
        step = 8
        while step < n_dp:
            count = total.shape[0] // 2
            total = total[:count] + over_dp(total[count:], step)
            step *= 2
        return lax.reduce_precision(total, 8, 7).astype(jnp.bfloat16)

    def joined(total):
        own, other = total[:LIVE], over_dp(total[LIVE:], 2)
        return jnp.where(
            low == 0,
            jnp.concatenate([own, other], axis=1),
            jnp.concatenate([other, own], axis=1),
        )

    def seq_sum(x):
        step = 1
        while step < n_seq:
            x = x + over_seq(x, step)
            step *= 2
        return x

    own_columns, other_given = pick_call(places, mine_first, shared, sibling_first, sibling, rows)
    other_columns = over_dp(other_given, 1)
    columns = jnp.concatenate([own_columns, other_columns], axis=0).T

    key_sent = over_dp(product(key_quad, True), 4)
    value_product, value_rest_product = product(value_quad, True), product(value_quad, False)
    key_sent = after(key_sent, value_product, value_rest_product, other_columns)
    value_sent = over_dp(after(value_product, key_sent), 4)
    key_total = reduced(product(key_quad, False) + key_sent)
    raw = joined(key_total)
    raw_wide = raw.astype(jnp.float32)
    squares = seq_sum(jnp.sum(raw_wide * raw_wide, axis=-1, keepdims=True))
    inv_rms = lax.rsqrt(squares / hid + 1e-06)
    gain = lax.dynamic_slice(key_gain, (lane * cols,), (cols,)).reshape(1, cols)
    value_total = reduced(value_rest_product + after(value_sent, inv_rms))
    values = joined(value_total)
    attends, keys, value_grad = attend_call(
        lengths, after(raw, columns, value_total), inv_rms, gain, moved, tokens
    )

    value_near_parts = [over_dp(value_grad, 2 * s) for s in range(1, lines)]
    value_first = over_dp(value_grad, 1)
    outs, scaled, inner = gradient_call(raw, keys, values, gain, moved, attends, tokens)
    inner = after(inner, value_first)
    inner_mean = seq_sum(jnp.sum(inner, axis=-1, keepdims=True)) / hid
    raw_grad = (inv_rms * scaled - raw_wide * inv_rms**3 * inner_mean).astype(jnp.bfloat16)
    value_rest = over_dp(jnp.concatenate(value_near_parts, axis=0), 1)
    raw_grad = after(raw_grad, *value_near_parts)
    key_near_parts = [over_dp(raw_grad, 2 * s) for s in range(1, lines)]
    placed = [outs[0]] + [None] * (n_seq - 1)
    previous = (inner_mean,)
    for s in range(2, n_seq):
        placed[s] = over_seq(after(outs[s], *previous), s)
        previous = (placed[s], value_rest, *key_near_parts)
    placed[1] = over_seq(after(outs[1], value_rest), 1)
    split = lines // 2
    key_early = jnp.concatenate([raw_grad, *key_near_parts[: split - 1]], axis=0)
    key_first = over_dp(key_early, 1)
    key_late = [after(x, key_first) for x in key_near_parts[split - 1 :]]
    key_rest = over_dp(jnp.concatenate(key_late, axis=0), 1)
    key_parts = (
        [(x, LIVE, 0) for x in (raw_grad, *key_near_parts)]
        + [(key_first, LIVE, s) for s in range(split)]
        + [(key_rest, LIVE, s) for s in range(split)]
    )
    value_parts = (
        [(x, LIVE, 0) for x in (value_grad, *value_near_parts)]
        + [(value_first, LIVE, 0)]
        + [(value_rest, LIVE, s) for s in range(lines - 1)]
    )
    key_weight_grad, value_weight_grad = weights_call(columns, key_parts + value_parts)

    (query_grad,) = pack_call(
        lanes,
        placed,
        [(tokens, hid)],
        [(s, 0, 0, tokens // 2, cols, 0, 0, (s,)) for s in range(n_seq)],
        2,
    )
    return query_grad[None], key_weight_grad, value_weight_grad


def solution(mesh):
    placed = (
        P("dp", "seq", None),
        P("dp", None, None),
        P("dp", "seq"),
        P("dp", "seq"),
        P(),
        P("dp"),
        P("dp", "seq", None),
    )
    return jax.shard_map(
        functools.partial(shards, mesh.shape["dp"], mesh.shape["seq"]),
        mesh=mesh,
        in_specs=placed,
        out_specs=(P("dp", "seq", None), P("dp", "seq"), P("dp", "seq")),
        check_vma=False,
    )
```

```python
import functools

import jax
import jax.numpy as jnp
from jax import lax
from jax.experimental import pallas as pl
from jax.experimental.pallas import tpu as pltpu
from jax.sharding import PartitionSpec as P

HD = 128
LIVE = 128
VMEM = 60 * 1024 * 1024


ROWS = (((1,), (1,)), ((), ()))
COLUMNS = (((0,), (0,)), ((), ()))
FACTOR = HD ** (-0.5)


def attend_kernel(parts, length_ref, raw_ref, inv_ref, gain_ref, *refs):
    query_refs, grad_refs = refs[:parts], refs[parts : 2 * parts]
    attend_refs = refs[2 * parts : 3 * parts]
    keys_ref, value_grad_ref = refs[3 * parts :]
    raw = raw_ref[...].astype(jnp.float32)
    keys = (raw * inv_ref[...] * gain_ref[...]).astype(jnp.bfloat16)
    keys_ref[...] = keys
    valid = lax.broadcasted_iota(jnp.int32, (LIVE, 1), 0) < length_ref[0]
    value_grad = jnp.zeros((LIVE, HD), jnp.float32)
    for query_ref, grad_ref, attend_ref in zip(query_refs, grad_refs, attend_refs):
        scores = lax.dot_general(keys, query_ref[...], ROWS, preferred_element_type=jnp.float32)
        scores = jnp.where(valid, scores * FACTOR, -jnp.inf)
        powers = jnp.exp(scores - jnp.max(scores, axis=0, keepdims=True))
        attend = powers * (1.0 / jnp.sum(powers, axis=0, keepdims=True))
        attend_ref[0] = attend
        value_grad += jnp.dot(
            attend.astype(jnp.bfloat16), grad_ref[...], preferred_element_type=jnp.float32
        )
    value_grad_ref[...] = value_grad.astype(jnp.bfloat16)


def gradient_kernel(parts, raw_ref, keys_ref, value_ref, gain_ref, *refs):
    query_refs, grad_refs = refs[:parts], refs[parts : 2 * parts]
    attend_refs, out_refs = refs[2 * parts : 3 * parts], refs[3 * parts : 4 * parts]
    scaled_ref, inner_ref = refs[4 * parts :]
    keys, values = keys_ref[...], value_ref[...]
    key_grad = jnp.zeros((LIVE, HD), jnp.float32)
    for query_ref, grad_ref, attend_ref, out_ref in zip(
        query_refs, grad_refs, attend_refs, out_refs
    ):
        attend = attend_ref[0]
        dattend = lax.dot_general(values, grad_ref[...], ROWS, preferred_element_type=jnp.float32)
        delta = jnp.sum(attend * dattend, axis=0, keepdims=True)
        dscores = (attend * (dattend - delta)).astype(jnp.bfloat16)
        out = lax.dot_general(dscores, keys, COLUMNS, preferred_element_type=jnp.float32)
        out_ref[...] = (out * FACTOR).astype(jnp.bfloat16)
        key_grad += jnp.dot(dscores, query_ref[...], preferred_element_type=jnp.float32)
    scaled = key_grad * FACTOR * gain_ref[...]
    scaled_ref[...] = scaled

    @pl.when(pl.program_id(0) == 0)
    def _():
        inner_ref[...] = jnp.zeros_like(inner_ref)

    inner_ref[...] += scaled * raw_ref[...].astype(jnp.float32)


def specs(tokens):
    head = pl.BlockSpec((LIVE, HD), lambda h: (0, h))
    block = pl.BlockSpec((tokens, HD), lambda h: (0, h))
    lower = pl.BlockSpec((tokens, HD), lambda h: (1, h))
    weights = pl.BlockSpec((1, LIVE, tokens), lambda h: (h, 0, 0))
    gain = pl.BlockSpec((1, HD), lambda h: (0, h))
    return head, block, lower, weights, gain


def attend_call(length, raw, inv, gain, moved, tokens):
    parts = len(moved)
    cols = moved[0].shape[1]
    heads = cols // HD
    head, block, lower, weights, gains = specs(tokens)
    outs = pl.pallas_call(
        functools.partial(attend_kernel, parts),
        grid=(heads,),
        in_specs=[
            pl.BlockSpec(memory_space=pltpu.SMEM),
            head,
            pl.BlockSpec((LIVE, 1), lambda h: (0, 0)),
            gains,
        ]
        + [block] * parts
        + [lower] * parts,
        out_specs=[weights] * parts + [head, head],
        out_shape=[jax.ShapeDtypeStruct((heads, LIVE, tokens), jnp.float32)] * parts
        + [jax.ShapeDtypeStruct((LIVE, cols), jnp.bfloat16)] * 2,
        compiler_params=pltpu.CompilerParams(vmem_limit_bytes=VMEM),
        cost_estimate=pl.CostEstimate(
            flops=16 * parts * tokens * cols * LIVE,
            bytes_accessed=16 * parts * tokens * cols,
            transcendentals=0,
        ),
    )(length, raw, inv, gain, *moved, *moved)
    return outs[:parts], outs[parts], outs[parts + 1]


def gradient_call(raw, keys, values, gain, moved, attends, tokens):
    parts = len(moved)
    cols = moved[0].shape[1]
    heads = cols // HD
    head, block, lower, weights, gains = specs(tokens)
    outs = pl.pallas_call(
        functools.partial(gradient_kernel, parts),
        grid=(heads,),
        in_specs=[head, head, head, gains] + [block] * parts + [lower] * parts + [weights] * parts,
        out_specs=[block] * parts + [head, pl.BlockSpec((LIVE, HD), lambda h: (0, 0))],
        out_shape=[jax.ShapeDtypeStruct((tokens, cols), jnp.bfloat16)] * parts
        + [
            jax.ShapeDtypeStruct((LIVE, cols), jnp.float32),
            jax.ShapeDtypeStruct((LIVE, HD), jnp.float32),
        ],
        compiler_params=pltpu.CompilerParams(vmem_limit_bytes=VMEM),
        cost_estimate=pl.CostEstimate(
            flops=24 * parts * tokens * cols * LIVE,
            bytes_accessed=16 * parts * tokens * cols,
            transcendentals=0,
        ),
    )(raw, keys, values, gain, *moved, *moved, *attends)
    return outs[:parts], outs[parts], outs[parts + 1]


def rows_spec(part, width, tiled=False):
    _, count, index = part
    if tiled:
        return pl.BlockSpec((count, width), lambda n: (index, n))
    return pl.BlockSpec((count, width), lambda n: (index, 0))


def pick_kernel(place_ref, first_ref, mine_ref, sibling_first_ref, sibling_ref, *out_refs):
    here = place_ref[0] == 0
    rows = out_refs[0].shape[1]
    for index, out_ref in enumerate(out_refs):
        at = pl.ds(pl.multiple_of(place_ref[2 + index] * rows, rows), rows)
        out_ref[:LIVE] = jnp.where(here, first_ref[:, at], sibling_first_ref[:, at])
        out_ref[LIVE:] = jnp.where(here, mine_ref[:, at], sibling_ref[:, at])


def pick_call(place, first, mine, sibling_first, sibling, rows):
    arrays = (first, mine, sibling_first, sibling)
    shape = (LIVE + mine.shape[0], rows)
    return pl.pallas_call(
        pick_kernel,
        grid=(1,),
        in_specs=[pl.BlockSpec(memory_space=pltpu.SMEM)]
        + [pl.BlockSpec(x.shape, lambda n: (0, 0)) for x in arrays],
        out_specs=[pl.BlockSpec(shape, lambda n: (0, 0))] * 2,
        out_shape=[jax.ShapeDtypeStruct(shape, jnp.bfloat16)] * 2,
        compiler_params=pltpu.CompilerParams(vmem_limit_bytes=VMEM),
        cost_estimate=pl.CostEstimate(flops=1000, bytes_accessed=1000, transcendentals=0),
    )(place, *arrays)


def product_kernel(videos, place_ref, *refs):
    mine_refs, sibling_refs = refs[:videos], refs[videos : 2 * videos]
    weight_refs, out_ref = refs[2 * videos : -1], refs[-1]
    rows = weight_refs[0].shape[0]
    total = None
    for step, weight_ref in enumerate(weight_refs):
        here = place_ref[step // 2] == 0
        at = pl.ds(pl.multiple_of(place_ref[2 + step % 2] * rows, rows), rows)
        block = jnp.concatenate(
            [jnp.where(here, m[:, at], s[:, at]) for m, s in zip(mine_refs, sibling_refs)], axis=0
        )
        term = jnp.dot(block, weight_ref[...], preferred_element_type=jnp.float32)
        total = term if total is None else total + term
    out_ref[...] = total


def product_call(place, mine, sibling, weights):
    videos = len(mine)
    width = weights[0][0].shape[1]
    parts = [*mine, *sibling, *weights]
    return pl.pallas_call(
        functools.partial(product_kernel, videos),
        grid=(1,),
        in_specs=[pl.BlockSpec(memory_space=pltpu.SMEM)]
        + [rows_spec(part, part[0].shape[1]) for part in parts],
        out_specs=pl.BlockSpec((videos * LIVE, width), lambda n: (0, 0)),
        out_shape=jax.ShapeDtypeStruct((videos * LIVE, width), jnp.float32),
        compiler_params=pltpu.CompilerParams(vmem_limit_bytes=VMEM),
        cost_estimate=pl.CostEstimate(flops=1000, bytes_accessed=1000, transcendentals=0),
    )(place, *[part[0] for part in parts])


def weights_kernel(columns_ref, *refs):
    parts = [ref[...] for ref in refs[:-1]]
    refs[-1][...] = jnp.dot(
        columns_ref[...], jnp.concatenate(parts, axis=0), preferred_element_type=jnp.float32
    )


def weights_call(columns, parts):
    rows, depth = columns.shape
    cols = parts[0][0].shape[1]
    tile = min(cols, 256)
    return pl.pallas_call(
        weights_kernel,
        grid=(cols // tile,),
        in_specs=[pl.BlockSpec(columns.shape, lambda n: (0, 0))]
        + [rows_spec(part, tile, True) for part in parts],
        out_specs=pl.BlockSpec((rows, tile), lambda n: (0, n)),
        out_shape=jax.ShapeDtypeStruct((rows, cols), jnp.float32),
        compiler_params=pltpu.CompilerParams(vmem_limit_bytes=VMEM),
        cost_estimate=pl.CostEstimate(
            flops=2 * rows * cols * depth,
            bytes_accessed=4 * rows * cols + 2 * depth * (rows + cols),
            transcendentals=0,
        ),
    )(columns, *[part[0] for part in parts])


def after(x, *others):
    return lax.optimization_barrier((x, *others))[0]


def pack_kernel(moves, inputs, place_ref, *refs):
    ins, outs = refs[:inputs], refs[inputs:]

    def span(at, width):
        if isinstance(at, int):
            return pl.ds(at, width)
        return pl.ds(pl.multiple_of(place_ref[at[0]] * width, width), width)

    for source, row, col, count, width, target, to_row, to_col in moves:
        block = ins[source][pl.ds(row, count), span(col, width)]
        outs[target][pl.ds(to_row, count), span(to_col, width)] = block


def pack_call(place, arrays, shapes, moves, tiles=1, size=1000):
    def spec(shape):
        return pl.BlockSpec((shape[0] // tiles, shape[1]), lambda n: (n, 0))

    return pl.pallas_call(
        functools.partial(pack_kernel, moves, len(arrays)),
        grid=(tiles,),
        in_specs=[pl.BlockSpec(memory_space=pltpu.SMEM)] + [spec(x.shape) for x in arrays],
        out_specs=[spec(shape) for shape in shapes],
        out_shape=[jax.ShapeDtypeStruct(shape, jnp.bfloat16) for shape in shapes],
        compiler_params=pltpu.CompilerParams(vmem_limit_bytes=VMEM),
        cost_estimate=pl.CostEstimate(flops=1000, bytes_accessed=size, transcendentals=0),
    )(place, *arrays)


def shards(n_dp, n_seq, query, caption, key_weight, value_weight, key_gain, lengths, out_grad):
    rows, cols = key_weight.shape
    hid = cols * n_seq
    lines = n_dp // 2
    half = cols // 2
    wide = 2 * rows
    tokens = query.shape[1]
    me = lax.axis_index("dp")
    lane = lax.axis_index("seq")
    quad, low, side = me // 4, me // 2 % 2, me % 2
    core = lane % 2

    def over_dp(x, step):
        return lax.ppermute(x, "dp", [(a, a ^ step) for a in range(n_dp)])

    def over_seq(x, step):
        return lax.ppermute(x, "seq", [(a, a ^ step) for a in range(n_seq)])

    def col_block(x, index, width):
        return lax.dynamic_slice(x, (0, index * width), (x.shape[0], width))

    pieces = wide // half
    quads = lines // 2
    scalars = [low, 1 - low, quad * 2 + core, quad * 2 + 1 - core]
    scalars += [(quad ^ (s // 2)) * 2 + core for s in range(2, lines)]
    scalars += [(quad * 2 + core) * pieces + p for p in range(pieces)]
    place = jnp.stack(scalars).astype(jnp.int32)
    near_at = lines + 2
    near_given, kept, value_given, mine_first, sibling_first, *given = pack_call(
        place,
        [key_weight, value_weight, caption[0]],
        [(rows + pieces * LIVE, half), (2 * rows, half), (rows, half)] + [(LIVE, wide)] * lines,
        [
            (0, 0, (1,), rows, half, 0, 0, 0),
            (0, 0, (0,), rows, half, 1, 0, 0),
            (1, 0, (0,), rows, half, 1, rows, 0),
            (1, 0, (1,), rows, half, 2, 0, 0),
        ]
        + [(2, 0, (near_at + p,), LIVE, half, 0, rows + p * LIVE, 0) for p in range(pieces)]
        + [(2, 0, (2 + s,), LIVE, wide, 3 + s, 0, 0) for s in range(lines)],
    )
    near = over_dp(near_given, 2)
    beside = over_dp(kept, 1)
    arrived = [over_dp(x, 2 * s) for s, x in enumerate(given, 2)]

    lanes = jnp.stack([lane ^ s for s in range(n_seq)]).astype(jnp.int32)
    packed = pack_call(
        after(lanes, kept),
        [query[0], out_grad[0]],
        [(2 * tokens, cols)] * n_seq,
        [
            (source, 0, (s,), tokens, cols, s, source * tokens, 0)
            for s in range(n_seq)
            for source in range(2)
        ],
        size=8 * tokens * hid,
    )
    moved = [packed[0]] + [None] * (n_seq - 1)
    previous = ()
    for s in range(2, n_seq):
        moved[s] = over_seq(after(packed[s], *previous), s)
        previous = (moved[s],)
    moved[1] = over_seq(after(packed[1], beside), 1)

    value_near = over_dp(after(value_given, near, *arrived), 2)
    key_near, shared, shared_given = pack_call(
        place,
        [near, *arrived],
        [(rows, half)] + [((lines - 1) * LIVE, wide)] * 2,
        [(0, 0, 0, rows, half, 0, 0, 0)]
        + [
            (0, rows + p * LIVE, 0, LIVE, half, out, 0, p * half)
            for p in range(pieces)
            for out in (1, 2)
        ]
        + [
            (s - 1, 0, 0, LIVE, wide, out, (s - 1) * LIVE, 0)
            for s in range(2, lines)
            for out in (1, 2)
        ],
    )
    key_far = over_dp(key_near, 1)
    value_far = over_dp(value_near, 1)
    sibling = over_seq(shared_given, 1)
    key_quad = ((kept, rows, 0), (beside, rows, 0), (key_near, rows, 0), (key_far, rows, 0))
    value_quad = ((kept, rows, 1), (beside, rows, 1), (value_near, rows, 0), (value_far, rows, 0))

    places = jnp.stack([core ^ low, 1 - (core ^ low), side, 1 - side]).astype(jnp.int32)

    def product(weights, other):
        chosen = [s for s in range(lines) if bool(s & 2) == other]
        return product_call(
            places,
            [(shared, LIVE, s - 1) if s else (mine_first, LIVE, 0) for s in chosen],
            [(sibling, LIVE, s - 1) if s else (sibling_first, LIVE, 0) for s in chosen],
            weights,
        )

    def reduced(total):
        step = 8
        while step < n_dp:
            count = total.shape[0] // 2
            total = total[:count] + over_dp(total[count:], step)
            step *= 2
        return lax.reduce_precision(total, 8, 7).astype(jnp.bfloat16)

    def joined(total):
        own, other = total[:LIVE], over_dp(total[LIVE:], 2)
        return jnp.where(
            low == 0,
            jnp.concatenate([own, other], axis=1),
            jnp.concatenate([other, own], axis=1),
        )

    def seq_sum(x, before=()):
        step = 1
        while step < n_seq:
            x = x + over_seq(x, step)
            if step == 1:
                x = after(x, *before)
            step *= 2
        return x

    key_product = product(key_quad, True)
    key_sent = over_dp(key_product, 4)
    own_columns, other_given = pick_call(
        after(places, key_product), mine_first, shared, sibling_first, sibling, rows
    )
    other_columns = over_dp(other_given, 1)
    columns = jnp.concatenate([own_columns, other_columns], axis=0).T
    value_product, value_rest_product = product(value_quad, True), product(value_quad, False)
    key_sent = after(key_sent, value_product, value_rest_product, other_columns)
    key_total = reduced(product(key_quad, False) + key_sent)
    raw = joined(key_total)
    value_sent = over_dp(after(value_product, raw), 4)
    raw_wide = raw.astype(jnp.float32)
    squares = seq_sum(jnp.sum(raw_wide * raw_wide, axis=-1, keepdims=True))
    inv_rms = lax.rsqrt(squares / hid + 1e-06)
    gain = lax.dynamic_slice(key_gain, (lane * cols,), (cols,)).reshape(1, cols)
    attends, keys, value_grad = attend_call(
        lengths, after(raw, columns), inv_rms, gain, moved, tokens
    )
    values = joined(reduced(value_rest_product + after(value_sent, value_grad)))

    value_given = after(value_grad, values)
    value_near_parts = [over_dp(value_given, 2 * s) for s in range(1, lines)]
    value_first = over_dp(value_given, 1)
    outs, scaled, inner = gradient_call(raw, keys, values, gain, moved, attends, tokens)
    inner = after(inner, value_first)
    inner_mean = seq_sum(jnp.sum(inner, axis=-1, keepdims=True), value_near_parts) / hid
    raw_grad = (inv_rms * scaled - raw_wide * inv_rms**3 * inner_mean).astype(jnp.bfloat16)
    value_rest = over_dp(jnp.concatenate(value_near_parts, axis=0), 1)
    key_near_parts = [over_dp(raw_grad, 2 * s) for s in range(1, lines)]
    placed = [outs[0]] + [None] * (n_seq - 1)
    previous = (inner_mean,)
    for s in range(2, n_seq):
        placed[s] = over_seq(after(outs[s], *previous), s)
        previous = (placed[s], value_rest, *key_near_parts)
    placed[1] = over_seq(after(outs[1], value_rest), 1)
    key_first = over_dp(raw_grad, 1)
    key_rest = over_dp(jnp.concatenate(key_near_parts, axis=0), 1)
    key_parts = (
        [(x, LIVE, 0) for x in (raw_grad, *key_near_parts)]
        + [(key_first, LIVE, 0)]
        + [(key_rest, LIVE, s) for s in range(lines - 1)]
    )
    value_parts = (
        [(x, LIVE, 0) for x in (value_grad, *value_near_parts)]
        + [(value_first, LIVE, 0)]
        + [(value_rest, LIVE, s) for s in range(lines - 1)]
    )
    value_weight_grad = weights_call(after(columns, key_first), value_parts)
    key_weight_grad = weights_call(columns, key_parts)

    (query_grad,) = pack_call(
        lanes,
        placed,
        [(tokens, hid)],
        [(s, 0, 0, tokens // 2, cols, 0, 0, (s,)) for s in range(n_seq)],
        2,
    )
    return query_grad[None], key_weight_grad, value_weight_grad


def solution(mesh):
    placed = (
        P("dp", "seq", None),
        P("dp", None, None),
        P("dp", "seq"),
        P("dp", "seq"),
        P(),
        P("dp"),
        P("dp", "seq", None),
    )
    return jax.shard_map(
        functools.partial(shards, mesh.shape["dp"], mesh.shape["seq"]),
        mesh=mesh,
        in_specs=placed,
        out_specs=(P("dp", "seq", None), P("dp", "seq"), P("dp", "seq")),
        check_vma=False,
    )
```

```python
import functools

import jax
import jax.numpy as jnp
from jax import lax
from jax.experimental import pallas as pl
from jax.experimental.pallas import tpu as pltpu
from jax.sharding import PartitionSpec as P

HD = 128
LIVE = 128
VMEM = 60 * 1024 * 1024


ROWS = (((1,), (1,)), ((), ()))
COLUMNS = (((0,), (0,)), ((), ()))
FACTOR = HD ** (-0.5)


def attend_kernel(parts, length_ref, raw_ref, inv_ref, gain_ref, *refs):
    query_refs, grad_refs = refs[:parts], refs[parts : 2 * parts]
    attend_refs = refs[2 * parts : 3 * parts]
    keys_ref, value_grad_ref = refs[3 * parts :]
    raw = raw_ref[...].astype(jnp.float32)
    keys = (raw * inv_ref[...] * gain_ref[...]).astype(jnp.bfloat16)
    keys_ref[...] = keys
    valid = lax.broadcasted_iota(jnp.int32, (LIVE, 1), 0) < length_ref[0]
    value_grad = jnp.zeros((LIVE, HD), jnp.float32)
    for query_ref, grad_ref, attend_ref in zip(query_refs, grad_refs, attend_refs):
        scores = lax.dot_general(keys, query_ref[...], ROWS, preferred_element_type=jnp.float32)
        scores = jnp.where(valid, scores * FACTOR, -jnp.inf)
        powers = jnp.exp(scores - jnp.max(scores, axis=0, keepdims=True))
        attend = powers * (1.0 / jnp.sum(powers, axis=0, keepdims=True))
        attend_ref[0] = attend
        value_grad += jnp.dot(
            attend.astype(jnp.bfloat16), grad_ref[...], preferred_element_type=jnp.float32
        )
    value_grad_ref[...] = value_grad.astype(jnp.bfloat16)


def gradient_kernel(parts, raw_ref, value_ref, gain_ref, *refs):
    query_refs, grad_refs = refs[:parts], refs[parts : 2 * parts]
    attend_refs, score_refs = refs[2 * parts : 3 * parts], refs[3 * parts : 4 * parts]
    scaled_ref, inner_ref = refs[4 * parts :]
    values = value_ref[...]
    key_grad = jnp.zeros((LIVE, HD), jnp.float32)
    for query_ref, grad_ref, attend_ref, score_ref in zip(
        query_refs, grad_refs, attend_refs, score_refs
    ):
        attend = attend_ref[0]
        dattend = lax.dot_general(values, grad_ref[...], ROWS, preferred_element_type=jnp.float32)
        delta = jnp.sum(attend * dattend, axis=0, keepdims=True)
        dscores = (attend * (dattend - delta)).astype(jnp.bfloat16)
        score_ref[0] = dscores
        key_grad += jnp.dot(dscores, query_ref[...], preferred_element_type=jnp.float32)
    scaled = key_grad * FACTOR * gain_ref[...]
    scaled_ref[...] = scaled

    @pl.when(pl.program_id(0) == 0)
    def _():
        inner_ref[...] = jnp.zeros_like(inner_ref)

    inner_ref[...] += scaled * raw_ref[...].astype(jnp.float32)


def query_kernel(parts, keys_ref, *refs):
    for score_ref, out_ref in zip(refs[:parts], refs[parts:]):
        out = lax.dot_general(
            score_ref[0], keys_ref[...], COLUMNS, preferred_element_type=jnp.float32
        )
        out_ref[...] = (out * FACTOR).astype(jnp.bfloat16)


def specs(tokens):
    head = pl.BlockSpec((LIVE, HD), lambda h: (0, h))
    block = pl.BlockSpec((tokens, HD), lambda h: (0, h))
    upper = pl.BlockSpec((None, tokens, HD), lambda h: (0, 0, h))
    lower = pl.BlockSpec((None, tokens, HD), lambda h: (1, 0, h))
    weights = pl.BlockSpec((1, LIVE, tokens), lambda h: (h, 0, 0))
    gain = pl.BlockSpec((1, HD), lambda h: (0, h))
    return head, block, upper, lower, weights, gain


def attend_call(length, raw, inv, gain, moved, tokens):
    parts = len(moved)
    cols = moved[0].shape[2]
    heads = cols // HD
    head, block, upper, lower, weights, gains = specs(tokens)
    outs = pl.pallas_call(
        functools.partial(attend_kernel, parts),
        grid=(heads,),
        in_specs=[
            pl.BlockSpec(memory_space=pltpu.SMEM),
            head,
            pl.BlockSpec((LIVE, 1), lambda h: (0, 0)),
            gains,
        ]
        + [upper] * parts
        + [lower] * parts,
        out_specs=[weights] * parts + [head, head],
        out_shape=[jax.ShapeDtypeStruct((heads, LIVE, tokens), jnp.float32)] * parts
        + [jax.ShapeDtypeStruct((LIVE, cols), jnp.bfloat16)] * 2,
        compiler_params=pltpu.CompilerParams(vmem_limit_bytes=VMEM),
        cost_estimate=pl.CostEstimate(
            flops=16 * parts * tokens * cols * LIVE,
            bytes_accessed=16 * parts * tokens * cols,
            transcendentals=0,
        ),
    )(length, raw, inv, gain, *moved, *moved)
    return outs[:parts], outs[parts], outs[parts + 1]


def gradient_call(raw, values, gain, moved, attends, tokens):
    parts = len(moved)
    cols = moved[0].shape[2]
    heads = cols // HD
    head, block, upper, lower, weights, gains = specs(tokens)
    outs = pl.pallas_call(
        functools.partial(gradient_kernel, parts),
        grid=(heads,),
        in_specs=[head, head, gains] + [upper] * parts + [lower] * parts + [weights] * parts,
        out_specs=[weights] * parts + [head, pl.BlockSpec((LIVE, HD), lambda h: (0, 0))],
        out_shape=[jax.ShapeDtypeStruct((heads, LIVE, tokens), jnp.bfloat16)] * parts
        + [
            jax.ShapeDtypeStruct((LIVE, cols), jnp.float32),
            jax.ShapeDtypeStruct((LIVE, HD), jnp.float32),
        ],
        compiler_params=pltpu.CompilerParams(vmem_limit_bytes=VMEM),
        cost_estimate=pl.CostEstimate(
            flops=16 * parts * tokens * cols * LIVE,
            bytes_accessed=16 * parts * tokens * cols,
            transcendentals=0,
        ),
    )(raw, values, gain, *moved, *moved, *attends)
    return outs[:parts], outs[parts], outs[parts + 1]


def query_call(keys, scores):
    parts = len(scores)
    heads, _, tokens = scores[0].shape
    head, block, _, _, weights, _ = specs(tokens)
    return pl.pallas_call(
        functools.partial(query_kernel, parts),
        grid=(heads,),
        in_specs=[head] + [weights] * parts,
        out_specs=[block] * parts,
        out_shape=[jax.ShapeDtypeStruct((tokens, keys.shape[1]), jnp.bfloat16)] * parts,
        compiler_params=pltpu.CompilerParams(vmem_limit_bytes=VMEM),
        cost_estimate=pl.CostEstimate(
            flops=8 * parts * tokens * keys.shape[1] * LIVE,
            bytes_accessed=8 * parts * tokens * keys.shape[1],
            transcendentals=0,
        ),
    )(keys, *scores)


def rows_spec(part, width, tiled=False):
    _, count, index = part
    if tiled:
        return pl.BlockSpec((count, width), lambda n: (index, n))
    return pl.BlockSpec((count, width), lambda n: (index, 0))


def pick_kernel(place_ref, first_ref, mine_ref, sibling_first_ref, sibling_ref, *out_refs):
    here = place_ref[0] == 0
    rows = out_refs[0].shape[1]
    for index, out_ref in enumerate(out_refs):
        at = pl.ds(pl.multiple_of(place_ref[2 + index] * rows, rows), rows)
        out_ref[:LIVE] = jnp.where(here, first_ref[:, at], sibling_first_ref[:, at])
        out_ref[LIVE:] = jnp.where(here, mine_ref[:, at], sibling_ref[:, at])


def pick_call(place, first, mine, sibling_first, sibling, rows):
    arrays = (first, mine, sibling_first, sibling)
    shape = (LIVE + mine.shape[0], rows)
    return pl.pallas_call(
        pick_kernel,
        grid=(1,),
        in_specs=[pl.BlockSpec(memory_space=pltpu.SMEM)]
        + [pl.BlockSpec(x.shape, lambda n: (0, 0)) for x in arrays],
        out_specs=[pl.BlockSpec(shape, lambda n: (0, 0))] * 2,
        out_shape=[jax.ShapeDtypeStruct(shape, jnp.bfloat16)] * 2,
        compiler_params=pltpu.CompilerParams(vmem_limit_bytes=VMEM),
        cost_estimate=pl.CostEstimate(flops=1000, bytes_accessed=1000, transcendentals=0),
    )(place, *arrays)


def product_kernel(videos, place_ref, *refs):
    mine_refs, sibling_refs = refs[:videos], refs[videos : 2 * videos]
    weight_refs, out_ref = refs[2 * videos : -1], refs[-1]
    rows = weight_refs[0].shape[0]
    total = None
    for step, weight_ref in enumerate(weight_refs):
        here = place_ref[step // 2] == 0
        at = pl.ds(pl.multiple_of(place_ref[2 + step % 2] * rows, rows), rows)
        block = jnp.concatenate(
            [jnp.where(here, m[:, at], s[:, at]) for m, s in zip(mine_refs, sibling_refs)], axis=0
        )
        term = jnp.dot(block, weight_ref[...], preferred_element_type=jnp.float32)
        total = term if total is None else total + term
    out_ref[...] = total


def product_call(place, mine, sibling, weights):
    videos = len(mine)
    width = weights[0][0].shape[1]
    parts = [*mine, *sibling, *weights]
    return pl.pallas_call(
        functools.partial(product_kernel, videos),
        grid=(1,),
        in_specs=[pl.BlockSpec(memory_space=pltpu.SMEM)]
        + [rows_spec(part, part[0].shape[1]) for part in parts],
        out_specs=pl.BlockSpec((videos * LIVE, width), lambda n: (0, 0)),
        out_shape=jax.ShapeDtypeStruct((videos * LIVE, width), jnp.float32),
        compiler_params=pltpu.CompilerParams(vmem_limit_bytes=VMEM),
        cost_estimate=pl.CostEstimate(flops=1000, bytes_accessed=1000, transcendentals=0),
    )(place, *[part[0] for part in parts])


def weights_kernel(columns_ref, *refs):
    parts = [ref[...] for ref in refs[:-1]]
    refs[-1][...] = jnp.dot(
        columns_ref[...], jnp.concatenate(parts, axis=0), preferred_element_type=jnp.float32
    )


def weights_call(columns, parts):
    rows, depth = columns.shape
    cols = parts[0][0].shape[1]
    tile = min(cols, 512)
    return pl.pallas_call(
        weights_kernel,
        grid=(cols // tile,),
        in_specs=[pl.BlockSpec(columns.shape, lambda n: (0, 0))]
        + [rows_spec(part, tile, True) for part in parts],
        out_specs=pl.BlockSpec((rows, tile), lambda n: (0, n)),
        out_shape=jax.ShapeDtypeStruct((rows, cols), jnp.float32),
        compiler_params=pltpu.CompilerParams(vmem_limit_bytes=VMEM),
        cost_estimate=pl.CostEstimate(
            flops=2 * rows * cols * depth,
            bytes_accessed=4 * rows * cols + 2 * depth * (rows + cols),
            transcendentals=0,
        ),
    )(columns, *[part[0] for part in parts])


def after(x, *others):
    return lax.optimization_barrier((x, *others))[0]


def blocks_kernel(lanes_ref, query_ref, grad_ref, *out_refs):
    cols = out_refs[0].shape[2]
    for index, out_ref in enumerate(out_refs):
        at = pl.ds(pl.multiple_of(lanes_ref[index] * cols, cols), cols)
        out_ref[0] = query_ref[:, at]
        out_ref[1] = grad_ref[:, at]


def blocks_call(lanes, query, grad):
    parts = lanes.shape[0]
    tokens, hid = query.shape
    cols, tiles = hid // parts, 4
    rows = tokens // tiles
    return pl.pallas_call(
        blocks_kernel,
        grid=(tiles,),
        in_specs=[pl.BlockSpec(memory_space=pltpu.SMEM)]
        + [pl.BlockSpec((rows, hid), lambda n: (n, 0))] * 2,
        out_specs=[pl.BlockSpec((2, rows, cols), lambda n: (0, n, 0))] * parts,
        out_shape=[jax.ShapeDtypeStruct((2, tokens, cols), jnp.bfloat16)] * parts,
        compiler_params=pltpu.CompilerParams(vmem_limit_bytes=VMEM),
        cost_estimate=pl.CostEstimate(
            flops=1000, bytes_accessed=8 * tokens * hid, transcendentals=0
        ),
    )(lanes, query, grad)


def pack_kernel(moves, inputs, place_ref, *refs):
    ins, outs = refs[:inputs], refs[inputs:]

    def span(at, width):
        if isinstance(at, int):
            return pl.ds(at, width)
        return pl.ds(pl.multiple_of(place_ref[at[0]] * width, width), width)

    for source, row, col, count, width, target, to_row, to_col in moves:
        block = ins[source][pl.ds(row, count), span(col, width)]
        outs[target][pl.ds(to_row, count), span(to_col, width)] = block


def pack_call(place, arrays, shapes, moves, tiles=1, size=1000):
    def spec(shape):
        return pl.BlockSpec((shape[0] // tiles, shape[1]), lambda n: (n, 0))

    return pl.pallas_call(
        functools.partial(pack_kernel, moves, len(arrays)),
        grid=(tiles,),
        in_specs=[pl.BlockSpec(memory_space=pltpu.SMEM)] + [spec(x.shape) for x in arrays],
        out_specs=[spec(shape) for shape in shapes],
        out_shape=[jax.ShapeDtypeStruct(shape, jnp.bfloat16) for shape in shapes],
        compiler_params=pltpu.CompilerParams(vmem_limit_bytes=VMEM),
        cost_estimate=pl.CostEstimate(flops=1000, bytes_accessed=size, transcendentals=0),
    )(place, *arrays)


def shards(n_dp, n_seq, query, caption, key_weight, value_weight, key_gain, lengths, out_grad):
    rows, cols = key_weight.shape
    hid = cols * n_seq
    lines = n_dp // 2
    half = cols // 2
    wide = 2 * rows
    tokens = query.shape[1]
    me = lax.axis_index("dp")
    lane = lax.axis_index("seq")
    quad, low, side = me // 4, me // 2 % 2, me % 2
    core = lane % 2

    def over_dp(x, step):
        return lax.ppermute(x, "dp", [(a, a ^ step) for a in range(n_dp)])

    def over_seq(x, step):
        return lax.ppermute(x, "seq", [(a, a ^ step) for a in range(n_seq)])

    def col_block(x, index, width):
        return lax.dynamic_slice(x, (0, index * width), (x.shape[0], width))

    pieces = wide // half
    quads = lines // 2
    scalars = [low, 1 - low, quad * 2 + core, quad * 2 + 1 - core]
    scalars += [(quad ^ (s // 2)) * 2 + core for s in range(2, lines)]
    scalars += [(quad * 2 + core) * pieces + p for p in range(pieces)]
    place = jnp.stack(scalars).astype(jnp.int32)
    near_at = lines + 2
    near_given, kept, value_given, mine_first, sibling_first, *given = pack_call(
        place,
        [key_weight, value_weight, caption[0]],
        [(rows + pieces * LIVE, half), (2 * rows, half), (rows, half)] + [(LIVE, wide)] * lines,
        [
            (0, 0, (1,), rows, half, 0, 0, 0),
            (0, 0, (0,), rows, half, 1, 0, 0),
            (1, 0, (0,), rows, half, 1, rows, 0),
            (1, 0, (1,), rows, half, 2, 0, 0),
        ]
        + [(2, 0, (near_at + p,), LIVE, half, 0, rows + p * LIVE, 0) for p in range(pieces)]
        + [(2, 0, (2 + s,), LIVE, wide, 3 + s, 0, 0) for s in range(lines)],
    )
    near = over_dp(near_given, 2)
    beside = over_dp(kept, 1)
    arrived = [over_dp(x, 2 * s) for s, x in enumerate(given, 2)]

    lanes = jnp.stack([lane ^ s for s in range(n_seq)]).astype(jnp.int32)
    packed = blocks_call(after(lanes, kept), query[0], out_grad[0])
    moved = [packed[0]] + [None] * (n_seq - 1)
    previous = ()
    for s in range(2, n_seq):
        moved[s] = over_seq(after(packed[s], *previous), s)
        previous = (moved[s],)
    moved[1] = over_seq(after(packed[1], beside), 1)

    key_near, shared, shared_given = pack_call(
        place,
        [near, *arrived],
        [(rows, half)] + [((lines - 1) * LIVE, wide)] * 2,
        [(0, 0, 0, rows, half, 0, 0, 0)]
        + [
            (0, rows + p * LIVE, 0, LIVE, half, out, 0, p * half)
            for p in range(pieces)
            for out in (1, 2)
        ]
        + [
            (s - 1, 0, 0, LIVE, wide, out, (s - 1) * LIVE, 0)
            for s in range(2, lines)
            for out in (1, 2)
        ],
    )
    key_far = over_dp(key_near, 1)
    value_near = over_dp(after(value_given, near, *arrived), 2)
    value_far = over_dp(value_near, 1)
    sibling = over_seq(shared_given, 1)
    key_quad = ((kept, rows, 0), (beside, rows, 0), (key_near, rows, 0), (key_far, rows, 0))
    value_quad = ((kept, rows, 1), (beside, rows, 1), (value_near, rows, 0), (value_far, rows, 0))

    places = jnp.stack([core ^ low, 1 - (core ^ low), side, 1 - side]).astype(jnp.int32)

    def product(places, weights, other):
        chosen = [s for s in range(lines) if bool(s & 2) == other]
        return product_call(
            places,
            [(shared, LIVE, s - 1) if s else (mine_first, LIVE, 0) for s in chosen],
            [(sibling, LIVE, s - 1) if s else (sibling_first, LIVE, 0) for s in chosen],
            weights,
        )

    def reduced(total):
        step = 8
        while step < n_dp:
            count = total.shape[0] // 2
            total = total[:count] + over_dp(total[count:], step)
            step *= 2
        return lax.reduce_precision(total, 8, 7).astype(jnp.bfloat16)

    def joined(total):
        own, other = total[:LIVE], over_dp(total[LIVE:], 2)
        return jnp.where(
            low == 0,
            jnp.concatenate([own, other], axis=1),
            jnp.concatenate([other, own], axis=1),
        )

    def seq_sum(x, before=()):
        step = 1
        while step < n_seq:
            x = x + over_seq(x, step)
            if step == 1:
                x = after(x, *before)
            step *= 2
        return x

    gain = lax.dynamic_slice(key_gain, (lane * cols,), (cols,)).reshape(1, cols)
    own_columns, other_given = pick_call(places, mine_first, shared, sibling_first, sibling, rows)
    key_product = product(after(places, own_columns), key_quad, True)
    key_sent = over_dp(key_product, 4)
    later = after(places, key_product)
    other_columns = over_dp(after(other_given, key_product), 1)
    columns = jnp.concatenate([own_columns, other_columns], axis=0).T
    value_product = product(later, value_quad, True)
    value_rest_product = product(later, value_quad, False)
    key_sent = after(key_sent, value_product, value_rest_product, columns, gain)
    key_total = reduced(product(later, key_quad, False) + key_sent)
    raw = joined(key_total)
    value_sent = over_dp(after(value_product, raw), 4)
    raw_wide = raw.astype(jnp.float32)
    squares = seq_sum(jnp.sum(raw_wide * raw_wide, axis=-1, keepdims=True))
    inv_rms = lax.rsqrt(squares / hid + 1e-06)
    attends, keys, value_grad = attend_call(
        lengths, after(raw, columns), inv_rms, gain, moved, tokens
    )
    values = joined(reduced(value_rest_product + after(value_sent, value_grad)))

    value_given = after(value_grad, values)
    value_near_parts = [over_dp(value_given, 2 * s) for s in range(1, lines)]
    value_first = over_dp(value_given, 1)
    scores, scaled, inner = gradient_call(raw, values, gain, moved, attends, tokens)
    outs = query_call(keys, scores)
    inner = after(inner, value_first)
    inner_mean = seq_sum(jnp.sum(inner, axis=-1, keepdims=True), value_near_parts) / hid
    raw_grad = (inv_rms * scaled - raw_wide * inv_rms**3 * inner_mean).astype(jnp.bfloat16)
    value_rest = over_dp(jnp.concatenate(value_near_parts, axis=0), 1)
    key_near_parts = [over_dp(raw_grad, 2 * s) for s in range(1, lines)]
    placed = [outs[0]] + [None] * (n_seq - 1)
    previous = (inner_mean,)
    for s in range(2, n_seq):
        placed[s] = over_seq(after(outs[s], *previous), s)
        previous = (placed[s], key_near_parts[0])
    placed[1] = over_seq(after(outs[1], value_rest), 1)
    key_first = over_dp(raw_grad, 1)
    key_rest = over_dp(after(jnp.concatenate(key_near_parts, axis=0), key_first), 1)
    key_parts = (
        [(x, LIVE, 0) for x in (raw_grad, *key_near_parts)]
        + [(key_first, LIVE, 0)]
        + [(key_rest, LIVE, s) for s in range(lines - 1)]
    )
    value_parts = (
        [(x, LIVE, 0) for x in (value_grad, *value_near_parts)]
        + [(value_first, LIVE, 0)]
        + [(value_rest, LIVE, s) for s in range(lines - 1)]
    )
    value_weight_grad = weights_call(after(columns, key_first), value_parts)
    key_weight_grad = weights_call(columns, key_parts)

    (query_grad,) = pack_call(
        lanes,
        placed,
        [(tokens, hid)],
        [(s, 0, 0, tokens // 2, cols, 0, 0, (s,)) for s in range(n_seq)],
        2,
    )
    return query_grad[None], key_weight_grad, value_weight_grad


def solution(mesh):
    placed = (
        P("dp", "seq", None),
        P("dp", None, None),
        P("dp", "seq"),
        P("dp", "seq"),
        P(),
        P("dp"),
        P("dp", "seq", None),
    )
    return jax.shard_map(
        functools.partial(shards, mesh.shape["dp"], mesh.shape["seq"]),
        mesh=mesh,
        in_specs=placed,
        out_specs=(P("dp", "seq", None), P("dp", "seq"), P("dp", "seq")),
        check_vma=False,
    )
```

```python
import functools

import jax
import jax.numpy as jnp
from jax import lax
from jax.experimental import pallas as pl
from jax.experimental.pallas import tpu as pltpu
from jax.sharding import PartitionSpec as P

HD = 128
LIVE = 128
VMEM = 60 * 1024 * 1024


ROWS = (((1,), (1,)), ((), ()))
COLUMNS = (((0,), (0,)), ((), ()))
FACTOR = HD ** (-0.5)


def attend_kernel(parts, length_ref, raw_ref, inv_ref, gain_ref, *refs):
    query_refs, grad_refs = refs[:parts], refs[parts : 2 * parts]
    attend_refs = refs[2 * parts : 3 * parts]
    keys_ref, value_grad_ref = refs[3 * parts :]
    keys = (raw_ref[...].astype(jnp.float32) * inv_ref[...] * gain_ref[...]).astype(jnp.bfloat16)
    keys_ref[...] = keys
    valid = lax.broadcasted_iota(jnp.int32, (LIVE, 1), 0) < length_ref[0]
    for head in range(keys.shape[1] // HD):
        at = slice(head * HD, (head + 1) * HD)
        value_grad = jnp.zeros((LIVE, HD), jnp.float32)
        for query_ref, grad_ref, attend_ref in zip(query_refs, grad_refs, attend_refs):
            scores = lax.dot_general(
                keys[:, at], query_ref[:, at], ROWS, preferred_element_type=jnp.float32
            )
            scores = jnp.where(valid, scores * FACTOR, -jnp.inf)
            powers = jnp.exp(scores - jnp.max(scores, axis=0, keepdims=True))
            attend = powers * (1.0 / jnp.sum(powers, axis=0, keepdims=True))
            attend_ref[head] = attend
            value_grad += jnp.dot(
                attend.astype(jnp.bfloat16), grad_ref[:, at], preferred_element_type=jnp.float32
            )
        value_grad_ref[:, at] = value_grad.astype(jnp.bfloat16)


def gradient_kernel(parts, raw_ref, value_ref, gain_ref, *refs):
    query_refs, grad_refs = refs[:parts], refs[parts : 2 * parts]
    attend_refs, score_refs = refs[2 * parts : 3 * parts], refs[3 * parts : 4 * parts]
    scaled_ref, inner_ref = refs[4 * parts :]

    @pl.when(pl.program_id(0) == 0)
    def _():
        inner_ref[...] = jnp.zeros_like(inner_ref)

    for head in range(value_ref.shape[1] // HD):
        at = slice(head * HD, (head + 1) * HD)
        key_grad = jnp.zeros((LIVE, HD), jnp.float32)
        for query_ref, grad_ref, attend_ref, score_ref in zip(
            query_refs, grad_refs, attend_refs, score_refs
        ):
            attend = attend_ref[head]
            dattend = lax.dot_general(
                value_ref[:, at], grad_ref[:, at], ROWS, preferred_element_type=jnp.float32
            )
            delta = jnp.sum(attend * dattend, axis=0, keepdims=True)
            dscores = (attend * (dattend - delta)).astype(jnp.bfloat16)
            score_ref[head] = dscores
            key_grad += jnp.dot(dscores, query_ref[:, at], preferred_element_type=jnp.float32)
        scaled = key_grad * FACTOR * gain_ref[:, at]
        scaled_ref[:, at] = scaled
        inner_ref[...] += scaled * raw_ref[:, at].astype(jnp.float32)


def query_kernel(parts, keys_ref, *refs):
    for head in range(keys_ref.shape[1] // HD):
        at = slice(head * HD, (head + 1) * HD)
        for score_ref, out_ref in zip(refs[:parts], refs[parts:]):
            out = lax.dot_general(
                score_ref[head], keys_ref[:, at], COLUMNS, preferred_element_type=jnp.float32
            )
            out_ref[:, at] = (out * FACTOR).astype(jnp.bfloat16)


def specs(tokens, heads):
    group = 2 - heads % 2
    width = group * HD
    head = pl.BlockSpec((LIVE, width), lambda h: (0, h))
    block = pl.BlockSpec((tokens, width), lambda h: (0, h))
    upper = pl.BlockSpec((None, tokens, width), lambda h: (0, 0, h))
    lower = pl.BlockSpec((None, tokens, width), lambda h: (1, 0, h))
    weights = pl.BlockSpec((group, LIVE, tokens), lambda h: (h, 0, 0))
    gain = pl.BlockSpec((1, width), lambda h: (0, h))
    return heads // group, head, block, upper, lower, weights, gain


def attend_call(length, raw, inv, gain, moved, tokens):
    parts = len(moved)
    cols = moved[0].shape[2]
    heads = cols // HD
    steps, head, block, upper, lower, weights, gains = specs(tokens, heads)
    outs = pl.pallas_call(
        functools.partial(attend_kernel, parts),
        grid=(steps,),
        in_specs=[
            pl.BlockSpec(memory_space=pltpu.SMEM),
            head,
            pl.BlockSpec((LIVE, 1), lambda h: (0, 0)),
            gains,
        ]
        + [upper] * parts
        + [lower] * parts,
        out_specs=[weights] * parts + [head, head],
        out_shape=[jax.ShapeDtypeStruct((heads, LIVE, tokens), jnp.float32)] * parts
        + [jax.ShapeDtypeStruct((LIVE, cols), jnp.bfloat16)] * 2,
        compiler_params=pltpu.CompilerParams(vmem_limit_bytes=VMEM),
        cost_estimate=pl.CostEstimate(
            flops=16 * parts * tokens * cols * LIVE,
            bytes_accessed=16 * parts * tokens * cols,
            transcendentals=0,
        ),
    )(length, raw, inv, gain, *moved, *moved)
    return outs[:parts], outs[parts], outs[parts + 1]


def gradient_call(raw, values, gain, moved, attends, tokens):
    parts = len(moved)
    cols = moved[0].shape[2]
    heads = cols // HD
    steps, head, block, upper, lower, weights, gains = specs(tokens, heads)
    outs = pl.pallas_call(
        functools.partial(gradient_kernel, parts),
        grid=(steps,),
        in_specs=[head, head, gains] + [upper] * parts + [lower] * parts + [weights] * parts,
        out_specs=[weights] * parts + [head, pl.BlockSpec((LIVE, HD), lambda h: (0, 0))],
        out_shape=[jax.ShapeDtypeStruct((heads, LIVE, tokens), jnp.bfloat16)] * parts
        + [
            jax.ShapeDtypeStruct((LIVE, cols), jnp.float32),
            jax.ShapeDtypeStruct((LIVE, HD), jnp.float32),
        ],
        compiler_params=pltpu.CompilerParams(vmem_limit_bytes=VMEM),
        cost_estimate=pl.CostEstimate(
            flops=16 * parts * tokens * cols * LIVE,
            bytes_accessed=16 * parts * tokens * cols,
            transcendentals=0,
        ),
    )(raw, values, gain, *moved, *moved, *attends)
    return outs[:parts], outs[parts], outs[parts + 1]


def query_call(keys, scores):
    parts = len(scores)
    heads, _, tokens = scores[0].shape
    steps, head, block, _, _, weights, _ = specs(tokens, heads)
    return pl.pallas_call(
        functools.partial(query_kernel, parts),
        grid=(steps,),
        in_specs=[head] + [weights] * parts,
        out_specs=[block] * parts,
        out_shape=[jax.ShapeDtypeStruct((tokens, keys.shape[1]), jnp.bfloat16)] * parts,
        compiler_params=pltpu.CompilerParams(vmem_limit_bytes=VMEM),
        cost_estimate=pl.CostEstimate(
            flops=8 * parts * tokens * keys.shape[1] * LIVE,
            bytes_accessed=8 * parts * tokens * keys.shape[1],
            transcendentals=0,
        ),
    )(keys, *scores)


def rows_spec(part, width, tiled=False):
    _, count, index = part
    if tiled:
        return pl.BlockSpec((count, width), lambda n: (index, n))
    return pl.BlockSpec((count, width), lambda n: (index, 0))


def pick_kernel(place_ref, first_ref, mine_ref, sibling_first_ref, sibling_ref, *out_refs):
    here = place_ref[0] == 0
    rows = out_refs[0].shape[1]
    for index, out_ref in enumerate(out_refs):
        at = pl.ds(pl.multiple_of(place_ref[2 + index] * rows, rows), rows)
        out_ref[:LIVE] = jnp.where(here, first_ref[:, at], sibling_first_ref[:, at])
        out_ref[LIVE:] = jnp.where(here, mine_ref[:, at], sibling_ref[:, at])


def pick_call(place, first, mine, sibling_first, sibling, rows):
    arrays = (first, mine, sibling_first, sibling)
    shape = (LIVE + mine.shape[0], rows)
    return pl.pallas_call(
        pick_kernel,
        grid=(1,),
        in_specs=[pl.BlockSpec(memory_space=pltpu.SMEM)]
        + [pl.BlockSpec(x.shape, lambda n: (0, 0)) for x in arrays],
        out_specs=[pl.BlockSpec(shape, lambda n: (0, 0))] * 2,
        out_shape=[jax.ShapeDtypeStruct(shape, jnp.bfloat16)] * 2,
        compiler_params=pltpu.CompilerParams(vmem_limit_bytes=VMEM),
        cost_estimate=pl.CostEstimate(flops=1000, bytes_accessed=1000, transcendentals=0),
    )(place, *arrays)


def product_kernel(videos, place_ref, *refs):
    mine_refs, sibling_refs = refs[:videos], refs[videos : 2 * videos]
    weight_refs, out_ref = refs[2 * videos : -1], refs[-1]
    rows = weight_refs[0].shape[0]
    total = None
    for step, weight_ref in enumerate(weight_refs):
        here = place_ref[step // 2] == 0
        at = pl.ds(pl.multiple_of(place_ref[2 + step % 2] * rows, rows), rows)
        block = jnp.concatenate(
            [jnp.where(here, m[:, at], s[:, at]) for m, s in zip(mine_refs, sibling_refs)], axis=0
        )
        term = jnp.dot(block, weight_ref[...], preferred_element_type=jnp.float32)
        total = term if total is None else total + term
    out_ref[...] = total


def product_call(place, mine, sibling, weights):
    videos = len(mine)
    width = weights[0][0].shape[1]
    parts = [*mine, *sibling, *weights]
    return pl.pallas_call(
        functools.partial(product_kernel, videos),
        grid=(1,),
        in_specs=[pl.BlockSpec(memory_space=pltpu.SMEM)]
        + [rows_spec(part, part[0].shape[1]) for part in parts],
        out_specs=pl.BlockSpec((videos * LIVE, width), lambda n: (0, 0)),
        out_shape=jax.ShapeDtypeStruct((videos * LIVE, width), jnp.float32),
        compiler_params=pltpu.CompilerParams(vmem_limit_bytes=VMEM),
        cost_estimate=pl.CostEstimate(flops=1000, bytes_accessed=1000, transcendentals=0),
    )(place, *[part[0] for part in parts])


def weights_kernel(columns_ref, *refs):
    parts = [ref[...] for ref in refs[:-1]]
    refs[-1][...] = jnp.dot(
        columns_ref[...], jnp.concatenate(parts, axis=0), preferred_element_type=jnp.float32
    )


def weights_call(columns, parts):
    rows, depth = columns.shape
    cols = parts[0][0].shape[1]
    tile = min(cols, 512)
    return pl.pallas_call(
        weights_kernel,
        grid=(cols // tile,),
        in_specs=[pl.BlockSpec(columns.shape, lambda n: (0, 0))]
        + [rows_spec(part, tile, True) for part in parts],
        out_specs=pl.BlockSpec((rows, tile), lambda n: (0, n)),
        out_shape=jax.ShapeDtypeStruct((rows, cols), jnp.float32),
        compiler_params=pltpu.CompilerParams(vmem_limit_bytes=VMEM),
        cost_estimate=pl.CostEstimate(
            flops=2 * rows * cols * depth,
            bytes_accessed=4 * rows * cols + 2 * depth * (rows + cols),
            transcendentals=0,
        ),
    )(columns, *[part[0] for part in parts])


def after(x, *others):
    return lax.optimization_barrier((x, *others))[0]


def blocks_kernel(lanes_ref, query_ref, grad_ref, *out_refs):
    cols = out_refs[0].shape[2]
    for index, out_ref in enumerate(out_refs):
        at = pl.ds(pl.multiple_of(lanes_ref[index] * cols, cols), cols)
        out_ref[0] = query_ref[:, at]
        out_ref[1] = grad_ref[:, at]


def blocks_call(lanes, query, grad):
    parts = lanes.shape[0]
    tokens, hid = query.shape
    cols, tiles = hid // parts, 4
    rows = tokens // tiles
    return pl.pallas_call(
        blocks_kernel,
        grid=(tiles,),
        in_specs=[pl.BlockSpec(memory_space=pltpu.SMEM)]
        + [pl.BlockSpec((rows, hid), lambda n: (n, 0))] * 2,
        out_specs=[pl.BlockSpec((2, rows, cols), lambda n: (0, n, 0))] * parts,
        out_shape=[jax.ShapeDtypeStruct((2, tokens, cols), jnp.bfloat16)] * parts,
        compiler_params=pltpu.CompilerParams(vmem_limit_bytes=VMEM),
        cost_estimate=pl.CostEstimate(
            flops=1000, bytes_accessed=8 * tokens * hid, transcendentals=0
        ),
    )(lanes, query, grad)


def pack_kernel(moves, inputs, place_ref, *refs):
    ins, outs = refs[:inputs], refs[inputs:]

    def span(at, width):
        if isinstance(at, int):
            return pl.ds(at, width)
        return pl.ds(pl.multiple_of(place_ref[at[0]] * width, width), width)

    for source, row, col, count, width, target, to_row, to_col in moves:
        block = ins[source][pl.ds(row, count), span(col, width)]
        outs[target][pl.ds(to_row, count), span(to_col, width)] = block


def pack_call(place, arrays, shapes, moves, tiles=1, size=1000):
    def spec(shape):
        return pl.BlockSpec((shape[0] // tiles, shape[1]), lambda n: (n, 0))

    return pl.pallas_call(
        functools.partial(pack_kernel, moves, len(arrays)),
        grid=(tiles,),
        in_specs=[pl.BlockSpec(memory_space=pltpu.SMEM)] + [spec(x.shape) for x in arrays],
        out_specs=[spec(shape) for shape in shapes],
        out_shape=[jax.ShapeDtypeStruct(shape, jnp.bfloat16) for shape in shapes],
        compiler_params=pltpu.CompilerParams(vmem_limit_bytes=VMEM),
        cost_estimate=pl.CostEstimate(flops=1000, bytes_accessed=size, transcendentals=0),
    )(place, *arrays)


def shards(n_dp, n_seq, query, caption, key_weight, value_weight, key_gain, lengths, out_grad):
    rows, cols = key_weight.shape
    hid = cols * n_seq
    lines = n_dp // 2
    half = cols // 2
    wide = 2 * rows
    tokens = query.shape[1]
    me = lax.axis_index("dp")
    lane = lax.axis_index("seq")
    quad, low, side = me // 4, me // 2 % 2, me % 2
    core = lane % 2

    def over_dp(x, step):
        return lax.ppermute(x, "dp", [(a, a ^ step) for a in range(n_dp)])

    def over_seq(x, step):
        return lax.ppermute(x, "seq", [(a, a ^ step) for a in range(n_seq)])

    def col_block(x, index, width):
        return lax.dynamic_slice(x, (0, index * width), (x.shape[0], width))

    pieces = wide // half
    quads = lines // 2
    scalars = [low, 1 - low, quad * 2 + core, quad * 2 + 1 - core]
    scalars += [(quad ^ (s // 2)) * 2 + core for s in range(2, lines)]
    scalars += [(quad * 2 + core) * pieces + p for p in range(pieces)]
    place = jnp.stack(scalars).astype(jnp.int32)
    near_at = lines + 2
    near_given, kept, value_given, mine_first, sibling_first, *given = pack_call(
        place,
        [key_weight, value_weight, caption[0]],
        [(rows + pieces * LIVE, half), (2 * rows, half), (rows, half)] + [(LIVE, wide)] * lines,
        [
            (0, 0, (1,), rows, half, 0, 0, 0),
            (0, 0, (0,), rows, half, 1, 0, 0),
            (1, 0, (0,), rows, half, 1, rows, 0),
            (1, 0, (1,), rows, half, 2, 0, 0),
        ]
        + [(2, 0, (near_at + p,), LIVE, half, 0, rows + p * LIVE, 0) for p in range(pieces)]
        + [(2, 0, (2 + s,), LIVE, wide, 3 + s, 0, 0) for s in range(lines)],
    )
    near = over_dp(near_given, 2)
    beside = over_dp(kept, 1)
    arrived = [over_dp(x, 2 * s) for s, x in enumerate(given, 2)]

    lanes = jnp.stack([lane ^ s for s in range(n_seq)]).astype(jnp.int32)
    packed = blocks_call(after(lanes, kept), query[0], out_grad[0])
    moved = [packed[0]] + [None] * (n_seq - 1)
    previous = ()
    for s in range(2, n_seq):
        moved[s] = over_seq(after(packed[s], *previous), s)
        previous = (moved[s],)
    moved[1] = over_seq(after(packed[1], beside), 1)

    key_near, shared, shared_given = pack_call(
        place,
        [near, *arrived],
        [(rows, half)] + [((lines - 1) * LIVE, wide)] * 2,
        [(0, 0, 0, rows, half, 0, 0, 0)]
        + [
            (0, rows + p * LIVE, 0, LIVE, half, out, 0, p * half)
            for p in range(pieces)
            for out in (1, 2)
        ]
        + [
            (s - 1, 0, 0, LIVE, wide, out, (s - 1) * LIVE, 0)
            for s in range(2, lines)
            for out in (1, 2)
        ],
    )
    key_far = over_dp(key_near, 1)
    value_near = over_dp(after(value_given, near, *arrived), 2)
    value_far = over_dp(value_near, 1)
    sibling = over_seq(shared_given, 1)
    key_quad = ((kept, rows, 0), (beside, rows, 0), (key_near, rows, 0), (key_far, rows, 0))
    value_quad = ((kept, rows, 1), (beside, rows, 1), (value_near, rows, 0), (value_far, rows, 0))

    places = jnp.stack([core ^ low, 1 - (core ^ low), side, 1 - side]).astype(jnp.int32)

    def product(places, weights, other):
        chosen = [s for s in range(lines) if bool(s & 2) == other]
        return product_call(
            places,
            [(shared, LIVE, s - 1) if s else (mine_first, LIVE, 0) for s in chosen],
            [(sibling, LIVE, s - 1) if s else (sibling_first, LIVE, 0) for s in chosen],
            weights,
        )

    def reduced(total):
        step = 8
        while step < n_dp:
            count = total.shape[0] // 2
            total = total[:count] + over_dp(total[count:], step)
            step *= 2
        return lax.reduce_precision(total, 8, 7).astype(jnp.bfloat16)

    def joined(own, other):
        return jnp.where(
            low == 0,
            jnp.concatenate([own, other], axis=1),
            jnp.concatenate([other, own], axis=1),
        )

    def seq_sum(x):
        for step in steps:
            x = x + over_seq(x, step)
        return x

    steps = [1 << k for k in reversed(range(n_seq.bit_length() - 1))]
    gain = lax.dynamic_slice(key_gain, (lane * cols,), (cols,)).reshape(1, cols)
    own_columns, other_given = pick_call(places, mine_first, shared, sibling_first, sibling, rows)
    key_product = product(after(places, own_columns), key_quad, True)
    key_sent = over_dp(key_product, 4)
    later = after(places, key_product)
    other_columns = over_dp(after(other_given, key_product), 1)
    columns = jnp.concatenate([own_columns, other_columns], axis=0).T
    value_product = product(later, value_quad, True)
    value_rest_product = product(later, value_quad, False)
    key_sent = after(key_sent, value_product, value_rest_product, columns, gain)
    value_sent = over_dp(after(value_product, key_sent), 4)
    key_total = reduced(product(later, key_quad, False) + key_sent)
    raw = joined(key_total[:LIVE], over_dp(key_total[LIVE:], 2))
    raw_wide = raw.astype(jnp.float32)
    squares = seq_sum(jnp.sum(raw_wide * raw_wide, axis=-1, keepdims=True))
    inv_rms = lax.rsqrt(squares / hid + 1e-06)
    value_total = reduced(value_rest_product + after(value_sent, inv_rms))
    value_other = over_dp(value_total[LIVE:], 2)
    attends, keys, value_grad = attend_call(
        lengths, after(raw, columns, value_total), inv_rms, gain, moved, tokens
    )

    values = joined(value_total[:LIVE], after(value_other, value_grad))

    value_near_parts = [over_dp(value_grad, 2 * s) for s in range(1, lines)]
    value_first = over_dp(value_grad, 1)
    scores, scaled, inner = gradient_call(raw, values, gain, moved, attends, tokens)
    outs = query_call(keys, scores)
    inner = jnp.sum(after(inner, value_first), axis=-1, keepdims=True)
    for step in steps[:-1]:
        inner = inner + over_seq(inner, step)
    far_sum = after(inner, *value_near_parts)
    inner_mean = (far_sum + over_seq(far_sum, 1)) / hid
    raw_grad = (inv_rms * scaled - raw_wide * inv_rms**3 * inner_mean).astype(jnp.bfloat16)
    value_rest = over_dp(jnp.concatenate(value_near_parts, axis=0), 1)
    key_near_parts = [over_dp(raw_grad, 2 * s) for s in range(1, lines)]
    placed = [outs[0]] + [None] * (n_seq - 1)
    previous = (inner,)
    for s in range(2, n_seq):
        placed[s] = over_seq(after(outs[s], *previous), s)
        previous = (placed[s], key_near_parts[0])
    placed[1] = over_seq(after(outs[1], value_rest), 1)
    key_first = over_dp(raw_grad, 1)
    key_rest = over_dp(after(jnp.concatenate(key_near_parts, axis=0), key_first), 1)
    key_parts = (
        [(x, LIVE, 0) for x in (raw_grad, *key_near_parts)]
        + [(key_first, LIVE, 0)]
        + [(key_rest, LIVE, s) for s in range(lines - 1)]
    )
    value_parts = (
        [(x, LIVE, 0) for x in (value_grad, *value_near_parts)]
        + [(value_first, LIVE, 0)]
        + [(value_rest, LIVE, s) for s in range(lines - 1)]
    )
    value_weight_grad = weights_call(after(columns, key_first), value_parts)
    (query_grad,) = pack_call(
        lanes,
        placed,
        [(tokens, hid)],
        [(s, 0, 0, tokens // 2, cols, 0, 0, (s,)) for s in range(n_seq)],
        2,
    )
    key_weight_grad = weights_call(after(columns, query_grad), key_parts)
    return query_grad[None], key_weight_grad, value_weight_grad


def solution(mesh):
    placed = (
        P("dp", "seq", None),
        P("dp", None, None),
        P("dp", "seq"),
        P("dp", "seq"),
        P(),
        P("dp"),
        P("dp", "seq", None),
    )
    return jax.shard_map(
        functools.partial(shards, mesh.shape["dp"], mesh.shape["seq"]),
        mesh=mesh,
        in_specs=placed,
        out_specs=(P("dp", "seq", None), P("dp", "seq"), P("dp", "seq")),
        check_vma=False,
    )
```

```python
import functools

import jax
import jax.numpy as jnp
from jax import lax
from jax.experimental import pallas as pl
from jax.experimental.pallas import tpu as pltpu
from jax.sharding import PartitionSpec as P

HD = 128
LIVE = 128
VMEM = 60 * 1024 * 1024


ROWS = (((1,), (1,)), ((), ()))
COLUMNS = (((0,), (0,)), ((), ()))
FACTOR = HD ** (-0.5)


def attend_kernel(parts, length_ref, raw_ref, inv_ref, gain_ref, *refs):
    query_refs, grad_refs = refs[:parts], refs[parts : 2 * parts]
    attend_refs = refs[2 * parts : 3 * parts]
    keys_ref, value_grad_ref = refs[3 * parts :]
    keys = (raw_ref[...].astype(jnp.float32) * inv_ref[...] * gain_ref[...]).astype(jnp.bfloat16)
    keys_ref[...] = keys
    valid = lax.broadcasted_iota(jnp.int32, (LIVE, 1), 0) < length_ref[0]
    for head in range(keys.shape[1] // HD):
        at = slice(head * HD, (head + 1) * HD)
        value_grad = jnp.zeros((LIVE, HD), jnp.float32)
        for query_ref, grad_ref, attend_ref in zip(query_refs, grad_refs, attend_refs):
            scores = lax.dot_general(
                keys[:, at], query_ref[:, at], ROWS, preferred_element_type=jnp.float32
            )
            scores = jnp.where(valid, scores * FACTOR, -jnp.inf)
            powers = jnp.exp(scores - jnp.max(scores, axis=0, keepdims=True))
            attend = powers * (1.0 / jnp.sum(powers, axis=0, keepdims=True))
            attend_ref[head] = attend
            value_grad += jnp.dot(
                attend.astype(jnp.bfloat16), grad_ref[:, at], preferred_element_type=jnp.float32
            )
        value_grad_ref[:, at] = value_grad.astype(jnp.bfloat16)


def gradient_kernel(parts, raw_ref, value_ref, gain_ref, *refs):
    query_refs, grad_refs = refs[:parts], refs[parts : 2 * parts]
    attend_refs, score_refs = refs[2 * parts : 3 * parts], refs[3 * parts : 4 * parts]
    scaled_ref, inner_ref = refs[4 * parts :]

    @pl.when(pl.program_id(0) == 0)
    def _():
        inner_ref[...] = jnp.zeros_like(inner_ref)

    for head in range(value_ref.shape[1] // HD):
        at = slice(head * HD, (head + 1) * HD)
        key_grad = jnp.zeros((LIVE, HD), jnp.float32)
        for query_ref, grad_ref, attend_ref, score_ref in zip(
            query_refs, grad_refs, attend_refs, score_refs
        ):
            attend = attend_ref[head]
            dattend = lax.dot_general(
                value_ref[:, at], grad_ref[:, at], ROWS, preferred_element_type=jnp.float32
            )
            delta = jnp.sum(attend * dattend, axis=0, keepdims=True)
            dscores = (attend * (dattend - delta)).astype(jnp.bfloat16)
            score_ref[head] = dscores
            key_grad += jnp.dot(dscores, query_ref[:, at], preferred_element_type=jnp.float32)
        scaled = key_grad * FACTOR * gain_ref[:, at]
        scaled_ref[:, at] = scaled
        inner_ref[...] += scaled * raw_ref[:, at].astype(jnp.float32)


def query_kernel(parts, keys_ref, *refs):
    for head in range(keys_ref.shape[1] // HD):
        at = slice(head * HD, (head + 1) * HD)
        for score_ref, out_ref in zip(refs[:parts], refs[parts:]):
            out = lax.dot_general(
                score_ref[head], keys_ref[:, at], COLUMNS, preferred_element_type=jnp.float32
            )
            out_ref[:, at] = (out * FACTOR).astype(jnp.bfloat16)


def specs(tokens, heads):
    group = 2 - heads % 2
    width = group * HD
    head = pl.BlockSpec((LIVE, width), lambda h: (0, h))
    block = pl.BlockSpec((tokens, width), lambda h: (0, h))
    upper = pl.BlockSpec((None, tokens, width), lambda h: (0, 0, h))
    lower = pl.BlockSpec((None, tokens, width), lambda h: (1, 0, h))
    weights = pl.BlockSpec((group, LIVE, tokens), lambda h: (h, 0, 0))
    gain = pl.BlockSpec((1, width), lambda h: (0, h))
    return heads // group, head, block, upper, lower, weights, gain


def attend_call(length, raw, inv, gain, moved, tokens):
    parts = len(moved)
    cols = moved[0].shape[2]
    heads = cols // HD
    steps, head, block, upper, lower, weights, gains = specs(tokens, heads)
    outs = pl.pallas_call(
        functools.partial(attend_kernel, parts),
        grid=(steps,),
        in_specs=[
            pl.BlockSpec(memory_space=pltpu.SMEM),
            head,
            pl.BlockSpec((LIVE, 1), lambda h: (0, 0)),
            gains,
        ]
        + [upper] * parts
        + [lower] * parts,
        out_specs=[weights] * parts + [head, head],
        out_shape=[jax.ShapeDtypeStruct((heads, LIVE, tokens), jnp.float32)] * parts
        + [jax.ShapeDtypeStruct((LIVE, cols), jnp.bfloat16)] * 2,
        compiler_params=pltpu.CompilerParams(vmem_limit_bytes=VMEM),
        cost_estimate=pl.CostEstimate(
            flops=16 * parts * tokens * cols * LIVE,
            bytes_accessed=16 * parts * tokens * cols,
            transcendentals=0,
        ),
    )(length, raw, inv, gain, *moved, *moved)
    return outs[:parts], outs[parts], outs[parts + 1]


def gradient_call(raw, values, gain, moved, attends, tokens):
    parts = len(moved)
    cols = moved[0].shape[2]
    heads = cols // HD
    steps, head, block, upper, lower, weights, gains = specs(tokens, heads)
    outs = pl.pallas_call(
        functools.partial(gradient_kernel, parts),
        grid=(steps,),
        in_specs=[head, head, gains] + [upper] * parts + [lower] * parts + [weights] * parts,
        out_specs=[weights] * parts + [head, pl.BlockSpec((LIVE, HD), lambda h: (0, 0))],
        out_shape=[jax.ShapeDtypeStruct((heads, LIVE, tokens), jnp.bfloat16)] * parts
        + [
            jax.ShapeDtypeStruct((LIVE, cols), jnp.float32),
            jax.ShapeDtypeStruct((LIVE, HD), jnp.float32),
        ],
        compiler_params=pltpu.CompilerParams(vmem_limit_bytes=VMEM),
        cost_estimate=pl.CostEstimate(
            flops=16 * parts * tokens * cols * LIVE,
            bytes_accessed=16 * parts * tokens * cols,
            transcendentals=0,
        ),
    )(raw, values, gain, *moved, *moved, *attends)
    return outs[:parts], outs[parts], outs[parts + 1]


def query_call(keys, scores):
    parts = len(scores)
    heads, _, tokens = scores[0].shape
    steps, head, block, _, _, weights, _ = specs(tokens, heads)
    return pl.pallas_call(
        functools.partial(query_kernel, parts),
        grid=(steps,),
        in_specs=[head] + [weights] * parts,
        out_specs=[block] * parts,
        out_shape=[jax.ShapeDtypeStruct((tokens, keys.shape[1]), jnp.bfloat16)] * parts,
        compiler_params=pltpu.CompilerParams(vmem_limit_bytes=VMEM),
        cost_estimate=pl.CostEstimate(
            flops=8 * parts * tokens * keys.shape[1] * LIVE,
            bytes_accessed=8 * parts * tokens * keys.shape[1],
            transcendentals=0,
        ),
    )(keys, *scores)


def rows_spec(part, width, tiled=False):
    _, count, index = part
    if tiled:
        return pl.BlockSpec((count, width), lambda n: (index, n))
    return pl.BlockSpec((count, width), lambda n: (index, 0))


def pick_kernel(place_ref, first_ref, mine_ref, sibling_first_ref, sibling_ref, *out_refs):
    here = place_ref[0] == 0
    rows = out_refs[0].shape[1]
    for index, out_ref in enumerate(out_refs):
        at = pl.ds(pl.multiple_of(place_ref[2 + index] * rows, rows), rows)
        out_ref[:LIVE] = jnp.where(here, first_ref[:, at], sibling_first_ref[:, at])
        out_ref[LIVE:] = jnp.where(here, mine_ref[:, at], sibling_ref[:, at])


def pick_call(place, first, mine, sibling_first, sibling, rows):
    arrays = (first, mine, sibling_first, sibling)
    shape = (LIVE + mine.shape[0], rows)
    return pl.pallas_call(
        pick_kernel,
        grid=(1,),
        in_specs=[pl.BlockSpec(memory_space=pltpu.SMEM)]
        + [pl.BlockSpec(x.shape, lambda n: (0, 0)) for x in arrays],
        out_specs=[pl.BlockSpec(shape, lambda n: (0, 0))] * 2,
        out_shape=[jax.ShapeDtypeStruct(shape, jnp.bfloat16)] * 2,
        compiler_params=pltpu.CompilerParams(vmem_limit_bytes=VMEM),
        cost_estimate=pl.CostEstimate(flops=1000, bytes_accessed=1000, transcendentals=0),
    )(place, *arrays)


def product_kernel(videos, place_ref, *refs):
    mine_refs, sibling_refs = refs[:videos], refs[videos : 2 * videos]
    weight_refs, out_ref = refs[2 * videos : -1], refs[-1]
    rows = weight_refs[0].shape[0]
    total = None
    for step, weight_ref in enumerate(weight_refs):
        here = place_ref[step // 2] == 0
        at = pl.ds(pl.multiple_of(place_ref[2 + step % 2] * rows, rows), rows)
        block = jnp.concatenate(
            [jnp.where(here, m[:, at], s[:, at]) for m, s in zip(mine_refs, sibling_refs)], axis=0
        )
        term = jnp.dot(block, weight_ref[...], preferred_element_type=jnp.float32)
        total = term if total is None else total + term
    out_ref[...] = total


def product_call(place, mine, sibling, weights):
    videos = len(mine)
    width = weights[0][0].shape[1]
    parts = [*mine, *sibling, *weights]
    return pl.pallas_call(
        functools.partial(product_kernel, videos),
        grid=(1,),
        in_specs=[pl.BlockSpec(memory_space=pltpu.SMEM)]
        + [rows_spec(part, part[0].shape[1]) for part in parts],
        out_specs=pl.BlockSpec((videos * LIVE, width), lambda n: (0, 0)),
        out_shape=jax.ShapeDtypeStruct((videos * LIVE, width), jnp.float32),
        compiler_params=pltpu.CompilerParams(vmem_limit_bytes=VMEM),
        cost_estimate=pl.CostEstimate(flops=1000, bytes_accessed=1000, transcendentals=0),
    )(place, *[part[0] for part in parts])


def weights_kernel(columns_ref, *refs):
    parts = [ref[...] for ref in refs[:-1]]
    refs[-1][...] = jnp.dot(
        columns_ref[...], jnp.concatenate(parts, axis=0), preferred_element_type=jnp.float32
    )


def weights_call(columns, parts):
    rows, depth = columns.shape
    cols = parts[0][0].shape[1]
    tile = min(cols, 1024)
    return pl.pallas_call(
        weights_kernel,
        grid=(cols // tile,),
        in_specs=[pl.BlockSpec(columns.shape, lambda n: (0, 0))]
        + [rows_spec(part, tile, True) for part in parts],
        out_specs=pl.BlockSpec((rows, tile), lambda n: (0, n)),
        out_shape=jax.ShapeDtypeStruct((rows, cols), jnp.float32),
        compiler_params=pltpu.CompilerParams(vmem_limit_bytes=VMEM),
        cost_estimate=pl.CostEstimate(
            flops=2 * rows * cols * depth,
            bytes_accessed=4 * rows * cols + 2 * depth * (rows + cols),
            transcendentals=0,
        ),
    )(columns, *[part[0] for part in parts])


def after(x, *others):
    return lax.optimization_barrier((x, *others))[0]


def blocks_kernel(lanes_ref, query_ref, grad_ref, *out_refs):
    cols = out_refs[0].shape[2]
    for index, out_ref in enumerate(out_refs):
        at = pl.ds(pl.multiple_of(lanes_ref[index] * cols, cols), cols)
        out_ref[0] = query_ref[:, at]
        out_ref[1] = grad_ref[:, at]


def blocks_call(lanes, query, grad):
    parts = lanes.shape[0]
    tokens, hid = query.shape
    cols, tiles = hid // parts, 4
    rows = tokens // tiles
    return pl.pallas_call(
        blocks_kernel,
        grid=(tiles,),
        in_specs=[pl.BlockSpec(memory_space=pltpu.SMEM)]
        + [pl.BlockSpec((rows, hid), lambda n: (n, 0))] * 2,
        out_specs=[pl.BlockSpec((2, rows, cols), lambda n: (0, n, 0))] * parts,
        out_shape=[jax.ShapeDtypeStruct((2, tokens, cols), jnp.bfloat16)] * parts,
        compiler_params=pltpu.CompilerParams(vmem_limit_bytes=VMEM),
        cost_estimate=pl.CostEstimate(
            flops=1000, bytes_accessed=8 * tokens * hid, transcendentals=0
        ),
    )(lanes, query, grad)


def pack_kernel(moves, inputs, place_ref, *refs):
    ins, outs = refs[:inputs], refs[inputs:]

    def span(at, width):
        if isinstance(at, int):
            return pl.ds(at, width)
        return pl.ds(pl.multiple_of(place_ref[at[0]] * width, width), width)

    for source, row, col, count, width, target, to_row, to_col in moves:
        block = ins[source][pl.ds(row, count), span(col, width)]
        outs[target][pl.ds(to_row, count), span(to_col, width)] = block


def pack_call(place, arrays, shapes, moves, tiles=1, size=1000):
    def spec(shape):
        return pl.BlockSpec((shape[0] // tiles, shape[1]), lambda n: (n, 0))

    return pl.pallas_call(
        functools.partial(pack_kernel, moves, len(arrays)),
        grid=(tiles,),
        in_specs=[pl.BlockSpec(memory_space=pltpu.SMEM)] + [spec(x.shape) for x in arrays],
        out_specs=[spec(shape) for shape in shapes],
        out_shape=[jax.ShapeDtypeStruct(shape, jnp.bfloat16) for shape in shapes],
        compiler_params=pltpu.CompilerParams(vmem_limit_bytes=VMEM),
        cost_estimate=pl.CostEstimate(flops=1000, bytes_accessed=size, transcendentals=0),
    )(place, *arrays)


def shards(n_dp, n_seq, query, caption, key_weight, value_weight, key_gain, lengths, out_grad):
    rows, cols = key_weight.shape
    hid = cols * n_seq
    lines = n_dp // 2
    half = cols // 2
    wide = 2 * rows
    tokens = query.shape[1]
    me = lax.axis_index("dp")
    lane = lax.axis_index("seq")
    line, side = me // 2, me % 2
    top = lines // 2
    low, base = line // top, line % top
    core = lane % 2

    def over_dp(x, step):
        return lax.ppermute(x, "dp", [(a, a ^ step) for a in range(n_dp)])

    def over_seq(x, step):
        return lax.ppermute(x, "seq", [(a, a ^ step) for a in range(n_seq)])

    def col_block(x, index, width):
        return lax.dynamic_slice(x, (0, index * width), (x.shape[0], width))

    pieces = wide // half
    scalars = [low, 1 - low, base + core * top, base + (1 - core) * top]
    scalars += [(line ^ s) % top + core * top for s in range(1, lines) if s != top]
    scalars += [(base + core * top) * pieces + p for p in range(pieces)]
    place = jnp.stack(scalars).astype(jnp.int32)
    near_at = lines + 2
    near_given, kept, value_given, mine_first, sibling_first, *given = pack_call(
        place,
        [key_weight, value_weight, caption[0]],
        [(rows + pieces * LIVE, half), (2 * rows, half), (rows, half)] + [(LIVE, wide)] * lines,
        [
            (0, 0, (1,), rows, half, 0, 0, 0),
            (0, 0, (0,), rows, half, 1, 0, 0),
            (1, 0, (0,), rows, half, 1, rows, 0),
            (1, 0, (1,), rows, half, 2, 0, 0),
        ]
        + [(2, 0, (near_at + p,), LIVE, half, 0, rows + p * LIVE, 0) for p in range(pieces)]
        + [(2, 0, (2 + s,), LIVE, wide, 3 + s, 0, 0) for s in range(lines)],
    )
    near = over_dp(near_given, 2 * top)
    beside = over_dp(kept, 1)
    direct = [s for s in range(1, lines) if s != top]
    arrived = [over_dp(x, 2 * s) for s, x in zip(direct, given)]

    lanes = jnp.stack([lane ^ s for s in range(n_seq)]).astype(jnp.int32)
    packed = blocks_call(after(lanes, kept), query[0], out_grad[0])
    moved = [packed[0]] + [None] * (n_seq - 1)
    previous = ()
    for s in range(2, n_seq):
        moved[s] = over_seq(after(packed[s], *previous), s)
        previous = (moved[s],)
    previous = moved[2 : n_seq // 2 + 1]
    moved[1] = over_seq(after(packed[1], beside), 1)

    key_near, shared, shared_given = pack_call(
        place,
        [near, *arrived],
        [(rows, half)] + [((lines - 1) * LIVE, wide)] * 2,
        [(0, 0, 0, rows, half, 0, 0, 0)]
        + [
            (0, rows + p * LIVE, 0, LIVE, half, out, (top - 1) * LIVE, p * half)
            for p in range(pieces)
            for out in (1, 2)
        ]
        + [
            (at, 0, 0, LIVE, wide, out, (s - 1) * LIVE, 0)
            for at, s in enumerate(direct, 1)
            for out in (1, 2)
        ],
    )
    key_far = over_dp(key_near, 1)
    value_near = over_dp(after(value_given, near, *arrived), 2 * top)
    value_far = over_dp(value_near, 1)
    sibling = over_seq(shared_given, 1)
    key_quad = ((kept, rows, 0), (beside, rows, 0), (key_near, rows, 0), (key_far, rows, 0))
    value_quad = ((kept, rows, 1), (beside, rows, 1), (value_near, rows, 0), (value_far, rows, 0))

    places = jnp.stack([core ^ low, 1 - (core ^ low), side, 1 - side]).astype(jnp.int32)

    bits = lines.bit_length() - 1
    kept_videos = sorted(range(0, lines, 2), key=lambda s: [s >> k & 1 for k in range(1, bits)])

    def product(places, weights, other):
        chosen = [s | 1 for s in kept_videos] if other else kept_videos
        return product_call(
            places,
            [(shared, LIVE, s - 1) if s else (mine_first, LIVE, 0) for s in chosen],
            [(sibling, LIVE, s - 1) if s else (sibling_first, LIVE, 0) for s in chosen],
            weights,
        )

    def reduced(total):
        step = 4
        while step < 2 * top:
            count = total.shape[0] // 2
            total = total[:count] + over_dp(total[count:], step)
            step *= 2
        return lax.reduce_precision(total, 8, 7).astype(jnp.bfloat16)

    def joined(own, other):
        return jnp.where(
            low == 0,
            jnp.concatenate([own, other], axis=1),
            jnp.concatenate([other, own], axis=1),
        )

    def seq_sum(x):
        for step in steps:
            x = x + over_seq(x, step)
        return x

    steps = [1 << k for k in reversed(range(n_seq.bit_length() - 1))]
    gain = lax.dynamic_slice(key_gain, (lane * cols,), (cols,)).reshape(1, cols)
    own_columns, other_given = pick_call(after(places, *previous[:1]), mine_first, shared, sibling_first, sibling, rows)
    key_product = product(after(places, own_columns), key_quad, True)
    key_sent = over_dp(key_product, 2)
    later = after(places, key_product)
    other_columns = over_dp(after(other_given, key_product), 1)
    columns = jnp.concatenate([own_columns, other_columns], axis=0).T
    value_product = product(later, value_quad, True)
    value_rest_product = product(later, value_quad, False)
    key_sent = after(key_sent, value_product, value_rest_product, columns, gain)
    value_sent = over_dp(after(value_product, key_sent), 2)
    key_total = reduced(product(later, key_quad, False) + key_sent)
    raw = joined(key_total[:LIVE], over_dp(key_total[LIVE:], 2 * top))
    raw_wide = raw.astype(jnp.float32)
    squares = seq_sum(jnp.sum(raw_wide * raw_wide, axis=-1, keepdims=True))
    inv_rms = lax.rsqrt(squares / hid + 1e-06)
    value_total = reduced(value_rest_product + after(value_sent, inv_rms))
    value_own, value_sent = value_total[:LIVE], value_total[LIVE:]
    value_other = over_dp(value_sent, 2 * top)
    attends, keys, value_grad = attend_call(
        lengths, after(raw, columns, value_own, value_sent), inv_rms, gain, moved, tokens
    )

    values = joined(value_own, after(value_other, value_grad))

    value_near_parts = [over_dp(value_grad, 2 * s) for s in range(1, lines)]
    scores, scaled, inner = gradient_call(raw, values, gain, moved, attends, tokens)
    outs = query_call(keys, scores)
    inner = jnp.sum(inner, axis=-1, keepdims=True)
    for step in steps[:-1]:
        inner = inner + over_seq(inner, step)
    far_sum = after(inner, value_near_parts[-1])
    inner_mean = (far_sum + over_seq(far_sum, 1)) / hid
    raw_grad = (inv_rms * scaled - raw_wide * inv_rms**3 * inner_mean).astype(jnp.bfloat16)
    value_parts = lax.optimization_barrier((value_grad, *value_near_parts, inner))[:-1]
    value_rest = over_dp(jnp.concatenate(value_parts, axis=0), 1)
    raw_grad = after(raw_grad, *value_near_parts)
    key_near_parts = [over_dp(raw_grad, 2 * s) for s in range(1, lines)]
    placed = [outs[0]] + [None] * (n_seq - 1)
    previous = (inner,)
    for s in range(2, n_seq):
        placed[s] = over_seq(after(outs[s], *previous), s)
        previous = (placed[s], key_near_parts[-1])
    placed[1] = over_seq(after(outs[1], value_rest), 1)
    key_first = over_dp(raw_grad, 1)
    key_rest = over_dp(after(jnp.concatenate(key_near_parts, axis=0), key_first), 1)
    key_parts = (
        [(x, LIVE, 0) for x in (raw_grad, *key_near_parts)]
        + [(key_first, LIVE, 0)]
        + [(key_rest, LIVE, s) for s in range(lines - 1)]
    )
    value_parts = (
        [(x, LIVE, 0) for x in (value_grad, *value_near_parts)]
        + [(value_rest, LIVE, s) for s in range(lines)]
    )
    value_weight_grad = weights_call(after(columns, key_first), value_parts)
    (query_grad,) = pack_call(
        lanes,
        placed,
        [(tokens, hid)],
        [(s, 0, 0, tokens // 2, cols, 0, 0, (s,)) for s in range(n_seq)],
        2,
    )
    key_weight_grad = weights_call(after(columns, query_grad), key_parts)
    return query_grad[None], key_weight_grad, value_weight_grad


def solution(mesh):
    placed = (
        P("dp", "seq", None),
        P("dp", None, None),
        P("dp", "seq"),
        P("dp", "seq"),
        P(),
        P("dp"),
        P("dp", "seq", None),
    )
    return jax.shard_map(
        functools.partial(shards, mesh.shape["dp"], mesh.shape["seq"]),
        mesh=mesh,
        in_specs=placed,
        out_specs=(P("dp", "seq", None), P("dp", "seq"), P("dp", "seq")),
        check_vma=False,
    )
```

```python
import functools

import jax
import jax.numpy as jnp
from jax import lax
from jax.experimental import pallas as pl
from jax.experimental.pallas import tpu as pltpu
from jax.sharding import PartitionSpec as P

HD = 128
LIVE = 128
VMEM = 60 * 1024 * 1024


ROWS = (((1,), (1,)), ((), ()))
COLUMNS = (((0,), (0,)), ((), ()))
FACTOR = HD ** (-0.5)


def attend_kernel(parts, length_ref, raw_ref, inv_ref, gain_ref, *refs):
    query_refs, grad_refs = refs[:parts], refs[parts : 2 * parts]
    attend_refs = refs[2 * parts : 3 * parts]
    keys_ref, value_grad_ref = refs[3 * parts :]
    keys = (raw_ref[...].astype(jnp.float32) * inv_ref[...] * gain_ref[...]).astype(jnp.bfloat16)
    keys_ref[...] = keys
    valid = lax.broadcasted_iota(jnp.int32, (LIVE, 1), 0) < length_ref[0]
    for head in range(keys.shape[1] // HD):
        at = slice(head * HD, (head + 1) * HD)
        value_grad = jnp.zeros((LIVE, HD), jnp.float32)
        for query_ref, grad_ref, attend_ref in zip(query_refs, grad_refs, attend_refs):
            scores = lax.dot_general(
                keys[:, at], query_ref[:, at], ROWS, preferred_element_type=jnp.float32
            )
            scores = jnp.where(valid, scores * FACTOR, -jnp.inf)
            powers = jnp.exp(scores - jnp.max(scores, axis=0, keepdims=True))
            attend = powers * (1.0 / jnp.sum(powers, axis=0, keepdims=True))
            attend_ref[head] = attend
            value_grad += jnp.dot(
                attend.astype(jnp.bfloat16), grad_ref[:, at], preferred_element_type=jnp.float32
            )
        value_grad_ref[:, at] = value_grad.astype(jnp.bfloat16)


def gradient_kernel(parts, raw_ref, value_ref, gain_ref, *refs):
    query_refs, grad_refs = refs[:parts], refs[parts : 2 * parts]
    attend_refs, score_refs = refs[2 * parts : 3 * parts], refs[3 * parts : 4 * parts]
    scaled_ref, inner_ref = refs[4 * parts :]

    @pl.when(pl.program_id(0) == 0)
    def _():
        inner_ref[...] = jnp.zeros_like(inner_ref)

    for head in range(value_ref.shape[1] // HD):
        at = slice(head * HD, (head + 1) * HD)
        key_grad = jnp.zeros((LIVE, HD), jnp.float32)
        for query_ref, grad_ref, attend_ref, score_ref in zip(
            query_refs, grad_refs, attend_refs, score_refs
        ):
            attend = attend_ref[head]
            dattend = lax.dot_general(
                value_ref[:, at], grad_ref[:, at], ROWS, preferred_element_type=jnp.float32
            )
            delta = jnp.sum(attend * dattend, axis=0, keepdims=True)
            dscores = (attend * (dattend - delta)).astype(jnp.bfloat16)
            score_ref[head] = dscores
            key_grad += jnp.dot(dscores, query_ref[:, at], preferred_element_type=jnp.float32)
        scaled = key_grad * FACTOR * gain_ref[:, at]
        scaled_ref[:, at] = scaled
        inner_ref[...] += scaled * raw_ref[:, at].astype(jnp.float32)


def query_kernel(parts, keys_ref, *refs):
    for head in range(keys_ref.shape[1] // HD):
        at = slice(head * HD, (head + 1) * HD)
        for score_ref, out_ref in zip(refs[:parts], refs[parts:]):
            out = lax.dot_general(
                score_ref[head], keys_ref[:, at], COLUMNS, preferred_element_type=jnp.float32
            )
            out_ref[:, at] = (out * FACTOR).astype(jnp.bfloat16)


def specs(tokens, heads):
    group = next(g for g in (4, 2, 1) if heads % g == 0)
    width = group * HD
    head = pl.BlockSpec((LIVE, width), lambda h: (0, h))
    block = pl.BlockSpec((tokens, width), lambda h: (0, h))
    upper = pl.BlockSpec((None, tokens, width), lambda h: (0, 0, h))
    lower = pl.BlockSpec((None, tokens, width), lambda h: (1, 0, h))
    weights = pl.BlockSpec((group, LIVE, tokens), lambda h: (h, 0, 0))
    gain = pl.BlockSpec((1, width), lambda h: (0, h))
    return heads // group, head, block, upper, lower, weights, gain


def attend_call(length, raw, inv, gain, moved, tokens):
    parts = len(moved)
    cols = moved[0].shape[2]
    heads = cols // HD
    steps, head, block, upper, lower, weights, gains = specs(tokens, heads)
    outs = pl.pallas_call(
        functools.partial(attend_kernel, parts),
        grid=(steps,),
        in_specs=[
            pl.BlockSpec(memory_space=pltpu.SMEM),
            head,
            pl.BlockSpec((LIVE, 1), lambda h: (0, 0)),
            gains,
        ]
        + [upper] * parts
        + [lower] * parts,
        out_specs=[weights] * parts + [head, head],
        out_shape=[jax.ShapeDtypeStruct((heads, LIVE, tokens), jnp.float32)] * parts
        + [jax.ShapeDtypeStruct((LIVE, cols), jnp.bfloat16)] * 2,
        compiler_params=pltpu.CompilerParams(vmem_limit_bytes=VMEM),
        cost_estimate=pl.CostEstimate(
            flops=16 * parts * tokens * cols * LIVE,
            bytes_accessed=16 * parts * tokens * cols,
            transcendentals=0,
        ),
    )(length, raw, inv, gain, *moved, *moved)
    return outs[:parts], outs[parts], outs[parts + 1]


def gradient_call(raw, values, gain, moved, attends, tokens):
    parts = len(moved)
    cols = moved[0].shape[2]
    heads = cols // HD
    steps, head, block, upper, lower, weights, gains = specs(tokens, heads)
    outs = pl.pallas_call(
        functools.partial(gradient_kernel, parts),
        grid=(steps,),
        in_specs=[head, head, gains] + [upper] * parts + [lower] * parts + [weights] * parts,
        out_specs=[weights] * parts + [head, pl.BlockSpec((LIVE, HD), lambda h: (0, 0))],
        out_shape=[jax.ShapeDtypeStruct((heads, LIVE, tokens), jnp.bfloat16)] * parts
        + [
            jax.ShapeDtypeStruct((LIVE, cols), jnp.float32),
            jax.ShapeDtypeStruct((LIVE, HD), jnp.float32),
        ],
        compiler_params=pltpu.CompilerParams(vmem_limit_bytes=VMEM),
        cost_estimate=pl.CostEstimate(
            flops=16 * parts * tokens * cols * LIVE,
            bytes_accessed=16 * parts * tokens * cols,
            transcendentals=0,
        ),
    )(raw, values, gain, *moved, *moved, *attends)
    return outs[:parts], outs[parts], outs[parts + 1]


def query_call(keys, scores):
    parts = len(scores)
    heads, _, tokens = scores[0].shape
    steps, head, block, _, _, weights, _ = specs(tokens, heads)
    return pl.pallas_call(
        functools.partial(query_kernel, parts),
        grid=(steps,),
        in_specs=[head] + [weights] * parts,
        out_specs=[block] * parts,
        out_shape=[jax.ShapeDtypeStruct((tokens, keys.shape[1]), jnp.bfloat16)] * parts,
        compiler_params=pltpu.CompilerParams(vmem_limit_bytes=VMEM),
        cost_estimate=pl.CostEstimate(
            flops=8 * parts * tokens * keys.shape[1] * LIVE,
            bytes_accessed=8 * parts * tokens * keys.shape[1],
            transcendentals=0,
        ),
    )(keys, *scores)


def rows_spec(part, width, tiled=False):
    _, count, index = part
    if tiled:
        return pl.BlockSpec((count, width), lambda n: (index, n))
    return pl.BlockSpec((count, width), lambda n: (index, 0))


def pick_kernel(place_ref, first_ref, mine_ref, sibling_first_ref, sibling_ref, *out_refs):
    here = place_ref[0] == 0
    rows = out_refs[0].shape[1]
    for index, out_ref in enumerate(out_refs):
        at = pl.ds(pl.multiple_of(place_ref[2 + index] * rows, rows), rows)
        out_ref[:LIVE] = jnp.where(here, first_ref[:, at], sibling_first_ref[:, at])
        out_ref[LIVE:] = jnp.where(here, mine_ref[:, at], sibling_ref[:, at])


def pick_call(place, first, mine, sibling_first, sibling, rows):
    arrays = (first, mine, sibling_first, sibling)
    shape = (LIVE + mine.shape[0], rows)
    return pl.pallas_call(
        pick_kernel,
        grid=(1,),
        in_specs=[pl.BlockSpec(memory_space=pltpu.SMEM)]
        + [pl.BlockSpec(x.shape, lambda n: (0, 0)) for x in arrays],
        out_specs=[pl.BlockSpec(shape, lambda n: (0, 0))] * 2,
        out_shape=[jax.ShapeDtypeStruct(shape, jnp.bfloat16)] * 2,
        compiler_params=pltpu.CompilerParams(vmem_limit_bytes=VMEM),
        cost_estimate=pl.CostEstimate(flops=1000, bytes_accessed=1000, transcendentals=0),
    )(place, *arrays)


def product_kernel(videos, place_ref, *refs):
    mine_refs, sibling_refs = refs[:videos], refs[videos : 2 * videos]
    weight_refs, out_ref = refs[2 * videos : -1], refs[-1]
    rows = weight_refs[0].shape[0]
    total = None
    for step, weight_ref in enumerate(weight_refs):
        here = place_ref[step // 2] == 0
        at = pl.ds(pl.multiple_of(place_ref[2 + step % 2] * rows, rows), rows)
        block = jnp.concatenate(
            [jnp.where(here, m[:, at], s[:, at]) for m, s in zip(mine_refs, sibling_refs)], axis=0
        )
        term = jnp.dot(block, weight_ref[...], preferred_element_type=jnp.float32)
        total = term if total is None else total + term
    out_ref[...] = total


def product_call(place, mine, sibling, weights):
    videos = len(mine)
    width = weights[0][0].shape[1]
    parts = [*mine, *sibling, *weights]
    return pl.pallas_call(
        functools.partial(product_kernel, videos),
        grid=(1,),
        in_specs=[pl.BlockSpec(memory_space=pltpu.SMEM)]
        + [rows_spec(part, part[0].shape[1]) for part in parts],
        out_specs=pl.BlockSpec((videos * LIVE, width), lambda n: (0, 0)),
        out_shape=jax.ShapeDtypeStruct((videos * LIVE, width), jnp.float32),
        compiler_params=pltpu.CompilerParams(vmem_limit_bytes=VMEM),
        cost_estimate=pl.CostEstimate(flops=1000, bytes_accessed=1000, transcendentals=0),
    )(place, *[part[0] for part in parts])


def weights_kernel(columns_ref, *refs):
    parts = [ref[...] for ref in refs[:-1]]
    refs[-1][...] = jnp.dot(
        columns_ref[...], jnp.concatenate(parts, axis=0), preferred_element_type=jnp.float32
    )


def weights_call(columns, parts):
    rows, depth = columns.shape
    cols = parts[0][0].shape[1]
    tile = min(cols, 1024)
    return pl.pallas_call(
        weights_kernel,
        grid=(cols // tile,),
        in_specs=[pl.BlockSpec(columns.shape, lambda n: (0, 0))]
        + [rows_spec(part, tile, True) for part in parts],
        out_specs=pl.BlockSpec((rows, tile), lambda n: (0, n)),
        out_shape=jax.ShapeDtypeStruct((rows, cols), jnp.float32),
        compiler_params=pltpu.CompilerParams(vmem_limit_bytes=VMEM),
        cost_estimate=pl.CostEstimate(
            flops=2 * rows * cols * depth,
            bytes_accessed=4 * rows * cols + 2 * depth * (rows + cols),
            transcendentals=0,
        ),
    )(columns, *[part[0] for part in parts])


def after(x, *others):
    return lax.optimization_barrier((x, *others))[0]


def blocks_kernel(lanes_ref, query_ref, grad_ref, *out_refs):
    cols = out_refs[0].shape[2]
    for index, out_ref in enumerate(out_refs):
        at = pl.ds(pl.multiple_of(lanes_ref[index] * cols, cols), cols)
        out_ref[0] = query_ref[:, at]
        out_ref[1] = grad_ref[:, at]


def blocks_call(lanes, query, grad):
    parts = lanes.shape[0]
    tokens, hid = query.shape
    cols, tiles = hid // parts, 4
    rows = tokens // tiles
    return pl.pallas_call(
        blocks_kernel,
        grid=(tiles,),
        in_specs=[pl.BlockSpec(memory_space=pltpu.SMEM)]
        + [pl.BlockSpec((rows, hid), lambda n: (n, 0))] * 2,
        out_specs=[pl.BlockSpec((2, rows, cols), lambda n: (0, n, 0))] * parts,
        out_shape=[jax.ShapeDtypeStruct((2, tokens, cols), jnp.bfloat16)] * parts,
        compiler_params=pltpu.CompilerParams(vmem_limit_bytes=VMEM),
        cost_estimate=pl.CostEstimate(
            flops=1000, bytes_accessed=8 * tokens * hid, transcendentals=0
        ),
    )(lanes, query, grad)


def pack_kernel(moves, inputs, place_ref, *refs):
    ins, outs = refs[:inputs], refs[inputs:]

    def span(at, width):
        if isinstance(at, int):
            return pl.ds(at, width)
        return pl.ds(pl.multiple_of(place_ref[at[0]] * width, width), width)

    for source, row, col, count, width, target, to_row, to_col in moves:
        block = ins[source][pl.ds(row, count), span(col, width)]
        outs[target][pl.ds(to_row, count), span(to_col, width)] = block


def pack_call(place, arrays, shapes, moves, tiles=1, size=1000):
    def spec(shape):
        return pl.BlockSpec((shape[0] // tiles, shape[1]), lambda n: (n, 0))

    return pl.pallas_call(
        functools.partial(pack_kernel, moves, len(arrays)),
        grid=(tiles,),
        in_specs=[pl.BlockSpec(memory_space=pltpu.SMEM)] + [spec(x.shape) for x in arrays],
        out_specs=[spec(shape) for shape in shapes],
        out_shape=[jax.ShapeDtypeStruct(shape, jnp.bfloat16) for shape in shapes],
        compiler_params=pltpu.CompilerParams(vmem_limit_bytes=VMEM),
        cost_estimate=pl.CostEstimate(flops=1000, bytes_accessed=size, transcendentals=0),
    )(place, *arrays)


def shards(n_dp, n_seq, query, caption, key_weight, value_weight, key_gain, lengths, out_grad):
    rows, cols = key_weight.shape
    hid = cols * n_seq
    lines = n_dp // 2
    half = cols // 2
    wide = 2 * rows
    tokens = query.shape[1]
    me = lax.axis_index("dp")
    lane = lax.axis_index("seq")
    line, side = me // 2, me % 2
    top = lines // 2
    low, base = line // top, line % top
    core = lane % 2

    def over_dp(x, step):
        return lax.ppermute(x, "dp", [(a, a ^ step) for a in range(n_dp)])

    def over_seq(x, step):
        return lax.ppermute(x, "seq", [(a, a ^ step) for a in range(n_seq)])

    def col_block(x, index, width):
        return lax.dynamic_slice(x, (0, index * width), (x.shape[0], width))

    pieces = wide // half
    scalars = [low, 1 - low, base + core * top, base + (1 - core) * top]
    scalars += [(line ^ s) % top + core * top for s in range(1, lines) if s != top]
    scalars += [(base + core * top) * pieces + p for p in range(pieces)]
    place = jnp.stack(scalars).astype(jnp.int32)
    near_at = lines + 2
    near_given, kept, value_given, mine_first, sibling_first, *given = pack_call(
        place,
        [key_weight, value_weight, caption[0]],
        [(rows + pieces * LIVE, half), (2 * rows, half), (rows, half)] + [(LIVE, wide)] * lines,
        [
            (0, 0, (1,), rows, half, 0, 0, 0),
            (0, 0, (0,), rows, half, 1, 0, 0),
            (1, 0, (0,), rows, half, 1, rows, 0),
            (1, 0, (1,), rows, half, 2, 0, 0),
        ]
        + [(2, 0, (near_at + p,), LIVE, half, 0, rows + p * LIVE, 0) for p in range(pieces)]
        + [(2, 0, (2 + s,), LIVE, wide, 3 + s, 0, 0) for s in range(lines)],
    )
    near = over_dp(near_given, 2 * top)
    beside = over_dp(kept, 1)
    direct = [s for s in range(1, lines) if s != top]
    arrived = [over_dp(x, 2 * s) for s, x in zip(direct, given)]

    lanes = jnp.stack([lane ^ s for s in range(n_seq)]).astype(jnp.int32)
    packed = blocks_call(after(lanes, kept), query[0], out_grad[0])
    moved = [packed[0]] + [None] * (n_seq - 1)
    previous = ()
    for s in range(2, n_seq):
        moved[s] = over_seq(after(packed[s], *previous), s)
        previous = (moved[s],)
    previous = moved[2 : n_seq // 2 + 1]
    moved[1] = over_seq(after(packed[1], beside), 1)

    key_near, shared, shared_given = pack_call(
        place,
        [near, *arrived],
        [(rows, half)] + [((lines - 1) * LIVE, wide)] * 2,
        [(0, 0, 0, rows, half, 0, 0, 0)]
        + [
            (0, rows + p * LIVE, 0, LIVE, half, out, (top - 1) * LIVE, p * half)
            for p in range(pieces)
            for out in (1, 2)
        ]
        + [
            (at, 0, 0, LIVE, wide, out, (s - 1) * LIVE, 0)
            for at, s in enumerate(direct, 1)
            for out in (1, 2)
        ],
    )
    key_far = over_dp(key_near, 1)
    value_near = over_dp(after(value_given, near, *arrived), 2 * top)
    sibling = over_seq(shared_given, 1)
    key_quad = ((kept, rows, 0), (beside, rows, 0), (key_near, rows, 0), (key_far, rows, 0))

    places = jnp.stack([core ^ low, 1 - (core ^ low), side, 1 - side]).astype(jnp.int32)

    bits = lines.bit_length() - 1
    kept_videos = sorted(range(0, lines, 2), key=lambda s: [s >> k & 1 for k in range(1, bits)])

    def product(places, weights, other):
        chosen = [s | 1 for s in kept_videos] if other else kept_videos
        return product_call(
            places,
            [(shared, LIVE, s - 1) if s else (mine_first, LIVE, 0) for s in chosen],
            [(sibling, LIVE, s - 1) if s else (sibling_first, LIVE, 0) for s in chosen],
            weights,
        )

    def reduced(total):
        step = 4
        while step < 2 * top:
            count = total.shape[0] // 2
            total = total[:count] + over_dp(total[count:], step)
            step *= 2
        return lax.reduce_precision(total, 8, 7).astype(jnp.bfloat16)

    def joined(own, other):
        return jnp.where(
            low == 0,
            jnp.concatenate([own, other], axis=1),
            jnp.concatenate([other, own], axis=1),
        )

    def seq_sum(x):
        for step in steps:
            x = x + over_seq(x, step)
        return x

    steps = [1 << k for k in reversed(range(n_seq.bit_length() - 1))]
    gain = lax.dynamic_slice(key_gain, (lane * cols,), (cols,)).reshape(1, cols)
    own_columns, other_given = pick_call(after(places, *previous[:1]), mine_first, shared, sibling_first, sibling, rows)
    key_product = product(after(places, own_columns), key_quad, True)
    key_sent = over_dp(key_product, 2)
    later = after(places, key_product)
    value_far = over_dp(after(value_near, key_product), 1)
    value_quad = ((kept, rows, 1), (beside, rows, 1), (value_near, rows, 0), (value_far, rows, 0))
    other_columns = over_dp(after(other_given, key_product), 1)
    columns = jnp.concatenate([own_columns, other_columns], axis=0).T
    value_product = product(later, value_quad, True)
    value_rest_product = product(later, value_quad, False)
    key_sent = after(key_sent, columns, gain)
    value_sent = over_dp(after(value_product, key_sent), 2)
    key_total = reduced(product(later, key_quad, False) + key_sent)
    raw = joined(key_total[:LIVE], over_dp(key_total[LIVE:], 2 * top))
    raw_wide = raw.astype(jnp.float32)
    squares = seq_sum(jnp.sum(raw_wide * raw_wide, axis=-1, keepdims=True))
    inv_rms = lax.rsqrt(squares / hid + 1e-06)
    attends, keys, value_grad = attend_call(
        lengths, after(raw, columns, value_rest_product), inv_rms, gain, moved, tokens
    )
    value_total = reduced(value_rest_product + after(value_sent, value_grad))
    values = joined(value_total[:LIVE], over_dp(value_total[LIVE:], 2 * top))

    value_given = after(value_grad, values)
    value_near_parts = [over_dp(value_given, 2 * s) for s in range(1, lines)]
    scores, scaled, inner = gradient_call(raw, values, gain, moved, attends, tokens)
    outs = query_call(keys, scores)
    inner = jnp.sum(inner, axis=-1, keepdims=True)
    for step in steps[:-1]:
        inner = inner + over_seq(inner, step)
    far_sum = after(inner, *value_near_parts)
    inner_mean = (far_sum + over_seq(far_sum, 1)) / hid
    raw_grad = (inv_rms * scaled - raw_wide * inv_rms**3 * inner_mean).astype(jnp.bfloat16)
    value_parts = lax.optimization_barrier((value_grad, *value_near_parts, inner, outs[0]))[:-2]
    value_rest = over_dp(jnp.concatenate(value_parts, axis=0), 1)
    key_near_parts = [over_dp(raw_grad, 2 * s) for s in range(1, lines)]
    placed = [outs[0]] + [None] * (n_seq - 1)
    previous = (inner,)
    for s in range(2, n_seq):
        placed[s] = over_seq(after(outs[s], *previous), s)
        previous = (placed[s], key_near_parts[-1])
    placed[1] = over_seq(after(outs[1], value_rest), 1)
    key_first = over_dp(raw_grad, 1)
    key_rest = over_dp(after(jnp.concatenate(key_near_parts, axis=0), key_first), 1)
    key_parts = (
        [(x, LIVE, 0) for x in (raw_grad, *key_near_parts)]
        + [(key_first, LIVE, 0)]
        + [(key_rest, LIVE, s) for s in range(lines - 1)]
    )
    value_parts = (
        [(x, LIVE, 0) for x in (value_grad, *value_near_parts)]
        + [(value_rest, LIVE, s) for s in range(lines)]
    )
    value_weight_grad = weights_call(after(columns, key_first), value_parts)
    (query_grad,) = pack_call(
        lanes,
        placed,
        [(tokens, hid)],
        [(s, 0, 0, tokens // 2, cols, 0, 0, (s,)) for s in range(n_seq)],
        2,
    )
    key_weight_grad = weights_call(after(columns, query_grad), key_parts)
    return query_grad[None], key_weight_grad, value_weight_grad


def solution(mesh):
    placed = (
        P("dp", "seq", None),
        P("dp", None, None),
        P("dp", "seq"),
        P("dp", "seq"),
        P(),
        P("dp"),
        P("dp", "seq", None),
    )
    return jax.shard_map(
        functools.partial(shards, mesh.shape["dp"], mesh.shape["seq"]),
        mesh=mesh,
        in_specs=placed,
        out_specs=(P("dp", "seq", None), P("dp", "seq"), P("dp", "seq")),
        check_vma=False,
    )
```

```python
import functools

import jax
import jax.numpy as jnp
from jax import lax
from jax.experimental import pallas as pl
from jax.experimental.pallas import tpu as pltpu
from jax.sharding import PartitionSpec as P

HD = 128
LIVE = 128
VMEM = 60 * 1024 * 1024


ROWS = (((1,), (1,)), ((), ()))
COLUMNS = (((0,), (0,)), ((), ()))
FACTOR = HD ** (-0.5)


def attend_kernel(parts, length_ref, raw_ref, inv_ref, gain_ref, *refs):
    query_refs, grad_refs = refs[:parts], refs[parts : 2 * parts]
    attend_refs = refs[2 * parts : 3 * parts]
    keys_ref, value_grad_ref = refs[3 * parts :]
    keys = (raw_ref[...].astype(jnp.float32) * inv_ref[...] * gain_ref[...]).astype(jnp.bfloat16)
    keys_ref[...] = keys
    valid = lax.broadcasted_iota(jnp.int32, (LIVE, 1), 0) < length_ref[0]
    for head in range(keys.shape[1] // HD):
        at = slice(head * HD, (head + 1) * HD)
        value_grad = jnp.zeros((LIVE, HD), jnp.float32)
        for query_ref, grad_ref, attend_ref in zip(query_refs, grad_refs, attend_refs):
            scores = lax.dot_general(
                keys[:, at], query_ref[:, at], ROWS, preferred_element_type=jnp.float32
            )
            scores = jnp.where(valid, scores * FACTOR, -jnp.inf)
            powers = jnp.exp(scores - jnp.max(scores, axis=0, keepdims=True))
            attend = powers * (1.0 / jnp.sum(powers, axis=0, keepdims=True))
            attend_ref[head] = attend
            value_grad += jnp.dot(
                attend.astype(jnp.bfloat16), grad_ref[:, at], preferred_element_type=jnp.float32
            )
        value_grad_ref[:, at] = value_grad.astype(jnp.bfloat16)


def gradient_kernel(parts, raw_ref, value_ref, gain_ref, *refs):
    query_refs, grad_refs = refs[:parts], refs[parts : 2 * parts]
    attend_refs, score_refs = refs[2 * parts : 3 * parts], refs[3 * parts : 4 * parts]
    scaled_ref, inner_ref = refs[4 * parts :]

    @pl.when(pl.program_id(0) == 0)
    def _():
        inner_ref[...] = jnp.zeros_like(inner_ref)

    for head in range(value_ref.shape[1] // HD):
        at = slice(head * HD, (head + 1) * HD)
        key_grad = jnp.zeros((LIVE, HD), jnp.float32)
        for query_ref, grad_ref, attend_ref, score_ref in zip(
            query_refs, grad_refs, attend_refs, score_refs
        ):
            attend = attend_ref[head]
            dattend = lax.dot_general(
                value_ref[:, at], grad_ref[:, at], ROWS, preferred_element_type=jnp.float32
            )
            delta = jnp.sum(attend * dattend, axis=0, keepdims=True)
            dscores = (attend * (dattend - delta)).astype(jnp.bfloat16)
            score_ref[head] = dscores
            key_grad += jnp.dot(dscores, query_ref[:, at], preferred_element_type=jnp.float32)
        scaled = key_grad * FACTOR * gain_ref[:, at]
        scaled_ref[:, at] = scaled
        inner_ref[...] += scaled * raw_ref[:, at].astype(jnp.float32)


def query_kernel(parts, keys_ref, *refs):
    for head in range(keys_ref.shape[1] // HD):
        at = slice(head * HD, (head + 1) * HD)
        for score_ref, out_ref in zip(refs[:parts], refs[parts:]):
            out = lax.dot_general(
                score_ref[head], keys_ref[:, at], COLUMNS, preferred_element_type=jnp.float32
            )
            out_ref[:, at] = (out * FACTOR).astype(jnp.bfloat16)


def specs(tokens, heads):
    group = next(g for g in (4, 2, 1) if heads % g == 0)
    width = group * HD
    head = pl.BlockSpec((LIVE, width), lambda h: (0, h))
    block = pl.BlockSpec((tokens, width), lambda h: (0, h))
    upper = pl.BlockSpec((None, tokens, width), lambda h: (0, 0, h))
    lower = pl.BlockSpec((None, tokens, width), lambda h: (1, 0, h))
    weights = pl.BlockSpec((group, LIVE, tokens), lambda h: (h, 0, 0))
    gain = pl.BlockSpec((1, width), lambda h: (0, h))
    return heads // group, head, block, upper, lower, weights, gain


def attend_call(length, raw, inv, gain, moved, tokens):
    parts = len(moved)
    cols = moved[0].shape[2]
    heads = cols // HD
    steps, head, block, upper, lower, weights, gains = specs(tokens, heads)
    outs = pl.pallas_call(
        functools.partial(attend_kernel, parts),
        grid=(steps,),
        in_specs=[
            pl.BlockSpec(memory_space=pltpu.SMEM),
            head,
            pl.BlockSpec((LIVE, 1), lambda h: (0, 0)),
            gains,
        ]
        + [upper] * parts
        + [lower] * parts,
        out_specs=[weights] * parts + [head, head],
        out_shape=[jax.ShapeDtypeStruct((heads, LIVE, tokens), jnp.float32)] * parts
        + [jax.ShapeDtypeStruct((LIVE, cols), jnp.bfloat16)] * 2,
        compiler_params=pltpu.CompilerParams(vmem_limit_bytes=VMEM),
        cost_estimate=pl.CostEstimate(
            flops=16 * parts * tokens * cols * LIVE,
            bytes_accessed=16 * parts * tokens * cols,
            transcendentals=0,
        ),
    )(length, raw, inv, gain, *moved, *moved)
    return outs[:parts], outs[parts], outs[parts + 1]


def gradient_call(raw, values, gain, moved, attends, tokens):
    parts = len(moved)
    cols = moved[0].shape[2]
    heads = cols // HD
    steps, head, block, upper, lower, weights, gains = specs(tokens, heads)
    outs = pl.pallas_call(
        functools.partial(gradient_kernel, parts),
        grid=(steps,),
        in_specs=[head, head, gains] + [upper] * parts + [lower] * parts + [weights] * parts,
        out_specs=[weights] * parts + [head, pl.BlockSpec((LIVE, HD), lambda h: (0, 0))],
        out_shape=[jax.ShapeDtypeStruct((heads, LIVE, tokens), jnp.bfloat16)] * parts
        + [
            jax.ShapeDtypeStruct((LIVE, cols), jnp.float32),
            jax.ShapeDtypeStruct((LIVE, HD), jnp.float32),
        ],
        compiler_params=pltpu.CompilerParams(vmem_limit_bytes=VMEM),
        cost_estimate=pl.CostEstimate(
            flops=16 * parts * tokens * cols * LIVE,
            bytes_accessed=16 * parts * tokens * cols,
            transcendentals=0,
        ),
    )(raw, values, gain, *moved, *moved, *attends)
    return outs[:parts], outs[parts], outs[parts + 1]


def query_call(keys, scores):
    parts = len(scores)
    heads, _, tokens = scores[0].shape
    steps, head, block, _, _, weights, _ = specs(tokens, heads)
    return pl.pallas_call(
        functools.partial(query_kernel, parts),
        grid=(steps,),
        in_specs=[head] + [weights] * parts,
        out_specs=[block] * parts,
        out_shape=[jax.ShapeDtypeStruct((tokens, keys.shape[1]), jnp.bfloat16)] * parts,
        compiler_params=pltpu.CompilerParams(vmem_limit_bytes=VMEM),
        cost_estimate=pl.CostEstimate(
            flops=8 * parts * tokens * keys.shape[1] * LIVE,
            bytes_accessed=8 * parts * tokens * keys.shape[1],
            transcendentals=0,
        ),
    )(keys, *scores)


def rows_spec(part, width, tiled=False):
    _, count, index = part
    if tiled:
        return pl.BlockSpec((count, width), lambda n: (index, n))
    return pl.BlockSpec((count, width), lambda n: (index, 0))


def pick_kernel(place_ref, first_ref, mine_ref, sibling_first_ref, sibling_ref, *out_refs):
    here = place_ref[0] == 0
    rows = out_refs[0].shape[1]
    for index, out_ref in enumerate(out_refs):
        at = pl.ds(pl.multiple_of(place_ref[2 + index] * rows, rows), rows)
        out_ref[:LIVE] = jnp.where(here, first_ref[:, at], sibling_first_ref[:, at])
        out_ref[LIVE:] = jnp.where(here, mine_ref[:, at], sibling_ref[:, at])


def pick_call(place, first, mine, sibling_first, sibling, rows):
    arrays = (first, mine, sibling_first, sibling)
    shape = (LIVE + mine.shape[0], rows)
    return pl.pallas_call(
        pick_kernel,
        grid=(1,),
        in_specs=[pl.BlockSpec(memory_space=pltpu.SMEM)]
        + [pl.BlockSpec(x.shape, lambda n: (0, 0)) for x in arrays],
        out_specs=[pl.BlockSpec(shape, lambda n: (0, 0))] * 2,
        out_shape=[jax.ShapeDtypeStruct(shape, jnp.bfloat16)] * 2,
        compiler_params=pltpu.CompilerParams(vmem_limit_bytes=VMEM),
        cost_estimate=pl.CostEstimate(flops=1000, bytes_accessed=1000, transcendentals=0),
    )(place, *arrays)


def product_kernel(videos, place_ref, *refs):
    mine_refs, sibling_refs = refs[:videos], refs[videos : 2 * videos]
    weight_refs, out_ref = refs[2 * videos : -1], refs[-1]
    rows = weight_refs[0].shape[0]
    total = None
    for step, weight_ref in enumerate(weight_refs):
        here = place_ref[step // 2] == 0
        at = pl.ds(pl.multiple_of(place_ref[2 + step % 2] * rows, rows), rows)
        block = jnp.concatenate(
            [jnp.where(here, m[:, at], s[:, at]) for m, s in zip(mine_refs, sibling_refs)], axis=0
        )
        term = jnp.dot(block, weight_ref[...], preferred_element_type=jnp.float32)
        total = term if total is None else total + term
    out_ref[...] = total


def product_call(place, mine, sibling, weights):
    videos = len(mine)
    width = weights[0][0].shape[1]
    parts = [*mine, *sibling, *weights]
    return pl.pallas_call(
        functools.partial(product_kernel, videos),
        grid=(1,),
        in_specs=[pl.BlockSpec(memory_space=pltpu.SMEM)]
        + [rows_spec(part, part[0].shape[1]) for part in parts],
        out_specs=pl.BlockSpec((videos * LIVE, width), lambda n: (0, 0)),
        out_shape=jax.ShapeDtypeStruct((videos * LIVE, width), jnp.float32),
        compiler_params=pltpu.CompilerParams(vmem_limit_bytes=VMEM),
        cost_estimate=pl.CostEstimate(flops=1000, bytes_accessed=1000, transcendentals=0),
    )(place, *[part[0] for part in parts])


def weights_kernel(columns_ref, *refs):
    parts = [ref[...] for ref in refs[:-1]]
    refs[-1][...] = jnp.dot(
        columns_ref[...], jnp.concatenate(parts, axis=0), preferred_element_type=jnp.float32
    )


def weights_call(columns, parts):
    rows, depth = columns.shape
    cols = parts[0][0].shape[1]
    tile = min(cols, 512)
    return pl.pallas_call(
        weights_kernel,
        grid=(cols // tile,),
        in_specs=[pl.BlockSpec(columns.shape, lambda n: (0, 0))]
        + [rows_spec(part, tile, True) for part in parts],
        out_specs=pl.BlockSpec((rows, tile), lambda n: (0, n)),
        out_shape=jax.ShapeDtypeStruct((rows, cols), jnp.float32),
        compiler_params=pltpu.CompilerParams(vmem_limit_bytes=VMEM),
        cost_estimate=pl.CostEstimate(
            flops=2 * rows * cols * depth,
            bytes_accessed=4 * rows * cols + 2 * depth * (rows + cols),
            transcendentals=0,
        ),
    )(columns, *[part[0] for part in parts])


def after(x, *others):
    return lax.optimization_barrier((x, *others))[0]


def blocks_kernel(lanes_ref, query_ref, grad_ref, *out_refs):
    cols = out_refs[0].shape[2]
    for index, out_ref in enumerate(out_refs):
        at = pl.ds(pl.multiple_of(lanes_ref[index] * cols, cols), cols)
        out_ref[0] = query_ref[:, at]
        out_ref[1] = grad_ref[:, at]


def blocks_call(lanes, query, grad):
    parts = lanes.shape[0]
    tokens, hid = query.shape
    cols, tiles = hid // parts, 4
    rows = tokens // tiles
    return pl.pallas_call(
        blocks_kernel,
        grid=(tiles,),
        in_specs=[pl.BlockSpec(memory_space=pltpu.SMEM)]
        + [pl.BlockSpec((rows, hid), lambda n: (n, 0))] * 2,
        out_specs=[pl.BlockSpec((2, rows, cols), lambda n: (0, n, 0))] * parts,
        out_shape=[jax.ShapeDtypeStruct((2, tokens, cols), jnp.bfloat16)] * parts,
        compiler_params=pltpu.CompilerParams(vmem_limit_bytes=VMEM),
        cost_estimate=pl.CostEstimate(
            flops=1000, bytes_accessed=8 * tokens * hid, transcendentals=0
        ),
    )(lanes, query, grad)


def pack_kernel(moves, inputs, place_ref, *refs):
    ins, outs = refs[:inputs], refs[inputs:]

    def span(at, width):
        if isinstance(at, int):
            return pl.ds(at, width)
        return pl.ds(pl.multiple_of(place_ref[at[0]] * width, width), width)

    for source, row, col, count, width, target, to_row, to_col in moves:
        block = ins[source][pl.ds(row, count), span(col, width)]
        outs[target][pl.ds(to_row, count), span(to_col, width)] = block


def pack_call(place, arrays, shapes, moves, tiles=1, size=1000):
    def spec(shape):
        return pl.BlockSpec((shape[0] // tiles, shape[1]), lambda n: (n, 0))

    return pl.pallas_call(
        functools.partial(pack_kernel, moves, len(arrays)),
        grid=(tiles,),
        in_specs=[pl.BlockSpec(memory_space=pltpu.SMEM)] + [spec(x.shape) for x in arrays],
        out_specs=[spec(shape) for shape in shapes],
        out_shape=[jax.ShapeDtypeStruct(shape, jnp.bfloat16) for shape in shapes],
        compiler_params=pltpu.CompilerParams(vmem_limit_bytes=VMEM),
        cost_estimate=pl.CostEstimate(flops=1000, bytes_accessed=size, transcendentals=0),
    )(place, *arrays)


def shards(n_dp, n_seq, query, caption, key_weight, value_weight, key_gain, lengths, out_grad):
    rows, cols = key_weight.shape
    hid = cols * n_seq
    lines = n_dp // 2
    half = cols // 2
    wide = 2 * rows
    tokens = query.shape[1]
    me = lax.axis_index("dp")
    lane = lax.axis_index("seq")
    quad, low, side = me // 4, me // 2 % 2, me % 2
    core = lane % 2

    def over_dp(x, step):
        return lax.ppermute(x, "dp", [(a, a ^ step) for a in range(n_dp)])

    def over_seq(x, step):
        return lax.ppermute(x, "seq", [(a, a ^ step) for a in range(n_seq)])

    def col_block(x, index, width):
        return lax.dynamic_slice(x, (0, index * width), (x.shape[0], width))

    pieces = wide // half
    quads = lines // 2
    scalars = [low, 1 - low, quad * 2 + core, quad * 2 + 1 - core]
    scalars += [(quad ^ (s // 2)) * 2 + core for s in range(2, lines)]
    scalars += [(quad * 2 + core) * pieces + p for p in range(pieces)]
    place = jnp.stack(scalars).astype(jnp.int32)
    near_at = lines + 2
    near_given, kept, value_given, mine_first, sibling_first, *given = pack_call(
        place,
        [key_weight, value_weight, caption[0]],
        [(rows + pieces * LIVE, half), (2 * rows, half), (rows, half)] + [(LIVE, wide)] * lines,
        [
            (0, 0, (1,), rows, half, 0, 0, 0),
            (0, 0, (0,), rows, half, 1, 0, 0),
            (1, 0, (0,), rows, half, 1, rows, 0),
            (1, 0, (1,), rows, half, 2, 0, 0),
        ]
        + [(2, 0, (near_at + p,), LIVE, half, 0, rows + p * LIVE, 0) for p in range(pieces)]
        + [(2, 0, (2 + s,), LIVE, wide, 3 + s, 0, 0) for s in range(lines)],
    )
    near = over_dp(near_given, 2)
    beside = over_dp(kept, 1)
    arrived = [over_dp(x, 2 * s) for s, x in enumerate(given, 2)]

    lanes = jnp.stack([lane ^ s for s in range(n_seq)]).astype(jnp.int32)
    packed = blocks_call(after(lanes, kept), query[0], out_grad[0])
    moved = [packed[0]] + [None] * (n_seq - 1)
    previous = ()
    for s in range(2, n_seq):
        moved[s] = over_seq(after(packed[s], *previous), s)
        previous = (moved[s],)
    moved[1] = over_seq(after(packed[1], beside), 1)

    key_near, shared, shared_given = pack_call(
        place,
        [near, *arrived],
        [(rows, half)] + [((lines - 1) * LIVE, wide)] * 2,
        [(0, 0, 0, rows, half, 0, 0, 0)]
        + [
            (0, rows + p * LIVE, 0, LIVE, half, out, 0, p * half)
            for p in range(pieces)
            for out in (1, 2)
        ]
        + [
            (s - 1, 0, 0, LIVE, wide, out, (s - 1) * LIVE, 0)
            for s in range(2, lines)
            for out in (1, 2)
        ],
    )
    key_far = over_dp(key_near, 1)
    value_near = over_dp(after(value_given, near, *arrived), 2)
    sibling = over_seq(shared_given, 1)
    key_quad = ((kept, rows, 0), (beside, rows, 0), (key_near, rows, 0), (key_far, rows, 0))

    places = jnp.stack([core ^ low, 1 - (core ^ low), side, 1 - side]).astype(jnp.int32)

    def product(places, weights, other):
        chosen = [s for s in range(lines) if bool(s & 2) == other]
        return product_call(
            places,
            [(shared, LIVE, s - 1) if s else (mine_first, LIVE, 0) for s in chosen],
            [(sibling, LIVE, s - 1) if s else (sibling_first, LIVE, 0) for s in chosen],
            weights,
        )

    def reduced(total):
        step = 8
        while step < n_dp:
            count = total.shape[0] // 2
            total = total[:count] + over_dp(total[count:], step)
            step *= 2
        return lax.reduce_precision(total, 8, 7).astype(jnp.bfloat16)

    def joined(own, other):
        return jnp.where(
            low == 0,
            jnp.concatenate([own, other], axis=1),
            jnp.concatenate([other, own], axis=1),
        )

    def seq_sum(x):
        for step in steps:
            x = x + over_seq(x, step)
        return x

    steps = [1 << k for k in reversed(range(n_seq.bit_length() - 1))]
    gain = lax.dynamic_slice(key_gain, (lane * cols,), (cols,)).reshape(1, cols)
    own_columns, other_given = pick_call(places, mine_first, shared, sibling_first, sibling, rows)
    key_product = product(after(places, own_columns), key_quad, True)
    key_sent = over_dp(key_product, 4)
    later = after(places, key_product)
    value_far = over_dp(after(value_near, key_product), 1)
    value_quad = ((kept, rows, 1), (beside, rows, 1), (value_near, rows, 0), (value_far, rows, 0))
    other_columns = over_dp(after(other_given, key_product), 1)
    columns = jnp.concatenate([own_columns, other_columns], axis=0).T
    value_product = product(later, value_quad, True)
    value_rest_product = product(later, value_quad, False)
    key_sent = after(key_sent, value_product, value_rest_product, columns, gain)
    value_sent = over_dp(after(value_product, key_sent), 4)
    key_total = reduced(product(later, key_quad, False) + key_sent)
    raw = joined(key_total[:LIVE], over_dp(key_total[LIVE:], 2))
    raw_wide = raw.astype(jnp.float32)
    squares = seq_sum(jnp.sum(raw_wide * raw_wide, axis=-1, keepdims=True))
    inv_rms = lax.rsqrt(squares / hid + 1e-06)
    value_total = reduced(value_rest_product + after(value_sent, inv_rms))
    value_other = over_dp(value_total[LIVE:], 2)
    attends, keys, value_grad = attend_call(
        lengths, after(raw, columns, value_total), inv_rms, gain, moved, tokens
    )

    values = joined(value_total[:LIVE], after(value_other, value_grad))

    value_near_parts = [over_dp(value_grad, 2 * s) for s in range(1, lines)]
    scores, scaled, inner = gradient_call(raw, values, gain, moved, attends, tokens)
    outs = query_call(keys, scores)
    inner = jnp.sum(inner, axis=-1, keepdims=True)
    for step in steps[:-1]:
        inner = inner + over_seq(inner, step)
    far_sum = after(inner, *value_near_parts)
    inner_mean = (far_sum + over_seq(far_sum, 1)) / hid
    raw_grad = (inv_rms * scaled - raw_wide * inv_rms**3 * inner_mean).astype(jnp.bfloat16)
    value_parts = lax.optimization_barrier((value_grad, *value_near_parts, inner, outs[0]))[:-2]
    value_rest = over_dp(jnp.concatenate(value_parts, axis=0), 1)
    key_near_parts = [over_dp(raw_grad, 2 * s) for s in range(1, lines)]
    placed = [outs[0]] + [None] * (n_seq - 1)
    previous = (inner,)
    for s in range(2, n_seq):
        placed[s] = over_seq(after(outs[s], *previous), s)
        previous = (placed[s], key_near_parts[-1])
    placed[1] = over_seq(after(outs[1], value_rest), 1)
    key_first = over_dp(raw_grad, 1)
    key_rest = over_dp(after(jnp.concatenate(key_near_parts, axis=0), key_first), 1)
    key_parts = (
        [(x, LIVE, 0) for x in (raw_grad, *key_near_parts)]
        + [(key_first, LIVE, 0)]
        + [(key_rest, LIVE, s) for s in range(lines - 1)]
    )
    value_parts = (
        [(x, LIVE, 0) for x in (value_grad, *value_near_parts)]
        + [(value_rest, LIVE, s) for s in range(lines)]
    )
    value_weight_grad = weights_call(after(columns, key_first), value_parts)
    (query_grad,) = pack_call(
        lanes,
        placed,
        [(tokens, hid)],
        [(s, 0, 0, tokens // 2, cols, 0, 0, (s,)) for s in range(n_seq)],
        2,
    )
    key_weight_grad = weights_call(columns, key_parts)
    return query_grad[None], key_weight_grad, value_weight_grad


def solution(mesh):
    placed = (
        P("dp", "seq", None),
        P("dp", None, None),
        P("dp", "seq"),
        P("dp", "seq"),
        P(),
        P("dp"),
        P("dp", "seq", None),
    )
    return jax.shard_map(
        functools.partial(shards, mesh.shape["dp"], mesh.shape["seq"]),
        mesh=mesh,
        in_specs=placed,
        out_specs=(P("dp", "seq", None), P("dp", "seq"), P("dp", "seq")),
        check_vma=False,
    )
```

```python
import functools

import jax
import jax.numpy as jnp
from jax import lax
from jax.experimental import pallas as pl
from jax.experimental.pallas import tpu as pltpu
from jax.sharding import PartitionSpec as P

HD = 128
LIVE = 128
VMEM = 60 * 1024 * 1024


ROWS = (((1,), (1,)), ((), ()))
COLUMNS = (((0,), (0,)), ((), ()))
FACTOR = HD ** (-0.5)


def attend_kernel(parts, length_ref, raw_ref, inv_ref, gain_ref, *refs):
    query_refs, grad_refs = refs[:parts], refs[parts : 2 * parts]
    attend_refs = refs[2 * parts : 3 * parts]
    keys_ref, value_grad_ref = refs[3 * parts :]
    keys = (raw_ref[...].astype(jnp.float32) * inv_ref[...] * gain_ref[...]).astype(jnp.bfloat16)
    keys_ref[...] = keys
    valid = lax.broadcasted_iota(jnp.int32, (LIVE, 1), 0) < length_ref[0]
    for head in range(keys.shape[1] // HD):
        at = slice(head * HD, (head + 1) * HD)
        value_grad = jnp.zeros((LIVE, HD), jnp.float32)
        for query_ref, grad_ref, attend_ref in zip(query_refs, grad_refs, attend_refs):
            scores = lax.dot_general(
                keys[:, at], query_ref[:, at], ROWS, preferred_element_type=jnp.float32
            )
            scores = jnp.where(valid, scores * FACTOR, -jnp.inf)
            powers = jnp.exp(scores - jnp.max(scores, axis=0, keepdims=True))
            attend = powers * (1.0 / jnp.sum(powers, axis=0, keepdims=True))
            attend_ref[head] = attend
            value_grad += jnp.dot(
                attend.astype(jnp.bfloat16), grad_ref[:, at], preferred_element_type=jnp.float32
            )
        value_grad_ref[:, at] = value_grad.astype(jnp.bfloat16)


def gradient_kernel(parts, raw_ref, value_ref, gain_ref, *refs):
    query_refs, grad_refs = refs[:parts], refs[parts : 2 * parts]
    attend_refs, score_refs = refs[2 * parts : 3 * parts], refs[3 * parts : 4 * parts]
    scaled_ref, inner_ref = refs[4 * parts :]

    @pl.when(pl.program_id(0) == 0)
    def _():
        inner_ref[...] = jnp.zeros_like(inner_ref)

    for head in range(value_ref.shape[1] // HD):
        at = slice(head * HD, (head + 1) * HD)
        key_grad = jnp.zeros((LIVE, HD), jnp.float32)
        for query_ref, grad_ref, attend_ref, score_ref in zip(
            query_refs, grad_refs, attend_refs, score_refs
        ):
            attend = attend_ref[head]
            dattend = lax.dot_general(
                value_ref[:, at], grad_ref[:, at], ROWS, preferred_element_type=jnp.float32
            )
            delta = jnp.sum(attend * dattend, axis=0, keepdims=True)
            dscores = (attend * (dattend - delta)).astype(jnp.bfloat16)
            score_ref[head] = dscores
            key_grad += jnp.dot(dscores, query_ref[:, at], preferred_element_type=jnp.float32)
        scaled = key_grad * FACTOR * gain_ref[:, at]
        scaled_ref[:, at] = scaled
        inner_ref[...] += scaled * raw_ref[:, at].astype(jnp.float32)


def query_kernel(parts, keys_ref, *refs):
    for head in range(keys_ref.shape[1] // HD):
        at = slice(head * HD, (head + 1) * HD)
        for score_ref, out_ref in zip(refs[:parts], refs[parts:]):
            out = lax.dot_general(
                score_ref[head], keys_ref[:, at], COLUMNS, preferred_element_type=jnp.float32
            )
            out_ref[:, at] = (out * FACTOR).astype(jnp.bfloat16)


def specs(tokens, heads):
    group = next(g for g in (4, 2, 1) if heads % g == 0)
    width = group * HD
    head = pl.BlockSpec((LIVE, width), lambda h: (0, h))
    block = pl.BlockSpec((tokens, width), lambda h: (0, h))
    upper = pl.BlockSpec((None, tokens, width), lambda h: (0, 0, h))
    lower = pl.BlockSpec((None, tokens, width), lambda h: (1, 0, h))
    weights = pl.BlockSpec((group, LIVE, tokens), lambda h: (h, 0, 0))
    gain = pl.BlockSpec((1, width), lambda h: (0, h))
    return heads // group, head, block, upper, lower, weights, gain


def attend_call(length, raw, inv, gain, moved, tokens):
    parts = len(moved)
    cols = moved[0].shape[2]
    heads = cols // HD
    steps, head, block, upper, lower, weights, gains = specs(tokens, heads)
    outs = pl.pallas_call(
        functools.partial(attend_kernel, parts),
        grid=(steps,),
        in_specs=[
            pl.BlockSpec(memory_space=pltpu.SMEM),
            head,
            pl.BlockSpec((LIVE, 1), lambda h: (0, 0)),
            gains,
        ]
        + [upper] * parts
        + [lower] * parts,
        out_specs=[weights] * parts + [head, head],
        out_shape=[jax.ShapeDtypeStruct((heads, LIVE, tokens), jnp.float32)] * parts
        + [jax.ShapeDtypeStruct((LIVE, cols), jnp.bfloat16)] * 2,
        compiler_params=pltpu.CompilerParams(vmem_limit_bytes=VMEM),
        cost_estimate=pl.CostEstimate(
            flops=16 * parts * tokens * cols * LIVE,
            bytes_accessed=16 * parts * tokens * cols,
            transcendentals=0,
        ),
    )(length, raw, inv, gain, *moved, *moved)
    return outs[:parts], outs[parts], outs[parts + 1]


def gradient_call(raw, values, gain, moved, attends, tokens):
    parts = len(moved)
    cols = moved[0].shape[2]
    heads = cols // HD
    steps, head, block, upper, lower, weights, gains = specs(tokens, heads)
    outs = pl.pallas_call(
        functools.partial(gradient_kernel, parts),
        grid=(steps,),
        in_specs=[head, head, gains] + [upper] * parts + [lower] * parts + [weights] * parts,
        out_specs=[weights] * parts + [head, pl.BlockSpec((LIVE, HD), lambda h: (0, 0))],
        out_shape=[jax.ShapeDtypeStruct((heads, LIVE, tokens), jnp.bfloat16)] * parts
        + [
            jax.ShapeDtypeStruct((LIVE, cols), jnp.float32),
            jax.ShapeDtypeStruct((LIVE, HD), jnp.float32),
        ],
        compiler_params=pltpu.CompilerParams(vmem_limit_bytes=VMEM),
        cost_estimate=pl.CostEstimate(
            flops=16 * parts * tokens * cols * LIVE,
            bytes_accessed=16 * parts * tokens * cols,
            transcendentals=0,
        ),
    )(raw, values, gain, *moved, *moved, *attends)
    return outs[:parts], outs[parts], outs[parts + 1]


def query_call(keys, scores):
    parts = len(scores)
    heads, _, tokens = scores[0].shape
    steps, head, block, _, _, weights, _ = specs(tokens, heads)
    return pl.pallas_call(
        functools.partial(query_kernel, parts),
        grid=(steps,),
        in_specs=[head] + [weights] * parts,
        out_specs=[block] * parts,
        out_shape=[jax.ShapeDtypeStruct((tokens, keys.shape[1]), jnp.bfloat16)] * parts,
        compiler_params=pltpu.CompilerParams(vmem_limit_bytes=VMEM),
        cost_estimate=pl.CostEstimate(
            flops=8 * parts * tokens * keys.shape[1] * LIVE,
            bytes_accessed=8 * parts * tokens * keys.shape[1],
            transcendentals=0,
        ),
    )(keys, *scores)


def rows_spec(part, width, tiled=False):
    _, count, index = part
    if tiled:
        return pl.BlockSpec((count, width), lambda n: (index, n))
    return pl.BlockSpec((count, width), lambda n: (index, 0))


def pick_kernel(place_ref, first_ref, mine_ref, sibling_first_ref, sibling_ref, *out_refs):
    here = place_ref[0] == 0
    rows = out_refs[0].shape[1]
    for index, out_ref in enumerate(out_refs):
        at = pl.ds(pl.multiple_of(place_ref[2 + index] * rows, rows), rows)
        out_ref[:LIVE] = jnp.where(here, first_ref[:, at], sibling_first_ref[:, at])
        out_ref[LIVE:] = jnp.where(here, mine_ref[:, at], sibling_ref[:, at])


def pick_call(place, first, mine, sibling_first, sibling, rows):
    arrays = (first, mine, sibling_first, sibling)
    shape = (LIVE + mine.shape[0], rows)
    return pl.pallas_call(
        pick_kernel,
        grid=(1,),
        in_specs=[pl.BlockSpec(memory_space=pltpu.SMEM)]
        + [pl.BlockSpec(x.shape, lambda n: (0, 0)) for x in arrays],
        out_specs=[pl.BlockSpec(shape, lambda n: (0, 0))] * 2,
        out_shape=[jax.ShapeDtypeStruct(shape, jnp.bfloat16)] * 2,
        compiler_params=pltpu.CompilerParams(vmem_limit_bytes=VMEM),
        cost_estimate=pl.CostEstimate(flops=1000, bytes_accessed=1000, transcendentals=0),
    )(place, *arrays)


def product_kernel(videos, place_ref, *refs):
    mine_refs, sibling_refs = refs[:videos], refs[videos : 2 * videos]
    weight_refs, out_ref = refs[2 * videos : -1], refs[-1]
    rows = weight_refs[0].shape[0]
    total = None
    for step, weight_ref in enumerate(weight_refs):
        here = place_ref[step // 2] == 0
        at = pl.ds(pl.multiple_of(place_ref[2 + step % 2] * rows, rows), rows)
        block = jnp.concatenate(
            [jnp.where(here, m[:, at], s[:, at]) for m, s in zip(mine_refs, sibling_refs)], axis=0
        )
        term = jnp.dot(block, weight_ref[...], preferred_element_type=jnp.float32)
        total = term if total is None else total + term
    out_ref[...] = total


def product_call(place, mine, sibling, weights):
    videos = len(mine)
    width = weights[0][0].shape[1]
    parts = [*mine, *sibling, *weights]
    return pl.pallas_call(
        functools.partial(product_kernel, videos),
        grid=(1,),
        in_specs=[pl.BlockSpec(memory_space=pltpu.SMEM)]
        + [rows_spec(part, part[0].shape[1]) for part in parts],
        out_specs=pl.BlockSpec((videos * LIVE, width), lambda n: (0, 0)),
        out_shape=jax.ShapeDtypeStruct((videos * LIVE, width), jnp.float32),
        compiler_params=pltpu.CompilerParams(vmem_limit_bytes=VMEM),
        cost_estimate=pl.CostEstimate(flops=1000, bytes_accessed=1000, transcendentals=0),
    )(place, *[part[0] for part in parts])


def weights_kernel(columns_ref, *refs):
    parts = [ref[...] for ref in refs[:-1]]
    refs[-1][...] = jnp.dot(
        columns_ref[...], jnp.concatenate(parts, axis=0), preferred_element_type=jnp.float32
    )


def weights_call(columns, parts):
    rows, depth = columns.shape
    cols = parts[0][0].shape[1]
    tile = min(cols, 512)
    return pl.pallas_call(
        weights_kernel,
        grid=(cols // tile,),
        in_specs=[pl.BlockSpec(columns.shape, lambda n: (0, 0))]
        + [rows_spec(part, tile, True) for part in parts],
        out_specs=pl.BlockSpec((rows, tile), lambda n: (0, n)),
        out_shape=jax.ShapeDtypeStruct((rows, cols), jnp.float32),
        compiler_params=pltpu.CompilerParams(vmem_limit_bytes=VMEM),
        cost_estimate=pl.CostEstimate(
            flops=2 * rows * cols * depth,
            bytes_accessed=4 * rows * cols + 2 * depth * (rows + cols),
            transcendentals=0,
        ),
    )(columns, *[part[0] for part in parts])


def after(x, *others):
    return lax.optimization_barrier((x, *others))[0]


def blocks_kernel(lanes_ref, query_ref, grad_ref, *out_refs):
    cols = out_refs[0].shape[2]
    for index, out_ref in enumerate(out_refs):
        at = pl.ds(pl.multiple_of(lanes_ref[index] * cols, cols), cols)
        out_ref[0] = query_ref[:, at]
        out_ref[1] = grad_ref[:, at]


def blocks_call(lanes, query, grad):
    parts = lanes.shape[0]
    tokens, hid = query.shape
    cols, tiles = hid // parts, 4
    rows = tokens // tiles
    return pl.pallas_call(
        blocks_kernel,
        grid=(tiles,),
        in_specs=[pl.BlockSpec(memory_space=pltpu.SMEM)]
        + [pl.BlockSpec((rows, hid), lambda n: (n, 0))] * 2,
        out_specs=[pl.BlockSpec((2, rows, cols), lambda n: (0, n, 0))] * parts,
        out_shape=[jax.ShapeDtypeStruct((2, tokens, cols), jnp.bfloat16)] * parts,
        compiler_params=pltpu.CompilerParams(vmem_limit_bytes=VMEM),
        cost_estimate=pl.CostEstimate(
            flops=1000, bytes_accessed=8 * tokens * hid, transcendentals=0
        ),
    )(lanes, query, grad)


def pack_kernel(moves, inputs, place_ref, *refs):
    ins, outs = refs[:inputs], refs[inputs:]

    def span(at, width):
        if isinstance(at, int):
            return pl.ds(at, width)
        return pl.ds(pl.multiple_of(place_ref[at[0]] * width, width), width)

    for source, row, col, count, width, target, to_row, to_col in moves:
        block = ins[source][pl.ds(row, count), span(col, width)]
        outs[target][pl.ds(to_row, count), span(to_col, width)] = block


def pack_call(place, arrays, shapes, moves, tiles=1, size=1000):
    def spec(shape):
        return pl.BlockSpec((shape[0] // tiles, shape[1]), lambda n: (n, 0))

    return pl.pallas_call(
        functools.partial(pack_kernel, moves, len(arrays)),
        grid=(tiles,),
        in_specs=[pl.BlockSpec(memory_space=pltpu.SMEM)] + [spec(x.shape) for x in arrays],
        out_specs=[spec(shape) for shape in shapes],
        out_shape=[jax.ShapeDtypeStruct(shape, jnp.bfloat16) for shape in shapes],
        compiler_params=pltpu.CompilerParams(vmem_limit_bytes=VMEM),
        cost_estimate=pl.CostEstimate(flops=1000, bytes_accessed=size, transcendentals=0),
    )(place, *arrays)


def insert_kernel(index_ref, whole_ref, block_ref, out_ref):
    out_ref[...] = block_ref[...]


def insert_call(index, whole, block):
    tokens, cols = block.shape
    return pl.pallas_call(
        insert_kernel,
        grid_spec=pltpu.PrefetchScalarGridSpec(
            num_scalar_prefetch=1,
            grid=(1,),
            in_specs=[
                pl.BlockSpec(memory_space=pl.ANY),
                pl.BlockSpec((tokens, cols), lambda n, at: (0, 0)),
            ],
            out_specs=pl.BlockSpec((tokens, cols), lambda n, at: (0, at[0])),
        ),
        out_shape=jax.ShapeDtypeStruct(whole.shape, whole.dtype),
        input_output_aliases={1: 0},
        compiler_params=pltpu.CompilerParams(vmem_limit_bytes=VMEM),
        cost_estimate=pl.CostEstimate(
            flops=1000, bytes_accessed=4 * tokens * cols, transcendentals=0
        ),
    )(index, whole, block)


def shards(n_dp, n_seq, query, caption, key_weight, value_weight, key_gain, lengths, out_grad):
    rows, cols = key_weight.shape
    hid = cols * n_seq
    lines = n_dp // 2
    half = cols // 2
    wide = 2 * rows
    tokens = query.shape[1]
    me = lax.axis_index("dp")
    lane = lax.axis_index("seq")
    quad, low, side = me // 4, me // 2 % 2, me % 2
    core = lane % 2

    def over_dp(x, step):
        return lax.ppermute(x, "dp", [(a, a ^ step) for a in range(n_dp)])

    def over_seq(x, step):
        return lax.ppermute(x, "seq", [(a, a ^ step) for a in range(n_seq)])

    def col_block(x, index, width):
        return lax.dynamic_slice(x, (0, index * width), (x.shape[0], width))

    pieces = wide // half
    quads = lines // 2
    scalars = [low, 1 - low, quad * 2 + core, quad * 2 + 1 - core]
    scalars += [(quad ^ (s // 2)) * 2 + core for s in range(2, lines)]
    scalars += [(quad * 2 + core) * pieces + p for p in range(pieces)]
    place = jnp.stack(scalars).astype(jnp.int32)
    near_at = lines + 2
    near_given, kept, value_given, mine_first, sibling_first, *given = pack_call(
        place,
        [key_weight, value_weight, caption[0]],
        [(rows + pieces * LIVE, half), (2 * rows, half), (rows, half)] + [(LIVE, wide)] * lines,
        [
            (0, 0, (1,), rows, half, 0, 0, 0),
            (0, 0, (0,), rows, half, 1, 0, 0),
            (1, 0, (0,), rows, half, 1, rows, 0),
            (1, 0, (1,), rows, half, 2, 0, 0),
        ]
        + [(2, 0, (near_at + p,), LIVE, half, 0, rows + p * LIVE, 0) for p in range(pieces)]
        + [(2, 0, (2 + s,), LIVE, wide, 3 + s, 0, 0) for s in range(lines)],
    )
    near = over_dp(near_given, 2)
    beside = over_dp(kept, 1)
    arrived = [over_dp(x, 2 * s) for s, x in enumerate(given, 2)]

    lanes = jnp.stack([lane ^ s for s in range(n_seq)]).astype(jnp.int32)
    packed = blocks_call(after(lanes, kept), query[0], out_grad[0])
    moved = [packed[0]] + [None] * (n_seq - 1)
    previous = ()
    for s in range(2, n_seq):
        moved[s] = over_seq(after(packed[s], *previous), s)
        previous = (moved[s],)
    moved[1] = over_seq(after(packed[1], beside), 1)

    key_near, shared, shared_given = pack_call(
        place,
        [near, *arrived],
        [(rows, half)] + [((lines - 1) * LIVE, wide)] * 2,
        [(0, 0, 0, rows, half, 0, 0, 0)]
        + [
            (0, rows + p * LIVE, 0, LIVE, half, out, 0, p * half)
            for p in range(pieces)
            for out in (1, 2)
        ]
        + [
            (s - 1, 0, 0, LIVE, wide, out, (s - 1) * LIVE, 0)
            for s in range(2, lines)
            for out in (1, 2)
        ],
    )
    key_far = over_dp(key_near, 1)
    value_near = over_dp(after(value_given, near, *arrived), 2)
    sibling = over_seq(shared_given, 1)
    key_quad = ((kept, rows, 0), (beside, rows, 0), (key_near, rows, 0), (key_far, rows, 0))

    places = jnp.stack([core ^ low, 1 - (core ^ low), side, 1 - side]).astype(jnp.int32)

    def product(places, weights, other):
        chosen = [s for s in range(lines) if bool(s & 2) == other]
        return product_call(
            places,
            [(shared, LIVE, s - 1) if s else (mine_first, LIVE, 0) for s in chosen],
            [(sibling, LIVE, s - 1) if s else (sibling_first, LIVE, 0) for s in chosen],
            weights,
        )

    def reduced(total):
        step = 8
        while step < n_dp:
            count = total.shape[0] // 2
            total = total[:count] + over_dp(total[count:], step)
            step *= 2
        return lax.reduce_precision(total, 8, 7).astype(jnp.bfloat16)

    def joined(own, other):
        return jnp.where(
            low == 0,
            jnp.concatenate([own, other], axis=1),
            jnp.concatenate([other, own], axis=1),
        )

    def seq_sum(x):
        for step in steps:
            x = x + over_seq(x, step)
        return x

    steps = [1 << k for k in reversed(range(n_seq.bit_length() - 1))]
    gain = lax.dynamic_slice(key_gain, (lane * cols,), (cols,)).reshape(1, cols)
    own_columns, other_given = pick_call(places, mine_first, shared, sibling_first, sibling, rows)
    key_product = product(after(places, own_columns), key_quad, True)
    key_sent = over_dp(key_product, 4)
    later = after(places, key_product)
    value_far = over_dp(after(value_near, key_product), 1)
    value_quad = ((kept, rows, 1), (beside, rows, 1), (value_near, rows, 0), (value_far, rows, 0))
    other_columns = over_dp(after(other_given, key_product), 1)
    columns = jnp.concatenate([own_columns, other_columns], axis=0).T
    value_product = product(later, value_quad, True)
    value_rest_product = product(later, value_quad, False)
    key_sent = after(key_sent, value_product, value_rest_product, columns, gain)
    value_sent = over_dp(after(value_product, key_sent), 4)
    key_total = reduced(product(later, key_quad, False) + key_sent)
    raw = joined(key_total[:LIVE], over_dp(key_total[LIVE:], 2))
    raw_wide = raw.astype(jnp.float32)
    squares = seq_sum(jnp.sum(raw_wide * raw_wide, axis=-1, keepdims=True))
    inv_rms = lax.rsqrt(squares / hid + 1e-06)
    value_total = reduced(value_rest_product + after(value_sent, inv_rms))
    value_other = over_dp(value_total[LIVE:], 2)
    attends, keys, value_grad = attend_call(
        lengths, after(raw, columns, value_total), inv_rms, gain, moved, tokens
    )

    values = joined(value_total[:LIVE], after(value_other, value_grad))

    value_near_parts = [over_dp(value_grad, 2 * s) for s in range(1, lines)]
    scores, scaled, inner = gradient_call(raw, values, gain, moved, attends, tokens)
    outs = query_call(keys, scores)
    value_first = over_dp(value_grad, 1)
    inner = jnp.sum(after(inner, value_first), axis=-1, keepdims=True)
    for step in steps[:-1]:
        inner = inner + over_seq(inner, step)
    far_sum = after(inner, *value_near_parts)
    inner_mean = (far_sum + over_seq(far_sum, 1)) / hid
    raw_grad = (inv_rms * scaled - raw_wide * inv_rms**3 * inner_mean).astype(jnp.bfloat16)
    value_parts = lax.optimization_barrier((*value_near_parts, inner, outs[0]))[:-2]
    value_rest = over_dp(jnp.concatenate(value_parts, axis=0), 1)
    key_near_parts = [over_dp(raw_grad, 2 * s) for s in range(1, lines)]
    placed = [outs[0]] + [None] * (n_seq - 1)
    previous = (inner,)
    for s in range(2, n_seq):
        placed[s] = over_seq(after(outs[s], *previous), s)
        previous = (placed[s], key_near_parts[-1])
    placed[1] = over_seq(after(outs[1], value_rest), 1)
    key_first = over_dp(raw_grad, 1)
    key_rest = over_dp(after(jnp.concatenate(key_near_parts, axis=0), key_first), 1)
    key_parts = (
        [(x, LIVE, 0) for x in (raw_grad, *key_near_parts)]
        + [(key_first, LIVE, 0)]
        + [(key_rest, LIVE, s) for s in range(lines - 1)]
    )
    value_parts = (
        [(x, LIVE, 0) for x in (value_grad, *value_near_parts)]
        + [(value_first, LIVE, 0)]
        + [(value_rest, LIVE, s) for s in range(lines - 1)]
    )
    value_weight_grad = weights_call(after(columns, key_first), value_parts)
    (assembled,) = pack_call(
        lanes,
        placed[:-1],
        [(tokens, hid)],
        [(s, 0, 0, tokens // 2, cols, 0, 0, (s,)) for s in range(n_seq - 1)],
        2,
    )
    query_grad = insert_call(lanes[-1:], assembled, placed[-1])
    key_weight_grad = weights_call(columns, key_parts)
    return query_grad[None], key_weight_grad, value_weight_grad


def solution(mesh):
    placed = (
        P("dp", "seq", None),
        P("dp", None, None),
        P("dp", "seq"),
        P("dp", "seq"),
        P(),
        P("dp"),
        P("dp", "seq", None),
    )
    return jax.shard_map(
        functools.partial(shards, mesh.shape["dp"], mesh.shape["seq"]),
        mesh=mesh,
        in_specs=placed,
        out_specs=(P("dp", "seq", None), P("dp", "seq"), P("dp", "seq")),
        check_vma=False,
    )
```
